256 devices in a mesh: ctx: 8 (over z_hi, y), tile: 8 (over z_lo, core), mp: 4 (over x).
Axes of the slice: x: 4, y: 4, z: 8 (z_hi: 2, z_lo: 4; z = z_hi * 4 + z_lo), core: 2. Of those that a mesh axis runs over, the one named last changes fastest.
Arguments:
- text_embed: bfloat16 [8192, 4096], P('ctx', ('tile', 'mp')), may hold values from -6 to 6
- latents: bfloat16 [16, 64, 512], P('ctx', 'tile'), may hold values from -6 to 6
- down_conv: bfloat16 [72, 256], P(None, 'mp'), may hold values from -0.75 to 0.75
- patch_in: bfloat16 [4096, 4096], P(None, ('tile', 'mp')), may hold values from -0.09375 to 0.09375
- norm_gain: bfloat16 [4096], P(('tile', 'mp')), may hold values from 0.25 to 1.75
- query_weight: bfloat16 [4096, 4096], P(None, ('tile', 'mp')), may hold values from -0.09375 to 0.09375
- key_weight: bfloat16 [4096, 4096], P(None, ('tile', 'mp')), may hold values from -0.09375 to 0.09375
- value_weight: bfloat16 [4096, 4096], P(None, ('tile', 'mp')), may hold values from -0.09375 to 0.09375
- query_gain: float32 [128], replicated, may hold values from 0.5 to 6
- key_gain: float32 [128], replicated, may hold values from 0.5 to 6
- out_weight: bfloat16 [4096, 4096], P(None, ('tile', 'mp')), may hold values from -0.5 to 0.5
- patch_out: bfloat16 [4096, 4096], P(('tile', 'mp')), may hold values from -0.09375 to 0.09375
- up_conv: bfloat16 [2304, 8], replicated, may hold values from -0.125 to 0.125
- span_start: int32 [16], replicated, may hold values from 0 to 7936, as said below
- image_of_slot: int32 [16], replicated, may hold values from 0 to 15, each once
Outputs:
- layer_out: bfloat16 [8192, 4096], P('ctx', ('tile', 'mp'))
- noise_pred: float32 [16, 64, 512], P('ctx', 'tile')
The draws below stay inside these ranges and needn't reach their ends.
Inputs may be any that keep to these rules, and one draw needn't show every extreme that they name: `span_start`: sorted ascending; each image spans 256 positions, spans do not intersect, the first image starts the document and the last one ends it; spans may cross the boundaries between indices of ctx. `image_of_slot`: each image appears in exactly one slot.
All inputs are finite; a program needn't handle non-finite values.
Results may differ from the reference program's by a relative error of at most 0.04.
Values may be sent and summed in bfloat16 or wider, within the bound.
A program may use at most 128 MiB of HBM per device.

```python
import jax
import jax.numpy as jnp
from jax import lax

D = 4096
HEADS = 32
HD = 128
CH = 256
CIN = 8
HL = 64
WL = 64
PATCH = 4
IMG_TOK = 256
NIMG = 16
TOKENS = 8192


def draw_span_start(key, part):
    key = jax.random.fold_in(key, 11)
    spare = TOKENS - NIMG * IMG_TOK
    weights = jax.random.randint(key, (NIMG - 1,), 1, 100, dtype=jnp.int32)
    gaps = spare * weights // jnp.sum(weights)
    gaps = gaps.at[NIMG - 2].add(spare - jnp.sum(gaps))
    leading = jnp.concatenate([jnp.zeros((1,), jnp.int32), jnp.cumsum(gaps).astype(jnp.int32)])
    return (leading + jnp.arange(NIMG, dtype=jnp.int32) * IMG_TOK).astype(jnp.int32)


def draw_query_gain(key, part):
    key = jax.random.fold_in(key, 21)
    return jax.random.uniform(key, (HD,), jnp.float32, 0.5, 2.5)


def draw_key_gain(key, part):
    key = jax.random.fold_in(key, 22)
    return jax.random.uniform(key, (HD,), jnp.float32, 0.5, 2.5)


def steps_of(key, dims, pieces, least, top_value):
    def one(dim, blocks):
        steps = jax.random.uniform(jax.random.fold_in(jax.random.fold_in(key, 6), dim), (blocks,), jnp.float32, least / len(pieces), top_value / len(pieces))
        return jnp.repeat(jnp.exp(steps), dims[dim] // blocks).reshape((-1,) + (1,) * (len(dims) - dim - 1))

    level = one(*pieces[0])
    for cut in pieces[1:]:
        level = level * one(*cut)
    return level


def normal_values(own_key, shape, width, limit, split=(), kind=jnp.bfloat16):
    entries = jax.random.normal(own_key, shape, jnp.float32) * width
    if len(split) > 0:
        entries = steps_of(own_key, shape, split, -0.22, 0.18) * entries
    return jnp.clip(entries, min=-limit, max=limit).astype(kind)


def setup_inputs(seed: int = 0) -> dict:
    keys = jax.random.split(jax.random.key(seed), 16)
    text_embed = normal_values(keys[0], (TOKENS, D), 1.0, 6.0, ((0, 8), (1, 32)))
    latents = normal_values(keys[1], (NIMG, HL, WL * CIN), 1.0, 6.0, ((0, 8), (1, 8)))
    down_conv = normal_values(keys[2], (9 * CIN, CH), (9 * CIN) ** -0.5, 0.75, ((1, 4),))
    patch_in = normal_values(keys[3], (PATCH * PATCH * CH, D), (PATCH * PATCH * CH) ** -0.5, 0.09375, ((1, 32),))
    norm_gain = jnp.clip(1.0 + 0.15 * jax.random.normal(keys[4], (D,), jnp.float32), 0.25, 1.75).astype(jnp.bfloat16)
    query_weight = normal_values(keys[5], (D, HEADS * HD), D ** -0.5, 0.09375, ((1, 32),))
    key_weight = normal_values(keys[6], (D, HEADS * HD), D ** -0.5, 0.09375, ((1, 32),))
    value_weight = normal_values(keys[7], (D, HEADS * HD), D ** -0.5, 0.09375, ((1, 32),))
    query_gain = draw_query_gain(jax.random.fold_in(keys[15], 71), 0)
    key_gain = draw_key_gain(jax.random.fold_in(keys[15], 71), 0)
    out_weight = normal_values(keys[10], (HEADS * HD, D), HD ** -0.5, 0.5, ((1, 32),))
    patch_out = normal_values(keys[11], (D, PATCH * PATCH * CH), D ** -0.5, 0.09375, ((0, 32),))
    up_conv = normal_values(keys[12], (9 * CH, CIN), (9 * CH) ** -0.5, 0.125)
    span_start = draw_span_start(jax.random.fold_in(keys[15], 71), 0)
    image_of_slot = jax.random.permutation(keys[14], NIMG).astype(jnp.int32)
    return {"text_embed": text_embed, "latents": latents, "down_conv": down_conv, "patch_in": patch_in, "norm_gain": norm_gain, "query_weight": query_weight, "key_weight": key_weight, "value_weight": value_weight, "query_gain": query_gain, "key_gain": key_gain, "out_weight": out_weight, "patch_out": patch_out, "up_conv": up_conv, "span_start": span_start, "image_of_slot": image_of_slot}


EPSILON = 1e-05
NEGATIVE_FILL = -1e+30

def rms_scale(values):
    return lax.rsqrt(lax.optimization_barrier(jnp.mean(values * values, axis=-1, keepdims=True)) + EPSILON)

def conv_same(image, weight):
    height, breadth = (image.shape[0], image.shape[1])
    padded = jnp.pad(image, ((1, 1), (1, 1), (0, 0)))
    taps = [padded[row_shift:row_shift + height, col_shift:col_shift + breadth, :] for row_shift in range(3) for col_shift in range(3)]
    stacked = jnp.concatenate(taps, axis=-1).reshape(height * breadth, -1)
    return jnp.dot(stacked, weight, preferred_element_type=jnp.float32).reshape(height, breadth, weight.shape[1])

def image_ids(positions, span_start):
    inside = (positions[:, None] >= span_start[None, :]) & (positions[:, None] < span_start[None, :] + IMG_TOK)
    numbers = jnp.arange(span_start.shape[0], dtype=jnp.int32)
    return (lax.optimization_barrier(jnp.sum(jnp.where(inside, numbers[None, :] + 1, 0), axis=1)) - 1).astype(jnp.int32)

def slot_lookup(image_of_slot):
    numbers = jnp.arange(image_of_slot.shape[0], dtype=jnp.int32)
    matches = image_of_slot[None, :] == numbers[:, None]
    return lax.optimization_barrier(jnp.sum(jnp.where(matches, numbers[None, :], 0), axis=1)).astype(jnp.int32)

def reference(text_embed, latents, down_conv, patch_in, norm_gain, query_weight, key_weight, value_weight, query_gain, key_gain, out_weight, patch_out, up_conv, span_start, image_of_slot):

    def down_block(latent):
        image = latent.reshape(HL, WL, CIN)
        activated = jax.nn.silu(conv_same(image, down_conv)).astype(jnp.bfloat16)
        patches = activated.reshape(HL // PATCH, PATCH, WL // PATCH, PATCH, CH).transpose(0, 2, 1, 3, 4)
        patches = patches.reshape(IMG_TOK, PATCH * PATCH * CH)
        return jnp.dot(patches, patch_in, preferred_element_type=jnp.float32).astype(jnp.bfloat16)
    image_tokens = lax.map(down_block, latents)
    positions = jnp.arange(TOKENS, dtype=jnp.int32)
    owners = image_ids(positions, span_start)
    safe_owner = jnp.maximum(owners, 0)
    slot_table = slot_lookup(image_of_slot)
    source_rows = slot_table[safe_owner] * IMG_TOK + positions - span_start[safe_owner]
    source_rows = jnp.clip(source_rows, 0, NIMG * IMG_TOK - 1).astype(jnp.int32)
    flat_tokens = image_tokens.reshape(NIMG * IMG_TOK, D)
    stream = jnp.where((owners >= 0)[:, None], flat_tokens[source_rows], text_embed)
    widened = stream.astype(jnp.float32)
    normed = (widened * rms_scale(widened) * norm_gain.astype(jnp.float32)).astype(jnp.bfloat16)
    visible = (positions[None, :] <= positions[:, None]) | (owners[None, :] == owners[:, None]) & (owners[:, None] >= 0)

    def one_head(head):
        first_col = head * HD
        query_cols = lax.dynamic_slice_in_dim(query_weight, first_col, HD, 1)
        key_cols = lax.dynamic_slice_in_dim(key_weight, first_col, HD, 1)
        value_cols = lax.dynamic_slice_in_dim(value_weight, first_col, HD, 1)
        query_raw = jnp.dot(normed, query_cols, preferred_element_type=jnp.float32)
        key_raw = jnp.dot(normed, key_cols, preferred_element_type=jnp.float32)
        value_raw = jnp.dot(normed, value_cols, preferred_element_type=jnp.float32)
        queries = (query_raw * rms_scale(query_raw) * query_gain * HD ** (-0.5)).astype(jnp.bfloat16)
        key_rows = (key_raw * rms_scale(key_raw) * key_gain * 1.0).astype(jnp.bfloat16)
        value_rows = value_raw.astype(jnp.bfloat16)
        scores = jnp.dot(queries, key_rows.T, preferred_element_type=jnp.float32)
        scores = jnp.where(visible, scores, NEGATIVE_FILL)
        row_top = lax.optimization_barrier(jnp.max(scores, axis=1, keepdims=True))
        weights = jnp.where(visible, jnp.exp(scores - row_top), 0.0)
        row_sum = lax.optimization_barrier(jnp.sum(weights, axis=1, keepdims=True))
        summed = jnp.dot(weights.astype(jnp.bfloat16), value_rows, preferred_element_type=jnp.float32)
        return (summed / row_sum).astype(jnp.bfloat16)
    heads_out = lax.map(one_head, jnp.arange(HEADS, dtype=jnp.int32))
    attended = heads_out.transpose(1, 0, 2).reshape(TOKENS, HEADS * HD)
    mixed = jnp.dot(attended, out_weight, preferred_element_type=jnp.float32)
    layer_out = (widened + mixed).astype(jnp.bfloat16)

    def up_block(slot):
        image = image_of_slot[slot]
        rows = lax.dynamic_slice_in_dim(layer_out, span_start[image], IMG_TOK, 0)
        projected = jax.nn.silu(jnp.dot(rows, patch_out, preferred_element_type=jnp.float32)).astype(jnp.bfloat16)
        pixels = projected.reshape(HL // PATCH, WL // PATCH, PATCH, PATCH, CH).transpose(0, 2, 1, 3, 4)
        pixels = pixels.reshape(HL, WL, CH)
        return conv_same(pixels, up_conv).reshape(HL, WL * CIN)
    noise_pred = lax.map(up_block, jnp.arange(NIMG, dtype=jnp.int32))
    return (layer_out, noise_pred)
```

```python
import functools

import jax
import jax.numpy as jnp
from jax import lax
from jax.experimental import pallas as pl
from jax.experimental.pallas import tpu as pltpu
from jax.sharding import PartitionSpec as P

HD = 128
CH = 256
CIN = 8
PATCH = 4
IMG_TOK = 256
UNIT = 512
EPSILON = 1e-05
NEGATIVE = -1e30
MESH = pl.DeviceIdType.MESH
ANY = pl.BlockSpec(memory_space=pl.ANY)
BF = jnp.bfloat16
F32 = jnp.float32


def remote(src, dst, send, recv, device):
    return pltpu.make_async_remote_copy(
        src_ref=src, dst_ref=dst, send_sem=send, recv_sem=recv, device_id=device, device_id_type=MESH
    )


def barrier(devices):
    sem = pltpu.get_barrier_semaphore()
    for device in devices:
        pl.semaphore_signal(sem, inc=1, device_id=device, device_id_type=MESH)
    pl.semaphore_wait(sem, len(devices))


def coordinates():
    return lax.axis_index("ctx"), lax.axis_index("tile"), lax.axis_index("mp")


class Gather:
    def __init__(self, over, sources, dst, send, recv, local):
        ctx, tile, mp = coordinates()
        self.sources, self.dst, self.send, self.recv, self.local = sources, dst, send, recv, local
        self.pending, self.count = [], 0
        if over == "xz":
            self.size, self.a, self.r, self.core = 4, tile // 2, mp, tile % 2
            self.dev = lambda a, r, core: (ctx, a * 2 + core, r)
            self.slot = lambda a, r, core: (a * 2 + core) * 4 + r
            self.sibling = 1 - self.core
        else:
            self.size, self.a, self.r, self.core = 2, ctx // 4, ctx % 4, 0
            self.dev = lambda a, r, core: (a * 4 + r, tile, mp)
            self.slot = lambda a, r, core: a * 4 + r
            self.sibling = None
        self.right, self.left, self.far = (self.r + 1) % 4, (self.r + 3) % 4, (self.r + 2) % 4

    def partners(self):
        found = [self.dev((self.a + d) % self.size, self.r, self.core) for d in range(1, self.size)]
        found += [self.dev(self.a, self.right, self.core), self.dev(self.a, self.left, self.core)]
        if self.sibling is not None:
            found.append(self.dev(self.a, self.r, self.sibling))
        return found

    def push(self, src, slot, unit, device, half=None):
        dst = self.dst.at[slot, unit]
        which = 0
        if half is not None:
            rows = pl.ds(half * (UNIT // 2), UNIT // 2)
            src, dst, which = src.at[rows], dst.at[rows], half
        copy = remote(src, dst, self.send.at[self.count], self.recv.at[unit, slot, which], device)
        self.count += 1
        copy.start()
        self.pending.append(copy)

    def arrive(self, slot, unit, half=None):
        dst = self.dst.at[slot, unit]
        which = 0
        if half is not None:
            dst, which = dst.at[pl.ds(half * (UNIT // 2), UNIT // 2)], half
        device = self.dev(self.a, self.right, self.core)
        remote(dst, dst, self.send.at[0], self.recv.at[unit, slot, which], device).wait_recv()

    def run(self):
        own = self.slot(self.a, self.r, self.core)
        units = len(self.sources)
        right = self.dev(self.a, self.right, self.core)
        left = self.dev(self.a, self.left, self.core)
        twin = None if self.sibling is None else self.dev(self.a, self.r, self.sibling)
        locals_ = []
        for u, src in enumerate(self.sources):
            for d in range(1, self.size):
                self.push(src, own, u, self.dev((self.a + d) % self.size, self.r, self.core))
            self.push(src, own, u, right)
            self.push(src, own, u, left)
            if twin is not None:
                self.push(src, own, u, twin)
            copy = pltpu.make_async_copy(src, self.dst.at[own, u], self.local.at[u])
            copy.start()
            locals_.append(copy)
        yield
        steps = [(k, u) for k in range(self.size) for u in range(units)]
        for n in range(len(steps) + 2 * units):
            if n < len(steps):
                k, u = steps[n]
                if k > 0:
                    slot = self.slot((self.a + k) % self.size, self.r, self.core)
                    self.arrive(slot, u)
                    src = self.dst.at[slot, u]
                    self.push(src, slot, u, right)
                    self.push(src, slot, u, left)
                    if twin is not None:
                        self.push(src, slot, u, twin)
                    yield
            if 0 <= n - units < len(steps):
                k, u = steps[n - units]
                a = (self.a + k) % self.size
                for ring, target, half in ((self.left, right, 0), (self.right, left, 1)):
                    slot = self.slot(a, ring, self.core)
                    self.arrive(slot, u)
                    self.push(self.dst.at[slot, u], slot, u, target, half)
                    if twin is not None:
                        self.push(self.dst.at[slot, u], slot, u, twin)
                yield
            if 0 <= n - 2 * units < len(steps):
                k, u = steps[n - 2 * units]
                slot = self.slot((self.a + k) % self.size, self.far, self.core)
                self.arrive(slot, u, 0)
                self.arrive(slot, u, 1)
                if twin is not None:
                    self.push(self.dst.at[slot, u], slot, u, twin)
                yield
        if twin is not None:
            for k in range(self.size):
                for ring in (self.r, self.left, self.right, self.far):
                    for u in range(units):
                        self.arrive(self.slot((self.a + k) % self.size, ring, self.sibling), u)
            yield
        for copy in locals_:
            copy.wait()
        for copy in self.pending:
            copy.wait_send()


def interleave(runs):
    runs = list(runs)
    while runs:
        left = []
        for run in runs:
            try:
                next(run)
                left.append(run)
            except StopIteration:
                pass
        runs = left


def gather_sems(over, units):
    slots, sends = (32, 35) if over == "xz" else (8, 9)
    return [
        pltpu.SemaphoreType.DMA((units * sends,)),
        pltpu.SemaphoreType.DMA((units, slots, 2)),
        pltpu.SemaphoreType.DMA((units,)),
    ]


def gather_call(jobs, collective_id):
    flat = [array for _, arrays in jobs for array in arrays]

    def kernel(*refs):
        inputs, refs = refs[: len(flat)], refs[len(flat) :]
        outputs, sems = refs[: len(jobs)], refs[len(jobs) :]
        built, at = [], 0
        for i, (over, arrays) in enumerate(jobs):
            sources = inputs[at : at + len(arrays)]
            at += len(arrays)
            built.append(Gather(over, sources, outputs[i], *sems[3 * i : 3 * i + 3]))
        barrier([device for job in built for device in job.partners()])
        interleave([job.run() for job in built])

    shapes, scratch = [], []
    for over, arrays in jobs:
        slots = 32 if over == "xz" else 8
        shapes.append(jax.ShapeDtypeStruct((slots, len(arrays), UNIT, HD), BF))
        scratch += gather_sems(over, len(arrays))
    return pl.pallas_call(
        kernel,
        out_shape=shapes,
        in_specs=[ANY] * len(flat),
        out_specs=[ANY] * len(jobs),
        scratch_shapes=scratch,
        compiler_params=pltpu.CompilerParams(collective_id=collective_id, has_side_effects=True),
    )(*flat)


def opening_kernel(
    text, patch_out, gain, latents, down, text_all, columns, gains, latents_all, down_all,
    send, recv, local, col_send, col_recv, gain_send, gain_recv, lat_send, lat_recv, down_send, down_recv, own_sem,
):
    ctx, tile, mp = coordinates()
    me = tile * 4 + mp
    job = Gather("ctx", [text.at[u] for u in range(2)], text_all, send, recv, local)
    others = []
    for i in range(1, 32):
        peer = (me + i) % 32
        others.append((ctx, peer // 4, peer % 4))
    barrier(others + job.partners())

    def part(peer):
        return patch_out.at[:, pl.ds(pl.multiple_of(peer * HD, HD), HD)]

    lat_copies, down_copies = [], []
    for i in range(1, 8):
        copy = remote(latents, latents_all.at[tile], lat_send.at[i], lat_recv.at[tile], (ctx, (tile + i) % 8, mp))
        copy.start()
        lat_copies.append(copy)
    for i in range(1, 4):
        copy = remote(down, down_all.at[mp], down_send.at[i], down_recv.at[mp], (ctx, tile, (mp + i) % 4))
        copy.start()
        down_copies.append(copy)
    own = [
        pltpu.make_async_copy(latents, latents_all.at[tile], own_sem.at[0]),
        pltpu.make_async_copy(down, down_all.at[mp], own_sem.at[1]),
        pltpu.make_async_copy(part(me), columns.at[me], own_sem.at[2]),
        pltpu.make_async_copy(gain, gains.at[me], own_sem.at[3]),
    ]
    for copy in own:
        copy.start()
    run = job.run()
    next(run)

    def column_copy(i):
        peer = (me + i) % 32
        device = (ctx, peer // 4, peer % 4)
        return remote(part(peer), columns.at[me], col_send.at[i], col_recv.at[me], device)

    def gain_copy(i):
        peer = (me + i) % 32
        device = (ctx, peer // 4, peer % 4)
        return remote(gain, gains.at[me], gain_send.at[i], gain_recv.at[me], device)

    def start(i, carry):
        column_copy(i).start()
        gain_copy(i).start()
        return carry

    lax.fori_loop(1, 32, start, 0)
    interleave([run])

    def finish(i, carry):
        peer = (me + i) % 32
        device = (ctx, peer // 4, peer % 4)
        column_copy(i).wait_send()
        gain_copy(i).wait_send()
        remote(columns.at[peer], columns.at[peer], col_send.at[i], col_recv.at[peer], device).wait_recv()
        remote(gain, gains.at[peer], gain_send.at[i], gain_recv.at[peer], device).wait_recv()
        return carry

    lax.fori_loop(1, 32, finish, 0)
    for i, copy in enumerate(lat_copies):
        peer = (tile + i + 1) % 8
        copy.wait_send()
        remote(latents, latents_all.at[peer], lat_send.at[0], lat_recv.at[peer], (ctx, peer, mp)).wait_recv()
    for i, copy in enumerate(down_copies):
        peer = (mp + i + 1) % 4
        copy.wait_send()
        remote(down, down_all.at[peer], down_send.at[0], down_recv.at[peer], (ctx, tile, peer)).wait_recv()
    for copy in own:
        copy.wait()


def opening(text, patch_out, gain, latents, down):
    dma = pltpu.SemaphoreType.DMA
    return pl.pallas_call(
        opening_kernel,
        out_shape=[
            jax.ShapeDtypeStruct((8, 2, UNIT, HD), BF),
            jax.ShapeDtypeStruct((32, HD, HD), BF),
            jax.ShapeDtypeStruct((32, 16, HD), BF),
            jax.ShapeDtypeStruct((8,) + latents.shape, BF),
            jax.ShapeDtypeStruct((4,) + down.shape, BF),
        ],
        in_specs=[ANY] * 5,
        out_specs=[ANY] * 5,
        scratch_shapes=gather_sems("ctx", 2)
        + [dma((32,)), dma((32,)), dma((32,)), dma((32,)), dma((8,)), dma((8,)), dma((4,)), dma((4,)), dma((4,))],
        compiler_params=pltpu.CompilerParams(collective_id=1, has_side_effects=True),
    )(text, patch_out, gain, latents, down)


def bands_kernel(up, out, send, recv, high_send, high_recv, low_send, low_recv, own_sem):
    ctx, tile, mp = coordinates()
    me = tile * 4 + mp
    row = tile // 2
    others = []
    for i in range(1, 32):
        peer = (me + i) % 32
        others.append((ctx, peer // 4, peer % 4))
    barrier(others)

    def band(target):
        return up.at[:, pl.ds(pl.multiple_of(target * 32, 32), 32)]

    def above(target):
        return up.at[:, pl.ds(pl.multiple_of(target * 32 - 16, 16), 16)]

    def below(target):
        return up.at[:, pl.ds(pl.multiple_of(target * 32 + 32, 16), 16)]

    spots = {"band": (16, 32), "high": (0, 16), "low": (48, 16)}

    def spot(source, kind):
        first, size = spots[kind]
        return out.at[source, :, pl.ds(first, size)]

    def copies(i):
        peer = (me + i) % 32
        target = peer // 4
        device = (ctx, target, peer % 4)
        return (
            target,
            lambda: remote(band(target), spot(me, "band"), send.at[i], recv.at[me], device),
            lambda: remote(above(target), spot(me, "high"), high_send.at[i], high_recv.at[me], device),
            lambda: remote(below(target), spot(me, "low"), low_send.at[i], low_recv.at[me], device),
        )

    def start(i, carry):
        target, mid, high, low = copies(i)
        mid().start()

        @pl.when((row == 3) & (target > 0))
        def _():
            high().start()

        @pl.when((row == 0) & (target < 7))
        def _():
            low().start()

        return carry

    lax.fori_loop(1, 32, start, 0)
    local = pltpu.make_async_copy(band(tile), spot(me, "band"), own_sem.at[0])
    local.start()

    @pl.when(row == 3)
    def _():
        copy = pltpu.make_async_copy(above(tile), spot(me, "high"), own_sem.at[1])
        copy.start()
        copy.wait()

    @pl.when(row == 0)
    def _():
        copy = pltpu.make_async_copy(below(tile), spot(me, "low"), own_sem.at[2])
        copy.start()
        copy.wait()

    def finish(i, carry):
        target, mid, high, low = copies(i)
        mid().wait_send()

        @pl.when((row == 3) & (target > 0))
        def _():
            high().wait_send()

        @pl.when((row == 0) & (target < 7))
        def _():
            low().wait_send()

        peer = (me + i) % 32
        device = (ctx, target, peer % 4)
        remote(band(tile), spot(peer, "band"), send.at[i], recv.at[peer], device).wait_recv()

        @pl.when((peer // 8 == 3) & (tile > 0))
        def _():
            remote(spot(peer, "high"), spot(peer, "high"), high_send.at[i], high_recv.at[peer], device).wait_recv()

        @pl.when((peer // 8 == 0) & (tile < 7))
        def _():
            remote(spot(peer, "low"), spot(peer, "low"), low_send.at[i], low_recv.at[peer], device).wait_recv()

        return carry

    lax.fori_loop(1, 32, finish, 0)
    local.wait()


def bands(up):
    return pl.pallas_call(
        bands_kernel,
        out_shape=jax.ShapeDtypeStruct((32, 2, 64, HD), BF),
        in_specs=[ANY],
        out_specs=ANY,
        scratch_shapes=[pltpu.SemaphoreType.DMA((32,))] * 6 + [pltpu.SemaphoreType.DMA((3,))],
        compiler_params=pltpu.CompilerParams(collective_id=2, has_side_effects=True),
    )(up)


def silu(v):
    return v / (1.0 + jnp.exp(-v))


def windows(latents_all):
    grid = latents_all.reshape(8, 2, 8, 512).transpose(1, 0, 2, 3).reshape(2, 64, 512)
    wide = jnp.pad(grid, ((0, 0), (1, 1), (8, 32)))
    before = wide[:, :, 0:512].reshape(2, 66, 16, 32)[..., :8]
    middle = wide[:, :, 8:520].reshape(2, 66, 16, 32)
    after = wide[:, :, 40:552].reshape(2, 66, 16, 32)[..., :8]
    joined = jnp.concatenate([before, middle, after], axis=-1)
    rows = [joined[:, k : k + 61 : 4] for k in range(6)]
    return jnp.concatenate(rows, axis=-1).reshape(UNIT, 288)


def tokens_kernel(w_ref, down_ref, patch_ref, out_ref, total):
    px = pl.program_id(0)
    pr, pc = px // 4, px % 4
    row = lax.broadcasted_iota(jnp.int32, (288, 72), 0)
    col = lax.broadcasted_iota(jnp.int32, (288, 72), 1)
    hit = ((col // 24 + pr) * 6 + (col // 8) % 3 + pc) * 8 + col % 8
    pick = jnp.where(row == hit, 1.0, 0.0).astype(BF)
    weight = jnp.dot(pick, down_ref[...], preferred_element_type=F32).astype(BF)
    act = silu(jnp.dot(w_ref[...], weight, preferred_element_type=F32)).astype(BF)
    term = jnp.dot(act, patch_ref[...], preferred_element_type=F32)

    @pl.when(px == 0)
    def _():
        total[...] = term

    @pl.when(px > 0)
    def _():
        total[...] += term

    @pl.when(px == 15)
    def _():
        out_ref[...] = total[...].astype(BF)


def tokens_of(w, down, patch_in):
    return pl.pallas_call(
        tokens_kernel,
        grid=(16,),
        out_shape=jax.ShapeDtypeStruct((UNIT, HD), BF),
        in_specs=[
            pl.BlockSpec((UNIT, 288), lambda i: (0, 0)),
            pl.BlockSpec((72, CH), lambda i: (0, 0)),
            pl.BlockSpec((CH, HD), lambda i: (i, 0)),
        ],
        out_specs=pl.BlockSpec((UNIT, HD), lambda i: (0, 0)),
        scratch_shapes=[pltpu.VMEM((UNIT, HD), F32)],
    )(w, down, patch_in)


TILE = 256


def qkv_kernel(x_ref, gain_ref, wq_ref, wk_ref, wv_ref, qg_ref, kg_ref, q_ref, kv_ref):
    squares = jnp.zeros((TILE, HD), F32)
    for i in range(32):
        part = x_ref[i, 0].astype(F32)
        squares += part * part
    scale = lax.rsqrt(jnp.sum(squares, axis=1, keepdims=True) * (1.0 / 4096.0) + EPSILON)
    normed = jnp.concatenate(
        [
            (x_ref[i, 0].astype(F32) * scale * gain_ref[:, i * HD : (i + 1) * HD].astype(F32)).astype(BF)
            for i in range(32)
        ],
        axis=1,
    )

    def head(weight, gain, factor):
        raw = jnp.dot(normed, weight, preferred_element_type=F32)
        mean = jnp.mean(raw * raw, axis=1, keepdims=True)
        return (raw * lax.rsqrt(mean + EPSILON) * gain * factor).astype(BF)

    q_ref[0] = head(wq_ref[...], qg_ref[...], HD**-0.5)
    kv_ref[0, 0] = head(wk_ref[...], kg_ref[...], 1.0)
    kv_ref[0, 1] = jnp.dot(normed, wv_ref[...], preferred_element_type=F32).astype(BF)


def qkv_of(x, gain, wq, wk, wv, qg, kg):
    units = x.shape[1]
    per = UNIT // TILE
    weight = pl.BlockSpec((4096, HD), lambda i: (0, 0))
    small = pl.BlockSpec((1, HD), lambda i: (0, 0))
    return pl.pallas_call(
        qkv_kernel,
        grid=(units * per,),
        out_shape=[
            jax.ShapeDtypeStruct((units, UNIT, HD), BF),
            jax.ShapeDtypeStruct((units, 2, UNIT, HD), BF),
        ],
        in_specs=[
            pl.BlockSpec((32, 1, TILE, HD), lambda i: (0, i // per, i % per, 0)),
            pl.BlockSpec((1, 4096), lambda i: (0, 0)),
            weight,
            weight,
            weight,
            small,
            small,
        ],
        out_specs=[
            pl.BlockSpec((1, TILE, HD), lambda i: (i // per, i % per, 0)),
            pl.BlockSpec((1, 2, TILE, HD), lambda i: (i // per, 0, i % per, 0)),
        ],
        compiler_params=pltpu.CompilerParams(vmem_limit_bytes=40 * 1024 * 1024),
    )(x, gain, wq, wk, wv, qg, kg)


def attention_kernel(top_ref, slot_ref, q_ref, lim_t_ref, lim_i_ref, kv_ref, out_ref):
    tile = pl.program_id(0)
    q = q_ref[...]
    cols = lax.broadcasted_iota(jnp.int32, (TILE, 1024), 1)

    def step(carry, k, v, limit):
        top, total, acc = carry
        s = lax.dot_general(q, k, (((1,), (1,)), ((), ())), preferred_element_type=F32)
        s = jnp.where(cols < limit, s, NEGATIVE)
        new = jnp.maximum(top, jnp.max(s, axis=1, keepdims=True))
        w = jnp.exp(s - new)
        factor = jnp.exp(top - new)
        total = total * factor + jnp.sum(w, axis=1, keepdims=True)
        acc = acc * factor + jnp.dot(w.astype(BF), v, preferred_element_type=F32)
        return new, total, acc

    def text_step(n, carry):
        k = jnp.concatenate([kv_ref[2 * n, 0], kv_ref[2 * n + 1, 0]], axis=0)
        v = jnp.concatenate([kv_ref[2 * n, 1], kv_ref[2 * n + 1, 1]], axis=0)
        return step(carry, k, v, lim_t_ref[...] - n * 1024)

    def image_step(n, carry):
        ks, vs = [], []
        for u in range(4):
            slot = slot_ref[n * 4 + u]
            rows = pl.ds(pl.multiple_of((slot % 2) * IMG_TOK, IMG_TOK), IMG_TOK)
            ks.append(kv_ref[slot // 2, 2, rows])
            vs.append(kv_ref[slot // 2, 3, rows])
        return step(carry, jnp.concatenate(ks, axis=0), jnp.concatenate(vs, axis=0), lim_i_ref[...] - n * 1024)

    carry = (jnp.full((TILE, 1), NEGATIVE, F32), jnp.zeros((TILE, 1), F32), jnp.zeros((TILE, HD), F32))
    carry = lax.fori_loop(0, (top_ref[1, tile] + 1023) // 1024, image_step, carry)
    carry = lax.fori_loop(0, (top_ref[0, tile] + 1023) // 1024, text_step, carry)
    _, total, acc = carry
    out_ref[...] = (acc / total).astype(BF)


def attention(tops, slots, q, lim_t, lim_i, kv):
    rows = q.shape[0]
    grid_spec = pltpu.PrefetchScalarGridSpec(
        num_scalar_prefetch=2,
        grid=(rows // TILE,),
        in_specs=[
            pl.BlockSpec((TILE, HD), lambda i, *_: (i, 0)),
            pl.BlockSpec((TILE, 1), lambda i, *_: (i, 0)),
            pl.BlockSpec((TILE, 1), lambda i, *_: (i, 0)),
            pl.BlockSpec((8, 4, UNIT, HD), lambda i, *_: (0, 0, 0, 0)),
        ],
        out_specs=pl.BlockSpec((TILE, HD), lambda i, *_: (i, 0)),
    )
    return pl.pallas_call(
        attention_kernel,
        grid_spec=grid_spec,
        out_shape=jax.ShapeDtypeStruct((rows, HD), BF),
        compiler_params=pltpu.CompilerParams(vmem_limit_bytes=48 * 1024 * 1024),
    )(tops, slots, q, lim_t, lim_i, kv)


def project_kernel(x_ref, w_ref, stream_ref, out_ref):
    x = jnp.concatenate([x_ref[i, 0] for i in range(32)], axis=1)
    mixed = jnp.dot(x, w_ref[...], preferred_element_type=F32)
    out_ref[0] = (stream_ref[0].astype(F32) + mixed).astype(BF)


def project(x, w, stream):
    per = UNIT // TILE
    row_block = pl.BlockSpec((1, TILE, HD), lambda i: (i // per, i % per, 0))
    return pl.pallas_call(
        project_kernel,
        grid=(2 * per,),
        out_shape=jax.ShapeDtypeStruct((2, UNIT, HD), BF),
        in_specs=[
            pl.BlockSpec((32, 1, TILE, HD), lambda i: (0, i // per, i % per, 0)),
            pl.BlockSpec((4096, HD), lambda i: (0, 0)),
            row_block,
        ],
        out_specs=row_block,
        compiler_params=pltpu.CompilerParams(vmem_limit_bytes=32 * 1024 * 1024),
    )(x, w, stream)


def expand_kernel(x_ref, w_ref, out_ref):
    x = jnp.concatenate([x_ref[i, 0] for i in range(32)], axis=1)
    out_ref[...] = silu(jnp.dot(x, w_ref[...], preferred_element_type=F32)).astype(BF)


def expand(x, w):
    per = UNIT // TILE
    return pl.pallas_call(
        expand_kernel,
        grid=(per,),
        out_shape=jax.ShapeDtypeStruct((UNIT, HD), BF),
        in_specs=[
            pl.BlockSpec((32, 1, TILE, HD), lambda i: (0, 0, i, 0)),
            pl.BlockSpec((4096, HD), lambda i: (0, 0)),
        ],
        out_specs=pl.BlockSpec((TILE, HD), lambda i: (i, 0)),
        compiler_params=pltpu.CompilerParams(vmem_limit_bytes=32 * 1024 * 1024),
    )(x, w)


def up_weights(up_conv):
    taps = up_conv.reshape(9, CH, CIN).transpose(1, 0, 2).reshape(CH, 72)
    row = lax.broadcasted_iota(jnp.int32, (72, 36 * HD), 0)
    col = lax.broadcasted_iota(jnp.int32, (72, 36 * HD), 1)
    cell, inner = col // HD, col % HD
    a, b = cell // 6 - inner // 32, cell % 6 - (inner // 8) % 4
    inside = (a >= 0) & (a <= 2) & (b >= 0) & (b <= 2)
    pick = jnp.where(inside & (row == (a * 3 + b) * 8 + inner % 8), 1.0, 0.0).astype(BF)
    return jnp.dot(taps, pick, preferred_element_type=F32).astype(BF)


def up_kernel(edge_ref, g_ref, w_ref, out_ref):
    first, last = edge_ref[0], edge_ref[1]
    inner = lax.broadcasted_iota(jnp.int32, (2, 32, CH), 1)
    sums = [jnp.zeros((64, HD), F32) for _ in range(3)]
    for wr in range(6):
        pr, start = ((3, 0) if wr == 0 else (0, 32) if wr == 5 else (wr - 1, 16))
        for wc in range(6):
            pc = 3 if wc == 0 else 0 if wc == 5 else wc - 1
            px = pr * 4 + pc
            a = jnp.concatenate(
                [g_ref[2 * px, :, start : start + 32], g_ref[2 * px + 1, :, start : start + 32]], axis=-1
            )
            if wr == 0:
                a = jnp.where((inner < 16) & (first == 1), jnp.zeros_like(a), a)
            if wr == 5:
                a = jnp.where((inner >= 16) & (last == 1), jnp.zeros_like(a), a)
            cell = wr * 6 + wc
            term = jnp.dot(
                a.reshape(64, CH), w_ref[:, cell * HD : (cell + 1) * HD], preferred_element_type=F32
            )
            which = 0 if wc == 0 else 2 if wc == 5 else 1
            sums[which] = sums[which] + term
    column = lax.broadcasted_iota(jnp.int32, (64, HD), 0) % 16
    blank = jnp.zeros((1, HD), F32)
    from_left = jnp.concatenate([blank, sums[0][:63]], axis=0)
    from_right = jnp.concatenate([sums[2][1:], blank], axis=0)
    out_ref[...] = (
        sums[1] + jnp.where(column == 0, 0.0, from_left) + jnp.where(column == 15, 0.0, from_right)
    )


def up_block(edges, g, w):
    whole = pl.BlockSpec(memory_space=pltpu.VMEM)
    return pl.pallas_call(
        up_kernel,
        out_shape=jax.ShapeDtypeStruct((64, HD), F32),
        in_specs=[pl.BlockSpec(memory_space=pltpu.SMEM), whole, whole],
        out_specs=whole,
        compiler_params=pltpu.CompilerParams(vmem_limit_bytes=32 * 1024 * 1024),
    )(edges, g, w)


def shards(
    text_embed,
    latents,
    down_conv,
    patch_in,
    norm_gain,
    query_weight,
    key_weight,
    value_weight,
    query_gain,
    key_gain,
    out_weight,
    patch_out,
    up_conv,
    span_start,
    image_of_slot,
):
    ctx, tile = lax.axis_index("ctx"), lax.axis_index("tile")
    images = jnp.arange(16, dtype=jnp.int32)
    before = span_start - images * IMG_TOK
    is_slot = image_of_slot[None, :] == images[:, None]
    slot_of = jnp.sum(jnp.where(is_slot, images[None, :], 0), axis=1)

    text_all, columns, gains, latents_all, down_all = opening(
        text_embed.reshape(2, UNIT, HD),
        patch_out,
        jnp.broadcast_to(norm_gain[None, :], (16, HD)),
        latents.reshape(16, 512),
        jnp.pad(down_conv, ((0, 8), (0, 64))),
    )
    down = jnp.concatenate([down_all[i, :72, :64] for i in range(4)], axis=1)
    gain = gains[:, 0, :].reshape(1, 4096)

    text_rows = ctx * UNIT + jnp.arange(UNIT, dtype=jnp.int32)
    seen = jnp.sum((before[None, :] <= text_rows[:, None]).astype(jnp.int32), axis=1)
    text = jnp.take(text_all.reshape(8192, HD), text_rows + IMG_TOK * seen, axis=0, mode="clip")
    image = tokens_of(windows(latents_all), down, patch_in)

    (x_all,) = gather_call([("xz", [text, image])], 3)
    q, kv = qkv_of(
        x_all, gain, query_weight, key_weight, value_weight, query_gain.reshape(1, HD), key_gain.reshape(1, HD)
    )
    (kv_all,) = gather_call([("ctx", [kv[0, 0], kv[0, 1], kv[1, 0], kv[1, 1]])], 4)

    slots = ctx * 2 + jnp.arange(2, dtype=jnp.int32)
    here = slots[:, None] == images[None, :]
    own_image = jnp.sum(jnp.where(here, image_of_slot[None, :], 0), axis=1)
    own_before = jnp.sum(jnp.where(own_image[:, None] == images[None, :], before[None, :], 0), axis=1)
    spread = lambda pair: jnp.broadcast_to(pair[:, None], (2, IMG_TOK)).reshape(UNIT)
    lim_t = jnp.concatenate([text_rows + 1, spread(own_before)])
    lim_i = jnp.concatenate([seen * IMG_TOK, spread((own_image + 1) * IMG_TOK)])
    tops = jnp.stack([jnp.max(lim_t.reshape(4, TILE), axis=1), jnp.max(lim_i.reshape(4, TILE), axis=1)])
    attended = attention(tops, slot_of, q.reshape(1024, HD), lim_t[:, None], lim_i[:, None], kv_all)

    (mixed_all,) = gather_call([("xz", [attended[:UNIT], attended[UNIT:]])], 5)
    work = project(mixed_all, out_weight, jnp.stack([text, image]))
    rows_all, work_all = gather_call([("xz", [work[1]]), ("ctx", [work[0], work[1]])], 6)
    up = expand(rows_all, columns.reshape(4096, HD))
    grid = bands(up.reshape(2, IMG_TOK, HD))
    edges = jnp.stack([(tile == 0).astype(jnp.int32), (tile == 7).astype(jnp.int32)])
    cells = up_block(edges, grid, up_weights(up_conv))
    noise_pred = cells.reshape(2, 2, 16, 4, 32).transpose(0, 1, 3, 2, 4).reshape(2, 8, 512)

    positions = ctx * 1024 + jnp.arange(1024, dtype=jnp.int32)
    started = (span_start[None, :] <= positions[:, None]).astype(jnp.int32)
    passed = jnp.sum((span_start[None, :] + IMG_TOK <= positions[:, None]).astype(jnp.int32), axis=1)
    inside = jnp.sum(started, axis=1) > passed
    now = passed[:, None] == images[None, :]
    slot = jnp.sum(jnp.where(now, slot_of[None, :], 0), axis=1)
    start = jnp.sum(jnp.where(now, span_start[None, :], 0), axis=1)
    row = positions - passed * IMG_TOK
    text_source = row // UNIT * 1024 + row % UNIT
    image_source = slot // 2 * 1024 + UNIT + slot % 2 * IMG_TOK + positions - start
    layer_out = jnp.take(
        work_all.reshape(8192, HD), jnp.where(inside, image_source, text_source), axis=0, mode="clip"
    )
    return layer_out, noise_pred


def solution(mesh):
    return jax.shard_map(
        shards,
        mesh=mesh,
        in_specs=(
            P("ctx", ("tile", "mp")),
            P("ctx", "tile", None),
            P(None, "mp"),
            P(None, ("tile", "mp")),
            P(("tile", "mp")),
            P(None, ("tile", "mp")),
            P(None, ("tile", "mp")),
            P(None, ("tile", "mp")),
            P(),
            P(),
            P(None, ("tile", "mp")),
            P(("tile", "mp"), None),
            P(),
            P(),
            P(),
        ),
        out_specs=(P("ctx", ("tile", "mp")), P("ctx", "tile", None)),
        check_vma=False,
    )
```

```python
import functools

import jax
import jax.numpy as jnp
from jax import lax
from jax.experimental import pallas as pl
from jax.experimental.pallas import tpu as pltpu
from jax.sharding import PartitionSpec as P

HD = 128
CH = 256
CIN = 8
PATCH = 4
IMG_TOK = 256
UNIT = 512
EPSILON = 1e-05
NEGATIVE = -1e30
MESH = pl.DeviceIdType.MESH
ANY = pl.BlockSpec(memory_space=pl.ANY)
BF = jnp.bfloat16
F32 = jnp.float32


def remote(src, dst, send, recv, device):
    return pltpu.make_async_remote_copy(
        src_ref=src, dst_ref=dst, send_sem=send, recv_sem=recv, device_id=device, device_id_type=MESH
    )


def barrier(devices):
    sem = pltpu.get_barrier_semaphore()
    for device in devices:
        pl.semaphore_signal(sem, inc=1, device_id=device, device_id_type=MESH)
    pl.semaphore_wait(sem, len(devices))


def coordinates():
    return lax.axis_index("ctx"), lax.axis_index("tile"), lax.axis_index("mp")


class Gather:
    def __init__(self, over, sources, dst, send, recv, local):
        ctx, tile, mp = coordinates()
        self.dst, self.send, self.recv, self.local = dst, send, recv, local
        self.rows = dst.shape[2]
        parts = dst.shape[1] // len(sources)
        self.sources = [
            source.at[pl.ds(part * self.rows, self.rows)] for source in sources for part in range(parts)
        ]
        self.pending, self.count = [], 0
        if over != "ctx":
            a = tile // 2
            self.a, self.r, self.core = a, mp, tile % 2
            self.dev = lambda a, r, core: (ctx, a * 2 + core, r)
            if over == "xz":
                self.slot = lambda a, r, core: (a * 2 + core) * 4 + r
            else:
                self.slot = lambda a, r, core: a * 2 + core
            self.sibling = 1 - self.core
            near = a + 1 - 2 * (a % 2)
            cross = 2 - a // 2
            self.order = [a, near, cross, 3 * (1 - a // 2)]
            self.onward = [None, 3 - a, near, near]
            self.middle = (a == 1) | (a == 2)
            self.inner, self.outer = 1 + a % 2, near
            self.others = [(a + d) % 4 for d in range(1, 4)]
        else:
            a = ctx // 4
            self.a, self.r, self.core = a, ctx % 4, 0
            self.dev = lambda a, r, core: (a * 4 + r, tile, mp)
            self.slot = lambda a, r, core: a * 4 + r
            self.sibling = None
            self.order = [a, 1 - a]
            self.middle = None
            self.inner = 1 - a
            self.others = [1 - a]
        self.right, self.left, self.far = (self.r + 1) % 4, (self.r + 3) % 4, (self.r + 2) % 4

    def partners(self):
        found = [self.dev(a, self.r, self.core) for a in self.others]
        found += [self.dev(self.a, self.right, self.core), self.dev(self.a, self.left, self.core)]
        if self.sibling is not None:
            found.append(self.dev(self.a, self.r, self.sibling))
        return found

    def push(self, src, slot, unit, device, half=None, when=None):
        dst = self.dst.at[slot, unit]
        which = 0
        if half is not None:
            rows = pl.ds(half * (self.rows // 2), self.rows // 2)
            src, dst, which = src.at[rows], dst.at[rows], half
        count = self.count
        self.count += 1
        make = lambda: remote(src, dst, self.send.at[count], self.recv.at[unit, slot, which], device)
        self.pending.append((make, when))
        if when is None:
            make().start()
        else:
            pl.when(when)(lambda: make().start())

    def arrive(self, slot, unit, half=None):
        dst = self.dst.at[slot, unit]
        which = 0
        if half is not None:
            dst, which = dst.at[pl.ds(half * (self.rows // 2), self.rows // 2)], half
        device = self.dev(self.a, self.right, self.core)
        remote(dst, dst, self.send.at[0], self.recv.at[unit, slot, which], device).wait_recv()

    def run(self):
        own = self.slot(self.a, self.r, self.core)
        units = len(self.sources)
        right = self.dev(self.a, self.right, self.core)
        left = self.dev(self.a, self.left, self.core)
        twin = None if self.sibling is None else self.dev(self.a, self.r, self.sibling)
        locals_ = []
        for u, src in enumerate(self.sources):
            self.push(src, own, u, self.dev(self.inner, self.r, self.core))
            if self.middle is not None:
                self.push(src, own, u, self.dev(self.outer, self.r, self.core), when=self.middle)
            self.push(src, own, u, right)
            self.push(src, own, u, left)
            if twin is not None:
                self.push(src, own, u, twin)
            copy = pltpu.make_async_copy(src, self.dst.at[own, u], self.local.at[u])
            copy.start()
            locals_.append(copy)
        yield
        steps = [(k, u) for k in range(len(self.order)) for u in range(units)]
        for n in range(len(steps) + 2 * units):
            if n < len(steps):
                k, u = steps[n]
                if k > 0:
                    slot = self.slot(self.order[k], self.r, self.core)
                    self.arrive(slot, u)
                    src = self.dst.at[slot, u]
                    if self.middle is not None:
                        device = self.dev(self.onward[k], self.r, self.core)
                        self.push(src, slot, u, device, when=self.middle)
                    self.push(src, slot, u, right)
                    self.push(src, slot, u, left)
                    if twin is not None:
                        self.push(src, slot, u, twin)
                    yield
            if 0 <= n - units < len(steps):
                k, u = steps[n - units]
                a = self.order[k]
                for ring, target, half in ((self.left, right, 0), (self.right, left, 1)):
                    slot = self.slot(a, ring, self.core)
                    self.arrive(slot, u)
                    self.push(self.dst.at[slot, u], slot, u, target, half)
                    if twin is not None:
                        self.push(self.dst.at[slot, u], slot, u, twin)
                yield
            if 0 <= n - 2 * units < len(steps):
                k, u = steps[n - 2 * units]
                slot = self.slot(self.order[k], self.far, self.core)
                self.arrive(slot, u, 0)
                self.arrive(slot, u, 1)
                if twin is not None:
                    self.push(self.dst.at[slot, u], slot, u, twin)
                yield
        if twin is not None:
            for k in range(len(self.order)):
                for ring in (self.r, self.left, self.right, self.far):
                    for u in range(units):
                        self.arrive(self.slot((self.a + k) % 4, ring, self.sibling), u)
            yield
        self.close(locals_)

    def close(self, locals_):
        for copy in locals_:
            copy.wait()
        for make, when in self.pending:
            if when is None:
                make().wait_send()
            else:
                pl.when(when)(lambda make=make: make().wait_send())

    def run_column(self):
        own = self.slot(self.a, self.r, self.core)
        units = len(self.sources)
        twin = self.dev(self.a, self.r, self.sibling)
        locals_ = []
        for u, src in enumerate(self.sources):
            self.push(src, own, u, self.dev(self.inner, self.r, self.core))
            self.push(src, own, u, self.dev(self.outer, self.r, self.core), when=self.middle)
            self.push(src, own, u, twin)
            copy = pltpu.make_async_copy(src, self.dst.at[own, u], self.local.at[u])
            copy.start()
            locals_.append(copy)
        for u in range(units):
            for k in range(1, 4):
                slot = self.slot(self.order[k], self.r, self.core)
                self.arrive(slot, u)
                src = self.dst.at[slot, u]
                self.push(src, slot, u, self.dev(self.onward[k], self.r, self.core), when=self.middle)
                self.push(src, slot, u, twin)
            locals_[u].wait()
            for k in range(4):
                self.arrive(self.slot(self.order[k], self.r, self.sibling), u)
            yield u
        self.close([])


def interleave(runs):
    runs = list(runs)
    while runs:
        left = []
        for run in runs:
            try:
                next(run)
                left.append(run)
            except StopIteration:
                pass
        runs = left


def gather_sems(over, units):
    slots, sends = {"xz": (32, 37), "ctx": (8, 12), "z": (8, 12)}[over]
    return [
        pltpu.SemaphoreType.DMA((units * sends,)),
        pltpu.SemaphoreType.DMA((units, slots, 2)),
        pltpu.SemaphoreType.DMA((units,)),
    ]


class Spread:
    def __init__(self, src, dst, send, recv, local):
        self.ctx, tile, mp = coordinates()
        self.me = tile * 4 + mp
        self.src, self.dst, self.send, self.recv, self.local = src, dst, send, recv, local

    def peer(self, i):
        peer = (self.me + i) % 32
        return peer, (self.ctx, peer // 4, peer % 4)

    def partners(self):
        return [self.peer(i)[1] for i in range(1, 32)]

    def copy(self, i):
        return remote(self.src, self.dst.at[self.me], self.send.at[i], self.recv.at[self.me], self.peer(i)[1])

    def run(self):
        own = pltpu.make_async_copy(self.src, self.dst.at[self.me], self.local.at[0])
        own.start()

        def start(i, carry):
            self.copy(i).start()
            return carry

        def finish(i, carry):
            self.copy(i).wait_send()
            peer, device = self.peer(i)
            remote(self.src, self.dst.at[peer], self.send.at[i], self.recv.at[peer], device).wait_recv()
            return carry

        yield
        lax.fori_loop(1, 32, start, 0)
        yield
        lax.fori_loop(1, 32, finish, 0)
        own.wait()


def spread_sems():
    return [pltpu.SemaphoreType.DMA((32,)), pltpu.SemaphoreType.DMA((32,)), pltpu.SemaphoreType.DMA((1,))]


class Weights:
    def __init__(self, out_weight, patch_out, out_all, patch_all, out_send, out_recv, patch_send, patch_recv, local):
        self.ctx, self.tile, self.mp = coordinates()
        self.core, self.z = self.tile % 2, self.tile // 2
        self.out_weight, self.patch_out, self.out_all, self.patch_all = out_weight, patch_out, out_all, patch_all
        self.out_send, self.out_recv, self.patch_send, self.patch_recv = out_send, out_recv, patch_send, patch_recv
        self.local = local

    def mates(self):
        found = []
        for i in range(1, 8):
            core, mp = (self.core + i // 4) % 2, (self.mp + i) % 4
            found.append((core, mp, (self.ctx, self.z * 2 + core, mp)))
        return found

    def partners(self):
        return [device for _, _, device in self.mates()]

    def columns(self, core, mp):
        return self.patch_out.at[:, pl.ds(pl.multiple_of(mp * 1024 + core * 512, 512), 512)]

    def run(self):
        own = self.core * 4 + self.mp
        copies = []
        for i, (core, mp, device) in enumerate(self.mates()):
            if i < 3:
                copies.append(
                    remote(
                        self.out_weight.at[:, mp], self.out_all.at[self.mp], self.out_send.at[i],
                        self.out_recv.at[self.mp], device,
                    )
                )
            copies.append(
                remote(
                    self.columns(core, mp), self.patch_all.at[own], self.patch_send.at[i],
                    self.patch_recv.at[own], device,
                )
            )
        here = [
            pltpu.make_async_copy(self.out_weight.at[:, self.mp], self.out_all.at[self.mp], self.local.at[0]),
            pltpu.make_async_copy(self.columns(self.core, self.mp), self.patch_all.at[own], self.local.at[1]),
        ]
        for copy in copies + here:
            copy.start()
        yield
        yield
        for i, (core, mp, device) in enumerate(self.mates()):
            slot = core * 4 + mp
            if i < 3:
                dst = self.out_all.at[mp]
                remote(dst, dst, self.out_send.at[0], self.out_recv.at[mp], device).wait_recv()
            dst = self.patch_all.at[slot]
            remote(dst, dst, self.patch_send.at[0], self.patch_recv.at[slot], device).wait_recv()
        for copy in copies:
            copy.wait_send()
        for copy in here:
            copy.wait()


def weight_sems():
    return [pltpu.SemaphoreType.DMA((n,)) for n in (3, 4, 7, 8, 2)]


def merge(groups):
    return [device for group in groups for device in group]


def gather_call(jobs, collective_id, gain=None, weights=None, parts=1):
    flat = [array for _, arrays in jobs for array in arrays]
    extra = ([gain] if gain is not None else []) + (list(weights) if weights is not None else [])
    inputs_in = flat + extra

    def kernel(*refs):
        inputs, refs = refs[: len(inputs_in)], refs[len(inputs_in) :]
        outputs, sems = refs[: len(shapes)], refs[len(shapes) :]
        built, at = [], 0
        for i, (over, arrays) in enumerate(jobs):
            sources = inputs[at : at + len(arrays)]
            at += len(arrays)
            built.append(Gather(over, sources, outputs[i], *sems[3 * i : 3 * i + 3]))
        rest = sems[3 * len(jobs) :]
        if gain is not None:
            built.append(Spread(inputs[at], outputs[len(jobs)], *rest))
        if weights is not None:
            built.append(Weights(inputs[at], inputs[at + 1], outputs[len(jobs)], outputs[len(jobs) + 1], *rest))
        barrier(merge(job.partners() for job in built))
        interleave([job.run() for job in built])

    shapes, scratch = [], []
    for over, arrays in jobs:
        slots = 32 if over == "xz" else 8
        rows, width = arrays[0].shape
        shapes.append(jax.ShapeDtypeStruct((slots, len(arrays) * parts, rows // parts, width), BF))
        scratch += gather_sems(over, len(arrays) * parts)
    if gain is not None:
        shapes.append(jax.ShapeDtypeStruct((32,) + gain.shape, BF))
        scratch += spread_sems()
    if weights is not None:
        shapes += [jax.ShapeDtypeStruct((4, 8, HD, HD), BF), jax.ShapeDtypeStruct((8, HD, 512), BF)]
        scratch += weight_sems()
    return pl.pallas_call(
        kernel,
        out_shape=shapes,
        in_specs=[ANY] * len(inputs_in),
        out_specs=[ANY] * len(shapes),
        scratch_shapes=scratch,
        compiler_params=pltpu.CompilerParams(collective_id=collective_id, has_side_effects=True),
    )(*inputs_in)


def opening_kernel(
    latents, down, latents_all, down_all, lat_send, lat_recv, down_send, down_recv, own_sem
):
    ctx, tile, mp = coordinates()
    tiles = [((tile + i) % 8) for i in range(1, 8)]
    mps = [((mp + i) % 4) for i in range(1, 4)]
    barrier([(ctx, t, mp) for t in tiles] + [(ctx, tile, m) for m in mps])
    copies = []
    for i, t in enumerate(tiles):
        copies.append(remote(latents, latents_all.at[tile], lat_send.at[i], lat_recv.at[tile], (ctx, t, mp)))
    for i, m in enumerate(mps):
        copies.append(remote(down, down_all.at[mp], down_send.at[i], down_recv.at[mp], (ctx, tile, m)))
    own = [
        pltpu.make_async_copy(latents, latents_all.at[tile], own_sem.at[0]),
        pltpu.make_async_copy(down, down_all.at[mp], own_sem.at[1]),
    ]
    for copy in copies + own:
        copy.start()
    for t in tiles:
        remote(latents, latents_all.at[t], lat_send.at[0], lat_recv.at[t], (ctx, t, mp)).wait_recv()
    for m in mps:
        remote(down, down_all.at[m], down_send.at[0], down_recv.at[m], (ctx, tile, m)).wait_recv()
    for copy in copies:
        copy.wait_send()
    for copy in own:
        copy.wait()


def opening(latents, down):
    dma = pltpu.SemaphoreType.DMA
    return pl.pallas_call(
        opening_kernel,
        out_shape=[
            jax.ShapeDtypeStruct((8,) + latents.shape, BF),
            jax.ShapeDtypeStruct((4,) + down.shape, BF),
        ],
        in_specs=[ANY] * 2,
        out_specs=[ANY] * 2,
        scratch_shapes=[dma((7,)), dma((8,)), dma((3,)), dma((4,)), dma((2,))],
        compiler_params=pltpu.CompilerParams(collective_id=1, has_side_effects=True),
    )(latents, down)


MIX = 256


def mix_kernel(
    image, text, w_ref, image_stream, text_stream, image_out, text_out,
    blocks, outgoing, incoming, send, recv, local, part_send, part_recv,
):
    ctx, tile, mp = coordinates()
    units = blocks.shape[1]
    job = Gather("z", [image, text], blocks, send, recv, local)
    rings = [(mp + 1) % 4, (mp + 3) % 4, (mp + 2) % 4]
    barrier(merge([job.partners(), [(ctx, tile, rings[2])]]))

    def settle(u):
        for i, ring in enumerate(rings):
            dst = incoming.at[ring, u]
            remote(dst, dst, part_send.at[0, 0], part_recv.at[ring, u], (ctx, tile, ring)).wait_recv()
        stream, out, row = (image_stream, image_out, u * MIX) if u < 2 else (text_stream, text_out, u * MIX - UNIT)
        total = stream[row : row + MIX].astype(F32) + kept[u]
        for ring in rings:
            total = total + incoming[ring, u].astype(F32)
        out[row : row + MIX] = total.astype(BF)

    kept, copies = {}, []
    for u in job.run_column():
        x = jnp.concatenate([blocks[t, u] for t in range(8)], axis=1)
        for i, ring in enumerate(rings):
            outgoing[i, u] = jnp.dot(x, w_ref[ring], preferred_element_type=F32).astype(BF)
            copy = remote(
                outgoing.at[i, u], incoming.at[mp, u], part_send.at[i, u], part_recv.at[mp, u], (ctx, tile, ring)
            )
            copy.start()
            copies.append(copy)
        kept[u] = jnp.dot(x, w_ref[mp], preferred_element_type=F32)
        if u > 0:
            settle(u - 1)
    settle(units - 1)
    for copy in copies:
        copy.wait_send()


def mix(image, text, w, image_stream, text_stream):
    dma = pltpu.SemaphoreType.DMA
    units = 2 * UNIT // MIX
    vmem = pl.BlockSpec(memory_space=pltpu.VMEM)
    return pl.pallas_call(
        mix_kernel,
        out_shape=[jax.ShapeDtypeStruct((UNIT, HD), BF)] * 2,
        in_specs=[ANY, ANY, vmem, vmem, vmem],
        out_specs=[vmem, vmem],
        scratch_shapes=[
            pltpu.VMEM((8, units, MIX, HD), BF),
            pltpu.VMEM((3, units, MIX, HD), BF),
            pltpu.VMEM((4, units, MIX, HD), BF),
        ]
        + gather_sems("z", units)
        + [dma((3, units)), dma((4, units))],
        compiler_params=pltpu.CompilerParams(
            collective_id=2, has_side_effects=True, vmem_limit_bytes=32 * 1024 * 1024
        ),
    )(image, text, w, image_stream, text_stream)


def up_kernel(
    image, text, w_ref, up_ref, image_work, text_work, cells_ref,
    blocks, product, terms, grid, above, below,
    image_send, image_recv, image_local, text_send, text_recv, text_local,
    block_send, block_recv, twin_send, twin_recv, term_send, term_recv, grid_send, grid_recv, edge_send, edge_recv,
    own_sem,
):
    ctx, tile, mp = coordinates()
    z, core = tile // 2, tile % 2
    jobs = [
        Gather("ctx", [image], image_work, image_send, image_recv, image_local),
        Gather("ctx", [text], text_work, text_send, text_recv, text_local),
    ]
    me = tile * 4 + mp
    group = []
    for i in range(1, 32):
        peer = (me + i) % 32
        group.append((ctx, peer // 4, peer % 4))
    barrier(merge([group, jobs[0].partners()]))
    rings = [(mp + 1) % 4, (mp + 3) % 4, (mp + 2) % 4]
    twin = (ctx, z * 2 + 1 - core, mp)
    own = core * 4 + mp
    copies = []

    def go(copy):
        copy.start()
        copies.append(copy)

    for i, ring in enumerate(rings):
        go(remote(image, blocks.at[own], block_send.at[i], block_recv.at[mp], (ctx, tile, ring)))
    go(remote(image, blocks.at[own], twin_send.at[mp], twin_recv.at[mp], twin))
    mine = pltpu.make_async_copy(image, blocks.at[own], own_sem.at[0])
    mine.start()
    runs = [job.run() for job in jobs]
    for run in runs:
        next(run)
    for ring in rings:
        dst = blocks.at[core * 4 + ring]
        remote(dst, dst, block_send.at[0], block_recv.at[ring], (ctx, tile, ring)).wait_recv()
        go(remote(dst, dst, twin_send.at[ring], twin_recv.at[ring], twin))
    mine.wait()
    for ring in range(4):
        dst = blocks.at[(1 - core) * 4 + ring]
        remote(dst, dst, twin_send.at[0], twin_recv.at[ring], twin).wait_recv()
    for s in range(2):
        x = jnp.concatenate([blocks[i, s * IMG_TOK : (s + 1) * IMG_TOK] for i in range(8)], axis=1)
        part = jnp.dot(x, w_ref[...].reshape(1024, 512), preferred_element_type=F32).astype(BF)
        product[:, s] = part.reshape(8, 32, 512)
    tiles = [(tile + i) % 8 for i in (2, 6, 4, 1, 7, 3, 5)]
    for i, t in enumerate(tiles):
        go(remote(product.at[t], terms.at[tile], term_send.at[i], term_recv.at[tile], (ctx, t, mp)))
    mine = pltpu.make_async_copy(product.at[tile], terms.at[tile], own_sem.at[1])
    mine.start()
    for run in runs:
        next(run)
    for t in tiles:
        dst = terms.at[t]
        remote(dst, dst, term_send.at[0], term_recv.at[t], (ctx, t, mp)).wait_recv()
    mine.wait()
    for c in range(2):
        total = terms[c].astype(F32)
        for k in range(1, 4):
            total = total + terms[2 * k + c].astype(F32)
        grid[mp, :, :, c * 512 : (c + 1) * 512] = silu(total).astype(BF)

    for i, ring in enumerate(rings):
        go(remote(grid.at[mp], grid.at[mp], grid_send.at[i], grid_recv.at[mp], (ctx, tile, ring)))
    down_edge = (mp == 3) & (tile < 7)
    up_edge = (mp == 0) & (tile > 0)
    down_copies = [
        lambda m=m: remote(
            grid.at[mp, :, pl.ds(16, 16)], above, edge_send.at[m], edge_recv.at[0], (ctx, (tile + 1) % 8, m)
        )
        for m in range(4)
    ]
    up_copies = [
        lambda m=m: remote(
            grid.at[mp, :, pl.ds(0, 16)], below, edge_send.at[m], edge_recv.at[1], (ctx, (tile + 7) % 8, m)
        )
        for m in range(4)
    ]

    @pl.when(down_edge)
    def _():
        for make in down_copies:
            make().start()

    @pl.when(up_edge)
    def _():
        for make in up_copies:
            make().start()

    @pl.when(tile == 0)
    def _():
        above[...] = jnp.zeros_like(above)

    @pl.when(tile == 7)
    def _():
        below[...] = jnp.zeros_like(below)

    for ring in rings:
        dst = grid.at[ring]
        remote(dst, dst, grid_send.at[0], grid_recv.at[ring], (ctx, tile, ring)).wait_recv()

    @pl.when(tile > 0)
    def _():
        remote(above, above, edge_send.at[0], edge_recv.at[0], (ctx, tile, rings[0])).wait_recv()

    @pl.when(tile < 7)
    def _():
        remote(below, below, edge_send.at[0], edge_recv.at[1], (ctx, tile, rings[0])).wait_recv()

    sums = [jnp.zeros((64, HD), F32) for _ in range(3)]
    for wr in range(6):
        for wc in range(6):
            pc = 3 if wc == 0 else 0 if wc == 5 else wc - 1
            lanes = slice(pc * CH, (pc + 1) * CH)
            if wr == 0:
                a = jnp.concatenate([above[:, :, lanes], grid[3, :, 0:16, lanes]], axis=1)
            elif wr == 5:
                a = jnp.concatenate([grid[0, :, 16:32, lanes], below[:, :, lanes]], axis=1)
            else:
                a = grid[wr - 1, :, :, lanes]
            cell = wr * 6 + wc
            term = jnp.dot(
                a.reshape(64, CH), up_ref[:, cell * HD : (cell + 1) * HD], preferred_element_type=F32
            )
            which = 0 if wc == 0 else 2 if wc == 5 else 1
            sums[which] = sums[which] + term
    column = lax.broadcasted_iota(jnp.int32, (64, HD), 0) % 16
    blank = jnp.zeros((1, HD), F32)
    from_left = jnp.concatenate([blank, sums[0][:63]], axis=0)
    from_right = jnp.concatenate([sums[2][1:], blank], axis=0)
    cells_ref[...] = (
        sums[1] + jnp.where(column == 0, 0.0, from_left) + jnp.where(column == 15, 0.0, from_right)
    )
    interleave(runs)
    for copy in copies:
        copy.wait_send()

    @pl.when(down_edge)
    def _():
        for make in down_copies:
            make().wait_send()

    @pl.when(up_edge)
    def _():
        for make in up_copies:
            make().wait_send()


def up_block(image, text, w, up_w):
    dma = pltpu.SemaphoreType.DMA
    vmem = pl.BlockSpec(memory_space=pltpu.VMEM)
    work = jax.ShapeDtypeStruct((8, 1, UNIT, HD), BF)
    return pl.pallas_call(
        up_kernel,
        out_shape=[work, work, jax.ShapeDtypeStruct((64, HD), F32)],
        in_specs=[ANY, ANY, vmem, vmem],
        out_specs=[ANY, ANY, vmem],
        scratch_shapes=[
            pltpu.VMEM((8, UNIT, HD), BF),
            pltpu.VMEM((8, 2, 32, 512), BF),
            pltpu.VMEM((8, 2, 32, 512), BF),
            pltpu.VMEM((4, 2, 32, 1024), BF),
            pltpu.VMEM((2, 16, 1024), BF),
            pltpu.VMEM((2, 16, 1024), BF),
        ]
        + gather_sems("ctx", 1)
        + gather_sems("ctx", 1)
        + [dma((n,)) for n in (3, 4, 4, 4, 7, 8, 3, 4, 4, 2, 2)],
        compiler_params=pltpu.CompilerParams(
            collective_id=6, has_side_effects=True, vmem_limit_bytes=32 * 1024 * 1024
        ),
    )(image, text, w, up_w)


def silu(v):
    half = 0.5 * v
    return half + half * jnp.tanh(half)


def window_rows(latents):
    wide = jnp.pad(latents, ((0, 0), (0, 0), (8, 32)))
    before = wide[:, :, 0:512].reshape(2, 8, 16, 32)[..., :8]
    middle = latents.reshape(2, 8, 16, 32)
    after = wide[:, :, 40:552].reshape(2, 8, 16, 32)[..., :8]
    joined = jnp.concatenate([before, middle, after], axis=-1)
    return jnp.pad(joined, ((0, 0), (0, 0), (0, 0), (0, 80)))


def down_weights(down_all):
    down = jnp.concatenate([down_all[i, :72, :64] for i in range(4)], axis=1).reshape(3, 24, CH)
    return jnp.stack([jnp.pad(down, ((0, 0), (8 * c, 104 - 8 * c), (0, 0))) for c in range(4)]).reshape(4, 384, CH)


def tokens_kernel(g_ref, w_ref, patch_ref, out_ref, rows, total):
    px = pl.program_id(0)

    @pl.when(px == 0)
    def _():
        rows[...] = jnp.zeros_like(rows)
        for t in range(8):
            for s in range(2):
                for i in range(8):
                    r = 1 + 8 * t + i
                    rows[s, r // 4, r % 4] = g_ref[t, s, i]

    def window_row(k):
        return rows[:, pl.ds(k // 4, 16), k % 4].reshape(UNIT, HD)

    lhs = jnp.concatenate([window_row(px), window_row(px + 1), window_row(px + 2)], axis=1)
    acts = [silu(jnp.dot(lhs, w_ref[c], preferred_element_type=F32)).astype(BF) for c in range(4)]
    term = jnp.dot(jnp.concatenate(acts, axis=1), patch_ref[...], preferred_element_type=F32)

    @pl.when(px == 0)
    def _():
        total[...] = term

    @pl.when(px > 0)
    def _():
        total[...] += term

    @pl.when(px == 3)
    def _():
        out_ref[...] = total[...].astype(BF)


def tokens_of(latents_all, w, patch_in):
    return pl.pallas_call(
        tokens_kernel,
        grid=(4,),
        out_shape=jax.ShapeDtypeStruct((UNIT, HD), BF),
        in_specs=[
            pl.BlockSpec((8, 2, 8, 16, HD), lambda i: (0, 0, 0, 0, 0)),
            pl.BlockSpec((4, 384, CH), lambda i: (0, 0, 0)),
            pl.BlockSpec((4 * CH, HD), lambda i: (i, 0)),
        ],
        out_specs=pl.BlockSpec((UNIT, HD), lambda i: (0, 0)),
        scratch_shapes=[pltpu.VMEM((2, 17, 4, 16, HD), BF), pltpu.VMEM((UNIT, HD), F32)],
    )(latents_all, w, patch_in)


TILE = 256


def qkv_kernel(x_ref, gain_ref, wq_ref, wk_ref, wv_ref, qg_ref, kg_ref, q_ref, k_ref, v_ref):
    squares = jnp.zeros((TILE, HD), F32)
    for i in range(32):
        part = x_ref[i, 0].astype(F32)
        squares += part * part
    scale = lax.rsqrt(jnp.sum(squares, axis=1, keepdims=True) * (1.0 / 4096.0) + EPSILON)
    normed = jnp.concatenate(
        [
            (x_ref[i, 0].astype(F32) * scale * gain_ref[:, i * HD : (i + 1) * HD].astype(F32)).astype(BF)
            for i in range(32)
        ],
        axis=1,
    )

    def head(weight, gain, factor):
        raw = jnp.dot(normed, weight, preferred_element_type=F32)
        mean = jnp.mean(raw * raw, axis=1, keepdims=True)
        return (raw * lax.rsqrt(mean + EPSILON) * gain * factor).astype(BF)

    q_ref[...] = head(wq_ref[...], qg_ref[...], HD**-0.5)
    k_ref[...] = head(wk_ref[...], kg_ref[...], 1.0)
    v_ref[...] = jnp.dot(normed, wv_ref[...], preferred_element_type=F32).astype(BF)


def qkv_of(x, gain, wq, wk, wv, qg, kg):
    rows = pl.BlockSpec((TILE, HD), lambda i: (i, 0))
    weight = pl.BlockSpec((4096, HD), lambda i: (0, 0))
    small = pl.BlockSpec((1, HD), lambda i: (0, 0))
    return pl.pallas_call(
        qkv_kernel,
        grid=(UNIT // TILE,),
        out_shape=[jax.ShapeDtypeStruct((UNIT, HD), BF)] * 3,
        in_specs=[
            pl.BlockSpec((32, 1, TILE, HD), lambda i: (0, 0, i, 0)),
            pl.BlockSpec((1, 4096), lambda i: (0, 0)),
            weight,
            weight,
            weight,
            small,
            small,
        ],
        out_specs=[rows] * 3,
        compiler_params=pltpu.CompilerParams(vmem_limit_bytes=40 * 1024 * 1024),
    )(x, gain, wq, wk, wv, qg, kg)


def attention_kernel(top_ref, slot_ref, q_ref, lim_t_ref, lim_i_ref, text_ref, image_ref, out_ref):
    tile = pl.program_id(0)
    q = q_ref[...]
    cols = lax.broadcasted_iota(jnp.int32, (TILE, 1024), 1)

    def step(carry, k, v, limit):
        top, total, acc = carry
        s = lax.dot_general(q, k, (((1,), (1,)), ((), ())), preferred_element_type=F32)
        s = jnp.where(cols < limit, s, NEGATIVE)
        new = jnp.maximum(top, jnp.max(s, axis=1, keepdims=True))
        w = jnp.exp(s - new)
        factor = jnp.exp(top - new)
        total = total * factor + jnp.sum(w, axis=1, keepdims=True)
        acc = acc * factor + jnp.dot(w.astype(BF), v, preferred_element_type=F32)
        return new, total, acc

    def text_step(n, carry):
        k = jnp.concatenate([text_ref[2 * n, 0], text_ref[2 * n + 1, 0]], axis=0)
        v = jnp.concatenate([text_ref[2 * n, 1], text_ref[2 * n + 1, 1]], axis=0)
        return step(carry, k, v, lim_t_ref[...] - n * 1024)

    def image_step(n, carry):
        ks, vs = [], []
        for u in range(4):
            slot = slot_ref[n * 4 + u]
            rows = pl.ds(pl.multiple_of((slot % 2) * IMG_TOK, IMG_TOK), IMG_TOK)
            ks.append(image_ref[slot // 2, 0, rows])
            vs.append(image_ref[slot // 2, 1, rows])
        return step(carry, jnp.concatenate(ks, axis=0), jnp.concatenate(vs, axis=0), lim_i_ref[...] - n * 1024)

    carry = (jnp.full((TILE, 1), NEGATIVE, F32), jnp.zeros((TILE, 1), F32), jnp.zeros((TILE, HD), F32))
    carry = lax.fori_loop(0, (top_ref[1, tile] + 1023) // 1024, image_step, carry)
    carry = lax.fori_loop(0, (top_ref[0, tile] + 1023) // 1024, text_step, carry)
    _, total, acc = carry
    out_ref[...] = (acc / total).astype(BF)


def attention(slots, q, lim_t, lim_i, text, image):
    rows = q.shape[0]
    tops = jnp.stack([jnp.max(lim_t.reshape(-1, TILE), axis=1), jnp.max(lim_i.reshape(-1, TILE), axis=1)])
    whole = pl.BlockSpec((8, 2, UNIT, HD), lambda i, *_: (0, 0, 0, 0))
    grid_spec = pltpu.PrefetchScalarGridSpec(
        num_scalar_prefetch=2,
        grid=(rows // TILE,),
        in_specs=[
            pl.BlockSpec((TILE, HD), lambda i, *_: (i, 0)),
            pl.BlockSpec((TILE, 1), lambda i, *_: (i, 0)),
            pl.BlockSpec((TILE, 1), lambda i, *_: (i, 0)),
            whole,
            whole,
        ],
        out_specs=pl.BlockSpec((TILE, HD), lambda i, *_: (i, 0)),
    )
    return pl.pallas_call(
        attention_kernel,
        grid_spec=grid_spec,
        out_shape=jax.ShapeDtypeStruct((rows, HD), BF),
        compiler_params=pltpu.CompilerParams(vmem_limit_bytes=48 * 1024 * 1024),
    )(tops, slots, q, lim_t[:, None], lim_i[:, None], text, image)


def up_weights(up_conv):
    taps = up_conv.reshape(9, CH, CIN).transpose(1, 0, 2).reshape(CH, 72)
    row = lax.broadcasted_iota(jnp.int32, (72, 36 * HD), 0)
    col = lax.broadcasted_iota(jnp.int32, (72, 36 * HD), 1)
    cell, inner = col // HD, col % HD
    a, b = cell // 6 - inner // 32, cell % 6 - (inner // 8) % 4
    inside = (a >= 0) & (a <= 2) & (b >= 0) & (b <= 2)
    pick = jnp.where(inside & (row == (a * 3 + b) * 8 + inner % 8), 1.0, 0.0).astype(BF)
    return jnp.dot(taps, pick, preferred_element_type=F32).astype(BF)


def shards(
    text_embed,
    latents,
    down_conv,
    patch_in,
    norm_gain,
    query_weight,
    key_weight,
    value_weight,
    query_gain,
    key_gain,
    out_weight,
    patch_out,
    up_conv,
    span_start,
    image_of_slot,
):
    ctx = lax.axis_index("ctx")
    images = jnp.arange(16, dtype=jnp.int32)
    before = span_start - images * IMG_TOK
    is_slot = image_of_slot[None, :] == images[:, None]
    slot_of = jnp.sum(jnp.where(is_slot, images[None, :], 0), axis=1)

    latents_all, down_all = opening(window_rows(latents), jnp.pad(down_conv, ((0, 8), (0, 64))))
    image = tokens_of(latents_all, down_weights(down_all), patch_in)
    text_all, image_all, gains = gather_call(
        [("ctx", [text_embed]), ("xz", [image])], 3, gain=jnp.broadcast_to(norm_gain[None, :], (16, HD)), parts=2
    )
    image_all = image_all.reshape(32, 1, UNIT, HD)
    gain = gains[:, 0, :].reshape(1, 4096)

    text_rows = ctx * UNIT + jnp.arange(UNIT, dtype=jnp.int32)
    seen = jnp.sum((before[None, :] <= text_rows[:, None]).astype(jnp.int32), axis=1)
    text = jnp.take(text_all.reshape(8192, HD), text_rows + IMG_TOK * seen, axis=0, mode="clip")
    heads = (
        gain, query_weight, key_weight, value_weight, query_gain.reshape(1, HD), key_gain.reshape(1, HD)
    )
    image_q, image_k, image_v = qkv_of(image_all, *heads)
    image_kv, text_x = gather_call([("ctx", [image_k, image_v]), ("xz", [text])], 4, parts=2)
    text_x = text_x.reshape(32, 1, UNIT, HD)
    image_kv = image_kv.reshape(8, 2, UNIT, HD)
    text_q, text_k, text_v = qkv_of(text_x, *heads)
    text_kv, out_all, patch_all = gather_call(
        [("ctx", [text_k, text_v])], 5, weights=(out_weight.reshape(8, 4, HD, HD), patch_out), parts=2
    )
    text_kv = text_kv.reshape(8, 2, UNIT, HD)

    slots = ctx * 2 + jnp.arange(2, dtype=jnp.int32)
    here = slots[:, None] == images[None, :]
    own_image = jnp.sum(jnp.where(here, image_of_slot[None, :], 0), axis=1)
    own_before = jnp.sum(jnp.where(own_image[:, None] == images[None, :], before[None, :], 0), axis=1)
    spread = lambda pair: jnp.broadcast_to(pair[:, None], (2, IMG_TOK)).reshape(UNIT)
    image_mix = attention(
        slot_of, image_q, spread(own_before), spread((own_image + 1) * IMG_TOK), text_kv, image_kv
    )
    text_mix = attention(slot_of, text_q, text_rows + 1, seen * IMG_TOK, text_kv, image_kv)

    image_out, text_out = mix(image_mix, text_mix, out_all.reshape(4, 1024, HD), image, text)
    image_work, text_work, cells = up_block(image_out, text_out, patch_all, up_weights(up_conv))
    noise_pred = cells.reshape(2, 2, 16, 4, 32).transpose(0, 1, 3, 2, 4).reshape(2, 8, 512)

    positions = ctx * 1024 + jnp.arange(1024, dtype=jnp.int32)
    started = (span_start[None, :] <= positions[:, None]).astype(jnp.int32)
    passed = jnp.sum((span_start[None, :] + IMG_TOK <= positions[:, None]).astype(jnp.int32), axis=1)
    inside = jnp.sum(started, axis=1) > passed
    now = passed[:, None] == images[None, :]
    slot = jnp.sum(jnp.where(now, slot_of[None, :], 0), axis=1)
    start = jnp.sum(jnp.where(now, span_start[None, :], 0), axis=1)
    row = positions - passed * IMG_TOK
    text_part = jnp.take(text_work.reshape(4096, HD), row, axis=0, mode="clip")
    image_part = jnp.take(
        image_work.reshape(4096, HD), slot * IMG_TOK + positions - start, axis=0, mode="clip"
    )
    layer_out = jnp.where(inside[:, None], image_part, text_part)
    return layer_out, noise_pred


def solution(mesh):
    return jax.shard_map(
        shards,
        mesh=mesh,
        in_specs=(
            P("ctx", ("tile", "mp")),
            P("ctx", "tile", None),
            P(None, "mp"),
            P(None, ("tile", "mp")),
            P(("tile", "mp")),
            P(None, ("tile", "mp")),
            P(None, ("tile", "mp")),
            P(None, ("tile", "mp")),
            P(),
            P(),
            P(None, ("tile", "mp")),
            P(("tile", "mp"), None),
            P(),
            P(),
            P(),
        ),
        out_specs=(P("ctx", ("tile", "mp")), P("ctx", "tile", None)),
        check_vma=False,
    )
```

```python
import functools

import jax
import jax.numpy as jnp
from jax import lax
from jax.experimental import pallas as pl
from jax.experimental.pallas import tpu as pltpu
from jax.sharding import PartitionSpec as P

HD = 128
CH = 256
CIN = 8
PATCH = 4
IMG_TOK = 256
UNIT = 512
EPSILON = 1e-05
NEGATIVE = -1e30
MESH = pl.DeviceIdType.MESH
ANY = pl.BlockSpec(memory_space=pl.ANY)
BF = jnp.bfloat16
F32 = jnp.float32


def remote(src, dst, send, recv, device):
    return pltpu.make_async_remote_copy(
        src_ref=src, dst_ref=dst, send_sem=send, recv_sem=recv, device_id=device, device_id_type=MESH
    )


def barrier(devices):
    sem = pltpu.get_barrier_semaphore()
    for device in devices:
        pl.semaphore_signal(sem, inc=1, device_id=device, device_id_type=MESH)
    pl.semaphore_wait(sem, len(devices))


def coordinates():
    return lax.axis_index("ctx"), lax.axis_index("tile"), lax.axis_index("mp")


LAG = 1.0


class Gather:
    def __init__(self, over, sources, dst, send, recv, local):
        ctx, tile, mp = coordinates()
        self.dst, self.send, self.recv, self.local = dst, send, recv, local
        self.rows = dst.shape[2]
        parts = dst.shape[1] // len(sources)
        self.sources = [
            source.at[pl.ds(part * self.rows, self.rows)] for source in sources for part in range(parts)
        ]
        self.pending, self.count = [], 0
        if over != "ctx":
            a = tile // 2
            self.a, self.r, self.core = a, mp, tile % 2
            self.dev = lambda a, r, core: (ctx, a * 2 + core, r)
            if over == "xz":
                self.slot = lambda a, r, core: (a * 2 + core) * 4 + r
            else:
                self.slot = lambda a, r, core: a * 2 + core
            self.sibling = 1 - self.core
            near = a + 1 - 2 * (a % 2)
            cross = 2 - a // 2
            self.order = [a, near, cross, 3 * (1 - a // 2)]
            self.onward = [None, 3 - a, near, near]
            self.middle = (a == 1) | (a == 2)
            self.inner, self.outer = 1 + a % 2, near
            self.others = [(a + d) % 4 for d in range(1, 4)]
        else:
            a = ctx // 4
            self.a, self.r, self.core = a, ctx % 4, 0
            self.dev = lambda a, r, core: (a * 4 + r, tile, mp)
            self.slot = lambda a, r, core: a * 4 + r
            self.sibling = None
            self.order = [a, 1 - a]
            self.middle = None
            self.inner = 1 - a
            self.others = [1 - a]
        self.right, self.left, self.far = (self.r + 1) % 4, (self.r + 3) % 4, (self.r + 2) % 4

    def partners(self):
        found = [self.dev(a, self.r, self.core) for a in self.others]
        found += [self.dev(self.a, self.right, self.core), self.dev(self.a, self.left, self.core)]
        if self.sibling is not None:
            found.append(self.dev(self.a, self.r, self.sibling))
        return found

    def push(self, src, slot, unit, device, half=None, when=None):
        dst = self.dst.at[slot, unit]
        which = 0
        if half is not None:
            rows = pl.ds(half * (self.rows // 2), self.rows // 2)
            src, dst, which = src.at[rows], dst.at[rows], half
        count = self.count
        self.count += 1
        make = lambda: remote(src, dst, self.send.at[count], self.recv.at[unit, slot, which], device)
        self.pending.append((make, when))
        if when is None:
            make().start()
        else:
            pl.when(when)(lambda: make().start())

    def arrive(self, slot, unit, half=None):
        dst = self.dst.at[slot, unit]
        which = 0
        if half is not None:
            dst, which = dst.at[pl.ds(half * (self.rows // 2), self.rows // 2)], half
        device = self.dev(self.a, self.right, self.core)
        remote(dst, dst, self.send.at[0], self.recv.at[unit, slot, which], device).wait_recv()

    def forward(self, k, unit):
        slot = self.slot(self.order[k], self.r, self.core)
        self.arrive(slot, unit)
        src = self.dst.at[slot, unit]
        if self.middle is not None:
            self.push(src, slot, unit, self.dev(self.onward[k], self.r, self.core), when=self.middle)
        self.push(src, slot, unit, self.dev(self.a, self.right, self.core))
        self.push(src, slot, unit, self.dev(self.a, self.left, self.core))
        self.twin(slot, unit)

    def twin(self, slot, unit):
        if self.sibling is not None:
            src = self.dst.at[slot, unit]
            self.push(src, slot, unit, self.dev(self.a, self.r, self.sibling))

    def halves(self, k, unit):
        for ring, target, half in ((self.left, self.right, 0), (self.right, self.left, 1)):
            slot = self.slot(self.order[k], ring, self.core)
            self.arrive(slot, unit)
            self.push(self.dst.at[slot, unit], slot, unit, self.dev(self.a, target, self.core), half)
            self.twin(slot, unit)

    def ends(self, k, unit):
        slot = self.slot(self.order[k], self.far, self.core)
        self.arrive(slot, unit, 0)
        self.arrive(slot, unit, 1)
        self.twin(slot, unit)

    def events(self, start=0.0):
        units = len(self.sources)
        self.own_copies = []

        def begin():
            own = self.slot(self.a, self.r, self.core)
            for u, src in enumerate(self.sources):
                self.push(src, own, u, self.dev(self.inner, self.r, self.core))
                if self.middle is not None:
                    self.push(src, own, u, self.dev(self.outer, self.r, self.core), when=self.middle)
                self.push(src, own, u, self.dev(self.a, self.right, self.core))
                self.push(src, own, u, self.dev(self.a, self.left, self.core))
                if self.sibling is not None:
                    self.push(src, own, u, self.dev(self.a, self.r, self.sibling))
            for u, src in enumerate(self.sources):
                copy = pltpu.make_async_copy(src, self.dst.at[own, u], self.local.at[u])
                copy.start()
                self.own_copies.append(copy)

        found = [(0.0, begin)]
        step = 4.0 / units
        for k in range(len(self.order)):
            for u in range(units):
                at = (k * units + u) * step
                if k > 0:
                    found.append((at, lambda k=k, u=u: self.forward(k, u)))
                found.append((at + LAG * 4.0 + 0.3, lambda k=k, u=u: self.halves(k, u)))
                found.append((at + LAG * 8.0 + 0.6, lambda k=k, u=u: self.ends(k, u)))
        found.append((25.0 if self.sibling is not None else 14.0, self.complete))
        found.append((2000.0, self.close))
        return [(start + at, act) for at, act in found]

    def complete(self):
        if self.sibling is not None:
            for a in self.order:
                for ring in (self.r, self.left, self.right, self.far):
                    for u in range(len(self.sources)):
                        self.arrive(self.slot(a, ring, self.sibling), u)
        for copy in self.own_copies:
            copy.wait()

    def close(self):
        for make, when in self.pending:
            if when is None:
                make().wait_send()
            else:
                pl.when(when)(lambda make=make: make().wait_send())

    def column_events(self, done):
        units = len(self.sources)
        link = 2 * self.rows * 2 * HD / 92000
        hop = 2.0
        own = self.slot(self.a, self.r, self.core)
        twin = self.dev(self.a, self.r, self.sibling)
        self.own_copies = []

        def begin(u):
            src = self.sources[u]
            self.push(src, own, u, self.dev(self.inner, self.r, self.core))
            self.push(src, own, u, self.dev(self.outer, self.r, self.core), when=self.middle)
            self.push(src, own, u, twin)
            copy = pltpu.make_async_copy(src, self.dst.at[own, u], self.local.at[u])
            copy.start()
            self.own_copies.append(copy)

        def pass_on(k, u):
            slot = self.slot(self.order[k], self.r, self.core)
            self.arrive(slot, u)
            src = self.dst.at[slot, u]
            self.push(src, slot, u, self.dev(self.onward[k], self.r, self.core), when=self.middle)
            self.push(src, slot, u, twin)

        def whole(u):
            self.own_copies[u].wait()
            for k in range(4):
                self.arrive(self.slot(self.order[k], self.r, self.sibling), u)
            done(u)

        found = []
        for u in range(units):
            at = u * 3 * link
            found.append((max(at - 2 * hop, 0.0), lambda u=u: begin(u)))
            for k in range(1, 4):
                found.append((at + k * (link + hop), lambda k=k, u=u: pass_on(k, u)))
            found.append((at + 3 * (link + hop) + hop, lambda u=u: whole(u)))
        return found

    def close_column(self):
        for make, when in self.pending:
            if when is None:
                make().wait_send()
            else:
                pl.when(when)(lambda make=make: make().wait_send())


def perform(events):
    for _, act in sorted(events, key=lambda event: event[0]):
        act()


def gather_sems(over, units):
    slots, sends = {"xz": (32, 37), "ctx": (8, 9), "z": (8, 9)}[over]
    return [
        pltpu.SemaphoreType.DMA((units * sends,)),
        pltpu.SemaphoreType.DMA((units, slots, 2)),
        pltpu.SemaphoreType.DMA((units,)),
    ]


class Weights:
    def __init__(self, out_weight, patch_out, out_all, patch_all, out_send, out_recv, patch_send, patch_recv, local):
        self.ctx, self.tile, self.mp = coordinates()
        self.core, self.z = self.tile % 2, self.tile // 2
        self.out_weight, self.patch_out, self.out_all, self.patch_all = out_weight, patch_out, out_all, patch_all
        self.out_send, self.out_recv, self.patch_send, self.patch_recv = out_send, out_recv, patch_send, patch_recv
        self.local = local

    def mates(self):
        found = []
        for i in range(1, 8):
            core, mp = (self.core + i // 4) % 2, (self.mp + i) % 4
            found.append((core, mp, (self.ctx, self.z * 2 + core, mp)))
        return found

    def partners(self):
        return [device for _, _, device in self.mates()]

    def columns(self, core, mp):
        return self.patch_out.at[:, pl.ds(pl.multiple_of(mp * 1024 + core * 512, 512), 512)]

    def events(self, start=0.0):
        own = self.core * 4 + self.mp
        copies = []
        for i, (core, mp, device) in enumerate(self.mates()):
            if i < 3:
                copies.append(
                    remote(
                        self.out_weight.at[:, mp], self.out_all.at[self.mp], self.out_send.at[i],
                        self.out_recv.at[self.mp], device,
                    )
                )
            copies.append(
                remote(
                    self.columns(core, mp), self.patch_all.at[own], self.patch_send.at[i],
                    self.patch_recv.at[own], device,
                )
            )
        here = [
            pltpu.make_async_copy(self.out_weight.at[:, self.mp], self.out_all.at[self.mp], self.local.at[0]),
            pltpu.make_async_copy(self.columns(self.core, self.mp), self.patch_all.at[own], self.local.at[1]),
        ]

        def begin():
            for copy in copies + here:
                copy.start()

        def end():
            for i, (core, mp, device) in enumerate(self.mates()):
                slot = core * 4 + mp
                if i < 3:
                    dst = self.out_all.at[mp]
                    remote(dst, dst, self.out_send.at[0], self.out_recv.at[mp], device).wait_recv()
                dst = self.patch_all.at[slot]
                remote(dst, dst, self.patch_send.at[0], self.patch_recv.at[slot], device).wait_recv()
            for copy in copies:
                copy.wait_send()
            for copy in here:
                copy.wait()

        return [(start, begin), (1000.0, end)]


def weight_sems():
    return [pltpu.SemaphoreType.DMA((n,)) for n in (3, 4, 7, 8, 2)]


def merge(groups):
    return [device for group in groups for device in group]


def silu(v):
    half = 0.5 * v
    return half + half * jnp.tanh(half)


def opening_kernel(
    pairs, down, text, patch_ref, gain_ref, image_ref, text_all,
    pairs_all, down_all, rows, weights, total,
    pair_send, pair_recv, down_send, down_recv, own_sem, send, recv, local,
):
    ctx, tile, mp = coordinates()
    job = Gather("ctx", [text], text_all, send, recv, local)
    tiles = [((tile + i) % 8) for i in range(1, 8)]
    mps = [((mp + i) % 4) for i in range(1, 4)]
    barrier([(ctx, t, mp) for t in tiles] + [(ctx, tile, m) for m in mps] + job.partners())
    copies = []
    for i, t in enumerate(tiles):
        copies.append(remote(pairs, pairs_all.at[tile], pair_send.at[i], pair_recv.at[tile], (ctx, t, mp)))
    for i, m in enumerate(mps):
        copies.append(remote(down, down_all.at[mp], down_send.at[i], down_recv.at[mp], (ctx, tile, m)))
    own = [
        pltpu.make_async_copy(pairs, pairs_all.at[tile], own_sem.at[0]),
        pltpu.make_async_copy(down, down_all.at[mp], own_sem.at[1]),
    ]
    for copy in copies + own:
        copy.start()

    def prepare():
        rows[...] = jnp.zeros_like(rows)
        weights[...] = jnp.zeros_like(weights)

    def arrange():
        for copy in own:
            copy.wait()
        for m in mps:
            remote(down, down_all.at[m], down_send.at[0], down_recv.at[m], (ctx, tile, m)).wait_recv()
        taps = sum(down_all[m].astype(F32) for m in range(4))
        for kind in range(2):
            for a in range(3):
                at = (a + 1 - kind) // 2 * HD + (a + 1 - kind) % 2 * 48
                for pc in range(4):
                    weights[kind * 4 + pc, at + 8 * pc : at + 8 * pc + 24] = taps[24 * a : 24 * a + 24]
        for t in tiles:
            remote(pairs, pairs_all.at[t], pair_send.at[0], pair_recv.at[t], (ctx, t, mp)).wait_recv()
        for t in range(8):
            for s in range(2):
                for i in range(4):
                    at = 1 + 4 * t + i
                    rows[s, at // 2, at % 2] = pairs_all[t, s, i]

    def pixel_row(pr):
        first = (0, 1, 1, 2)[pr]
        lhs = jnp.concatenate(
            [rows[:, p // 2 : p // 2 + 16, p % 2].reshape(UNIT, HD) for p in (first, first + 1)], axis=1
        )
        acts = [
            silu(jnp.dot(lhs, weights[pr % 2 * 4 + pc].astype(BF), preferred_element_type=F32)).astype(BF)
            for pc in range(4)
        ]
        term = jnp.dot(
            jnp.concatenate(acts, axis=1), patch_ref[pr * 1024 : (pr + 1) * 1024], preferred_element_type=F32
        )
        if pr == 0:
            total[...] = term
        elif pr < 3:
            total[...] += term
        else:
            image_ref[:UNIT] = (total[...] + term).astype(BF)
            image_ref[UNIT:] = jnp.broadcast_to(gain_ref[...], (32, HD))

    perform(
        job.events()
        + [(0.1, prepare), (1.0, arrange)]
        + [(at, lambda pr=pr: pixel_row(pr)) for pr, at in enumerate((1.5, 4.4, 7.0, 9.0))]
    )
    for copy in copies:
        copy.wait_send()


def opening(pairs, down, text, patch_in, gain, parts=2):
    dma = pltpu.SemaphoreType.DMA
    vmem = pl.BlockSpec(memory_space=pltpu.VMEM)
    return pl.pallas_call(
        opening_kernel,
        out_shape=[
            jax.ShapeDtypeStruct((UNIT + 32, HD), BF),
            jax.ShapeDtypeStruct((8, parts, 1024 // parts, HD), BF),
        ],
        in_specs=[ANY, ANY, ANY, vmem, vmem],
        out_specs=[vmem, ANY],
        scratch_shapes=[
            pltpu.VMEM((8,) + pairs.shape, BF),
            pltpu.VMEM((4,) + down.shape, BF),
            pltpu.VMEM((2, 17, 2, 16, HD), BF),
            pltpu.VMEM((8, 2 * HD, CH), F32),
            pltpu.VMEM((UNIT, HD), F32),
        ]
        + [dma((7,)), dma((8,)), dma((3,)), dma((4,)), dma((2,))]
        + gather_sems("ctx", parts),
        compiler_params=pltpu.CompilerParams(
            collective_id=1, has_side_effects=True, vmem_limit_bytes=32 * 1024 * 1024
        ),
    )(pairs, down, text, patch_in, gain)


TILE = 256


def heads_kernel(
    image, text, wq_ref, wk_ref, wv_ref, qg_ref, kg_ref, out_weight, patch_out,
    image_q, text_q, image_kv, text_kv, out_all, patch_all,
    image_x, text_x, image_own, text_own, *sems
):
    image_job = Gather("xz", [image], image_x, *sems[0:3])
    text_job = Gather("xz", [text], text_x, *sems[3:6])
    image_keys = Gather("ctx", [image_own.at[0], image_own.at[1]], image_kv, *sems[6:9])
    text_keys = Gather("ctx", [text_own.at[0], text_own.at[1]], text_kv, *sems[9:12])
    moved = Weights(out_weight, patch_out, out_all, patch_all, *sems[12:])
    barrier(merge([image_job.partners(), image_keys.partners(), moved.partners()]))

    def heads(x_ref, q_ref, own, part):
        rows = slice(part * TILE, (part + 1) * TILE)
        squares = jnp.zeros((TILE, HD), F32)
        for i in range(32):
            piece = x_ref[i, 0, rows].astype(F32)
            squares += piece * piece
        scale = lax.rsqrt(jnp.sum(squares, axis=1, keepdims=True) * (1.0 / 4096.0) + EPSILON)
        normed = jnp.concatenate(
            [
                (x_ref[i, 0, rows].astype(F32) * scale * image_x[i, 0, UNIT : UNIT + 1].astype(F32)).astype(BF)
                for i in range(32)
            ],
            axis=1,
        )

        def head(weight, gain, factor):
            raw = jnp.dot(normed, weight, preferred_element_type=F32)
            mean = jnp.mean(raw * raw, axis=1, keepdims=True)
            return (raw * lax.rsqrt(mean + EPSILON) * gain * factor).astype(BF)

        own[0, rows] = head(wk_ref[...], kg_ref[...], 1.0)
        own[1, rows] = jnp.dot(normed, wv_ref[...], preferred_element_type=F32).astype(BF)
        q_ref[rows] = head(wq_ref[...], qg_ref[...], HD**-0.5)

    times = TIMES
    perform(
        image_job.events()
        + text_job.events(times[0])
        + [(times[1], lambda: heads(image_x, image_q, image_own, 0))]
        + [(times[1] + 1.0, lambda: heads(image_x, image_q, image_own, 1))]
        + image_keys.events(times[1] + 2.0)
        + [(times[2], lambda: heads(text_x, text_q, text_own, 0))]
        + [(times[2] + 1.0, lambda: heads(text_x, text_q, text_own, 1))]
        + text_keys.events(times[2] + 2.0)
        + moved.events(times[2] + 2.5)
    )


TIMES = (8.0, 26.0, 35.0)


def heads_of(image, text, wq, wk, wv, qg, kg, out_weight, patch_out):
    vmem = pl.BlockSpec(memory_space=pltpu.VMEM)
    rows = jax.ShapeDtypeStruct((UNIT, HD), BF)
    keys = jax.ShapeDtypeStruct((8, 2, UNIT, HD), BF)
    return pl.pallas_call(
        heads_kernel,
        out_shape=[
            rows,
            rows,
            keys,
            keys,
            jax.ShapeDtypeStruct((4, 8, HD, HD), BF),
            jax.ShapeDtypeStruct((8, HD, 512), BF),
        ],
        in_specs=[ANY, ANY] + [vmem] * 5 + [ANY, ANY],
        out_specs=[vmem, vmem] + [ANY] * 4,
        scratch_shapes=[
            pltpu.VMEM((32, 1) + image.shape, BF),
            pltpu.VMEM((32, 1) + text.shape, BF),
            pltpu.VMEM((2, UNIT, HD), BF),
            pltpu.VMEM((2, UNIT, HD), BF),
        ]
        + gather_sems("xz", 1)
        + gather_sems("xz", 1)
        + gather_sems("ctx", 2)
        + gather_sems("ctx", 2)
        + weight_sems(),
        compiler_params=pltpu.CompilerParams(
            collective_id=3, has_side_effects=True, vmem_limit_bytes=48 * 1024 * 1024
        ),
    )(image, text, wq, wk, wv, qg, kg, out_weight, patch_out)


MIX = 256


def mix_kernel(
    image, text, w_ref, image_stream, text_stream, image_out, text_out,
    blocks, outgoing, incoming, send, recv, local, part_send, part_recv,
):
    ctx, tile, mp = coordinates()
    units = blocks.shape[1]
    job = Gather("z", [image, text], blocks, send, recv, local)
    rings = [(mp + 1) % 4, (mp + 3) % 4, (mp + 2) % 4]
    barrier(merge([job.partners(), [(ctx, tile, rings[2])]]))

    def settle(u):
        for i, ring in enumerate(rings):
            dst = incoming.at[ring, u]
            remote(dst, dst, part_send.at[0, 0], part_recv.at[ring, u], (ctx, tile, ring)).wait_recv()
        stream, out, row = (image_stream, image_out, u * MIX) if u < 2 else (text_stream, text_out, u * MIX - UNIT)
        total = stream[row : row + MIX].astype(F32) + kept[u]
        for ring in rings:
            total = total + incoming[ring, u].astype(F32)
        out[row : row + MIX] = total.astype(BF)

    kept, copies = {}, []

    def multiply(u):
        x = jnp.concatenate([blocks[t, u] for t in range(8)], axis=1)
        for i, ring in enumerate(rings):
            outgoing[i, u] = jnp.dot(x, w_ref[ring], preferred_element_type=F32).astype(BF)
            copy = remote(
                outgoing.at[i, u], incoming.at[mp, u], part_send.at[i, u], part_recv.at[mp, u], (ctx, tile, ring)
            )
            copy.start()
            copies.append(copy)
        kept[u] = jnp.dot(x, w_ref[mp], preferred_element_type=F32)
        if u > 0:
            settle(u - 1)

    perform(job.column_events(multiply))
    settle(units - 1)
    job.close_column()
    for copy in copies:
        copy.wait_send()


def mix(image, text, w, image_stream, text_stream):
    dma = pltpu.SemaphoreType.DMA
    units = 2 * UNIT // MIX
    vmem = pl.BlockSpec(memory_space=pltpu.VMEM)
    return pl.pallas_call(
        mix_kernel,
        out_shape=[jax.ShapeDtypeStruct((UNIT, HD), BF)] * 2,
        in_specs=[ANY, ANY, vmem, vmem, vmem],
        out_specs=[vmem, vmem],
        scratch_shapes=[
            pltpu.VMEM((8, units, MIX, HD), BF),
            pltpu.VMEM((3, units, MIX, HD), BF),
            pltpu.VMEM((4, units, MIX, HD), BF),
        ]
        + gather_sems("z", units)
        + [dma((3, units)), dma((4, units))],
        compiler_params=pltpu.CompilerParams(
            collective_id=2, has_side_effects=True, vmem_limit_bytes=32 * 1024 * 1024
        ),
    )(image, text, w, image_stream, text_stream)


def up_kernel(
    image, text, w_ref, up_ref, work, cells_ref,
    blocks, product, terms, grid, above, below,
    work_send, work_recv, work_local,
    block_send, block_recv, twin_send, twin_recv, term_send, term_recv, grid_send, grid_recv, edge_send, edge_recv,
    own_sem,
):
    ctx, tile, mp = coordinates()
    z, core = tile // 2, tile % 2
    job = Gather("ctx", [image, text], work, work_send, work_recv, work_local)
    me = tile * 4 + mp
    group = []
    for i in range(1, 32):
        peer = (me + i) % 32
        group.append((ctx, peer // 4, peer % 4))
    barrier(merge([group, job.partners()]))
    rings = [(mp + 1) % 4, (mp + 3) % 4, (mp + 2) % 4]
    twin = (ctx, z * 2 + 1 - core, mp)
    own = core * 4 + mp
    copies = []

    def go(copy):
        copy.start()
        copies.append(copy)

    mine = [
        pltpu.make_async_copy(image, blocks.at[own], own_sem.at[0]),
        pltpu.make_async_copy(product.at[tile], terms.at[tile], own_sem.at[1]),
    ]
    tiles = [(tile + i) % 8 for i in (2, 6, 4, 1, 7, 3, 5)]
    down_edge = (mp == 3) & (tile < 7)
    up_edge = (mp == 0) & (tile > 0)
    down_copies = [
        lambda m=m: remote(
            grid.at[mp, :, pl.ds(16, 16)], above, edge_send.at[m], edge_recv.at[0], (ctx, (tile + 1) % 8, m)
        )
        for m in range(4)
    ]
    up_copies = [
        lambda m=m: remote(
            grid.at[mp, :, pl.ds(0, 16)], below, edge_send.at[m], edge_recv.at[1], (ctx, (tile + 7) % 8, m)
        )
        for m in range(4)
    ]

    def begin():
        for i, ring in enumerate(rings):
            go(remote(image, blocks.at[own], block_send.at[i], block_recv.at[mp], (ctx, tile, ring)))
        go(remote(image, blocks.at[own], twin_send.at[mp], twin_recv.at[mp], twin))
        mine[0].start()

    def pair(i):
        ring = rings[i]
        dst = blocks.at[core * 4 + ring]
        remote(dst, dst, block_send.at[0], block_recv.at[ring], (ctx, tile, ring)).wait_recv()
        go(remote(dst, dst, twin_send.at[ring], twin_recv.at[ring], twin))

    def multiply():
        mine[0].wait()
        for ring in range(4):
            dst = blocks.at[(1 - core) * 4 + ring]
            remote(dst, dst, twin_send.at[0], twin_recv.at[ring], twin).wait_recv()
        for s in range(2):
            x = jnp.concatenate([blocks[i, s * IMG_TOK : (s + 1) * IMG_TOK] for i in range(8)], axis=1)
            part = jnp.dot(x, w_ref[...].reshape(1024, 512), preferred_element_type=F32).astype(BF)
            product[:, s] = part.reshape(8, 32, 512)
        for i, t in enumerate(tiles):
            go(remote(product.at[t], terms.at[tile], term_send.at[i], term_recv.at[tile], (ctx, t, mp)))
        mine[1].start()

        @pl.when(tile == 0)
        def _():
            above[...] = jnp.zeros_like(above)

        @pl.when(tile == 7)
        def _():
            below[...] = jnp.zeros_like(below)

    def total():
        for t in tiles:
            dst = terms.at[t]
            remote(dst, dst, term_send.at[0], term_recv.at[t], (ctx, t, mp)).wait_recv()
        mine[1].wait()
        for c in range(2):
            total = terms[c].astype(F32)
            for k in range(1, 4):
                total = total + terms[2 * k + c].astype(F32)
            grid[mp, :, :, c * 512 : (c + 1) * 512] = silu(total).astype(BF)

        @pl.when(down_edge)
        def _():
            for make in down_copies:
                make().start()

        @pl.when(up_edge)
        def _():
            for make in up_copies:
                make().start()

        for i, ring in enumerate(rings):
            go(remote(grid.at[mp], grid.at[mp], grid_send.at[i], grid_recv.at[mp], (ctx, tile, ring)))

    def gathered():
        for ring in rings:
            dst = grid.at[ring]
            remote(dst, dst, grid_send.at[0], grid_recv.at[ring], (ctx, tile, ring)).wait_recv()

        @pl.when(tile > 0)
        def _():
            remote(above, above, edge_send.at[0], edge_recv.at[0], (ctx, tile, rings[0])).wait_recv()

        @pl.when(tile < 7)
        def _():
            remote(below, below, edge_send.at[0], edge_recv.at[1], (ctx, tile, rings[0])).wait_recv()

        convolve()

    def convolve():
        sums = [jnp.zeros((64, HD), F32) for _ in range(3)]
        for wr in range(6):
            for wc in range(6):
                pc = 3 if wc == 0 else 0 if wc == 5 else wc - 1
                lanes = slice(pc * CH, (pc + 1) * CH)
                if wr == 0:
                    a = jnp.concatenate([above[:, :, lanes], grid[3, :, 0:16, lanes]], axis=1)
                elif wr == 5:
                    a = jnp.concatenate([grid[0, :, 16:32, lanes], below[:, :, lanes]], axis=1)
                else:
                    a = grid[wr - 1, :, :, lanes]
                cell = wr * 6 + wc
                term = jnp.dot(
                    a.reshape(64, CH), up_ref[:, cell * HD : (cell + 1) * HD], preferred_element_type=F32
                )
                which = 0 if wc == 0 else 2 if wc == 5 else 1
                sums[which] = sums[which] + term
        column = lax.broadcasted_iota(jnp.int32, (64, HD), 0) % 16
        blank = jnp.zeros((1, HD), F32)
        from_left = jnp.concatenate([blank, sums[0][:63]], axis=0)
        from_right = jnp.concatenate([sums[2][1:], blank], axis=0)
        cells_ref[...] = (
            sums[1] + jnp.where(column == 0, 0.0, from_left) + jnp.where(column == 15, 0.0, from_right)
        )

    perform(
        job.events()
        + [(0.0, begin), (6.0, lambda: pair(0)), (6.0, lambda: pair(1)), (8.0, lambda: pair(2))]
        + [(10.0, multiply), (24.0, total), (32.0, gathered)]
    )
    for copy in copies:
        copy.wait_send()

    @pl.when(down_edge)
    def _():
        for make in down_copies:
            make().wait_send()

    @pl.when(up_edge)
    def _():
        for make in up_copies:
            make().wait_send()


def up_block(image, text, w, up_w):
    dma = pltpu.SemaphoreType.DMA
    vmem = pl.BlockSpec(memory_space=pltpu.VMEM)
    work = jax.ShapeDtypeStruct((8, 2, UNIT, HD), BF)
    return pl.pallas_call(
        up_kernel,
        out_shape=[work, jax.ShapeDtypeStruct((64, HD), F32)],
        in_specs=[ANY, ANY, vmem, vmem],
        out_specs=[ANY, vmem],
        scratch_shapes=[
            pltpu.VMEM((8, UNIT, HD), BF),
            pltpu.VMEM((8, 2, 32, 512), BF),
            pltpu.VMEM((8, 2, 32, 512), BF),
            pltpu.VMEM((4, 2, 32, 1024), BF),
            pltpu.VMEM((2, 16, 1024), BF),
            pltpu.VMEM((2, 16, 1024), BF),
        ]
        + gather_sems("ctx", 2)
        + [dma((n,)) for n in (3, 4, 4, 4, 7, 8, 3, 4, 4, 2, 2)],
        compiler_params=pltpu.CompilerParams(
            collective_id=6, has_side_effects=True, vmem_limit_bytes=32 * 1024 * 1024
        ),
    )(image, text, w, up_w)


def attention_kernel(top_ref, slot_ref, q_ref, lim_t_ref, lim_i_ref, text_ref, image_ref, out_ref):
    tile = pl.program_id(0)
    q = q_ref[...]
    cols = lax.broadcasted_iota(jnp.int32, (TILE, 1024), 1)

    def step(carry, k, v, limit):
        top, total, acc = carry
        s = lax.dot_general(q, k, (((1,), (1,)), ((), ())), preferred_element_type=F32)
        s = jnp.where(cols < limit, s, NEGATIVE)
        new = jnp.maximum(top, jnp.max(s, axis=1, keepdims=True))
        w = jnp.exp(s - new)
        factor = jnp.exp(top - new)
        total = total * factor + jnp.sum(w, axis=1, keepdims=True)
        acc = acc * factor + jnp.dot(w.astype(BF), v, preferred_element_type=F32)
        return new, total, acc

    def text_step(n, carry):
        k = jnp.concatenate([text_ref[2 * n, 0], text_ref[2 * n + 1, 0]], axis=0)
        v = jnp.concatenate([text_ref[2 * n, 1], text_ref[2 * n + 1, 1]], axis=0)
        return step(carry, k, v, lim_t_ref[...] - n * 1024)

    def image_step(n, carry):
        ks, vs = [], []
        for u in range(4):
            slot = slot_ref[n * 4 + u]
            rows = pl.ds(pl.multiple_of((slot % 2) * IMG_TOK, IMG_TOK), IMG_TOK)
            ks.append(image_ref[slot // 2, 0, rows])
            vs.append(image_ref[slot // 2, 1, rows])
        return step(carry, jnp.concatenate(ks, axis=0), jnp.concatenate(vs, axis=0), lim_i_ref[...] - n * 1024)

    carry = (jnp.full((TILE, 1), NEGATIVE, F32), jnp.zeros((TILE, 1), F32), jnp.zeros((TILE, HD), F32))
    carry = lax.fori_loop(0, (top_ref[1, tile] + 1023) // 1024, image_step, carry)
    carry = lax.fori_loop(0, (top_ref[0, tile] + 1023) // 1024, text_step, carry)
    _, total, acc = carry
    out_ref[...] = (acc / total).astype(BF)


def attention(slots, q, lim_t, lim_i, text, image):
    rows = q.shape[0]
    tops = jnp.stack([jnp.max(lim_t.reshape(-1, TILE), axis=1), jnp.max(lim_i.reshape(-1, TILE), axis=1)])
    whole = pl.BlockSpec((8, 2, UNIT, HD), lambda i, *_: (0, 0, 0, 0))
    grid_spec = pltpu.PrefetchScalarGridSpec(
        num_scalar_prefetch=2,
        grid=(rows // TILE,),
        in_specs=[
            pl.BlockSpec((TILE, HD), lambda i, *_: (i, 0)),
            pl.BlockSpec((TILE, 1), lambda i, *_: (i, 0)),
            pl.BlockSpec((TILE, 1), lambda i, *_: (i, 0)),
            whole,
            whole,
        ],
        out_specs=pl.BlockSpec((TILE, HD), lambda i, *_: (i, 0)),
    )
    return pl.pallas_call(
        attention_kernel,
        grid_spec=grid_spec,
        out_shape=jax.ShapeDtypeStruct((rows, HD), BF),
        compiler_params=pltpu.CompilerParams(vmem_limit_bytes=48 * 1024 * 1024),
    )(tops, slots, q, lim_t[:, None], lim_i[:, None], text, image)


def window_pairs(latents):
    wide = jnp.pad(latents, ((0, 0), (0, 0), (8, 32)))
    before = wide[..., 0:512].reshape(2, 8, 16, 32)[..., :8]
    middle = latents.reshape(2, 8, 16, 32)
    after = wide[..., 40:552].reshape(2, 8, 16, 32)[..., :8]
    joined = jnp.concatenate([before, middle, after], axis=-1)
    return jnp.concatenate([joined[:, 0::2], joined[:, 1::2], jnp.zeros((2, 4, 16, 32), BF)], axis=-1)


def up_weights(up_conv):
    taps = up_conv.reshape(9, CH, CIN).transpose(1, 0, 2).reshape(CH, 72)
    row = lax.broadcasted_iota(jnp.int32, (72, 36 * HD), 0)
    col = lax.broadcasted_iota(jnp.int32, (72, 36 * HD), 1)
    cell, inner = col // HD, col % HD
    a, b = cell // 6 - inner // 32, cell % 6 - (inner // 8) % 4
    inside = (a >= 0) & (a <= 2) & (b >= 0) & (b <= 2)
    pick = jnp.where(inside & (row == (a * 3 + b) * 8 + inner % 8), 1.0, 0.0).astype(BF)
    return jnp.dot(taps, pick, preferred_element_type=F32).astype(BF)


def shards(
    text_embed,
    latents,
    down_conv,
    patch_in,
    norm_gain,
    query_weight,
    key_weight,
    value_weight,
    query_gain,
    key_gain,
    out_weight,
    patch_out,
    up_conv,
    span_start,
    image_of_slot,
):
    ctx = lax.axis_index("ctx")
    images = jnp.arange(16, dtype=jnp.int32)
    before = span_start - images * IMG_TOK
    is_slot = image_of_slot[None, :] == images[:, None]
    slot_of = jnp.sum(jnp.where(is_slot, images[None, :], 0), axis=1)

    mp = lax.axis_index("mp")
    channels = jnp.arange(CH, dtype=jnp.int32)[None, :] // 64 == mp
    down = jnp.where(channels, jnp.tile(down_conv, (1, 4)), 0)
    image, text_all = opening(
        window_pairs(latents), jnp.pad(down, ((0, 8), (0, 0))), text_embed, patch_in, norm_gain[None, :]
    )

    text_rows = ctx * UNIT + jnp.arange(UNIT, dtype=jnp.int32)
    seen = jnp.sum((before[None, :] <= text_rows[:, None]).astype(jnp.int32), axis=1)
    text = jnp.take(text_all.reshape(8192, HD), text_rows + IMG_TOK * seen, axis=0, mode="clip")
    image_q, text_q, image_kv, text_kv, out_all, patch_all = heads_of(
        image, text, query_weight, key_weight, value_weight, query_gain.reshape(1, HD), key_gain.reshape(1, HD),
        out_weight.reshape(8, 4, HD, HD), patch_out,
    )

    slots = ctx * 2 + jnp.arange(2, dtype=jnp.int32)
    here = slots[:, None] == images[None, :]
    own_image = jnp.sum(jnp.where(here, image_of_slot[None, :], 0), axis=1)
    own_before = jnp.sum(jnp.where(own_image[:, None] == images[None, :], before[None, :], 0), axis=1)
    spread = lambda pair: jnp.broadcast_to(pair[:, None], (2, IMG_TOK)).reshape(UNIT)
    image_mix = attention(
        slot_of, image_q, spread(own_before), spread((own_image + 1) * IMG_TOK), text_kv, image_kv
    )
    text_mix = attention(slot_of, text_q, text_rows + 1, seen * IMG_TOK, text_kv, image_kv)

    image_out, text_out = mix(image_mix, text_mix, out_all.reshape(4, 1024, HD), image, text)
    work, cells = up_block(image_out, text_out, patch_all, up_weights(up_conv))
    noise_pred = cells.reshape(2, 2, 16, 4, 32).transpose(0, 1, 3, 2, 4).reshape(2, 8, 512)

    positions = ctx * 1024 + jnp.arange(1024, dtype=jnp.int32)
    started = (span_start[None, :] <= positions[:, None]).astype(jnp.int32)
    passed = jnp.sum((span_start[None, :] + IMG_TOK <= positions[:, None]).astype(jnp.int32), axis=1)
    inside = jnp.sum(started, axis=1) > passed
    now = passed[:, None] == images[None, :]
    slot = jnp.sum(jnp.where(now, slot_of[None, :], 0), axis=1)
    start = jnp.sum(jnp.where(now, span_start[None, :], 0), axis=1)
    row = positions - passed * IMG_TOK
    text_source = row // UNIT * 1024 + UNIT + row % UNIT
    image_source = slot // 2 * 1024 + slot % 2 * IMG_TOK + positions - start
    source = jnp.where(inside, image_source, text_source)
    layer_out = jnp.take(work.reshape(8192, HD), source, axis=0, mode="clip")
    return layer_out, noise_pred


def solution(mesh):
    return jax.shard_map(
        shards,
        mesh=mesh,
        in_specs=(
            P("ctx", ("tile", "mp")),
            P("ctx", "tile", None),
            P(None, "mp"),
            P(None, ("tile", "mp")),
            P(("tile", "mp")),
            P(None, ("tile", "mp")),
            P(None, ("tile", "mp")),
            P(None, ("tile", "mp")),
            P(),
            P(),
            P(None, ("tile", "mp")),
            P(("tile", "mp"), None),
            P(),
            P(),
            P(),
        ),
        out_specs=(P("ctx", ("tile", "mp")), P("ctx", "tile", None)),
        check_vma=False,
    )
```

```python
import functools

import jax
import jax.numpy as jnp
from jax import lax
from jax.experimental import pallas as pl
from jax.experimental.pallas import tpu as pltpu
from jax.sharding import PartitionSpec as P

HD = 128
CH = 256
CIN = 8
PATCH = 4
IMG_TOK = 256
UNIT = 512
EPSILON = 1e-05
NEGATIVE = -1e30
MESH = pl.DeviceIdType.MESH
ANY = pl.BlockSpec(memory_space=pl.ANY)
BF = jnp.bfloat16
F32 = jnp.float32


def remote(src, dst, send, recv, device):
    return pltpu.make_async_remote_copy(
        src_ref=src, dst_ref=dst, send_sem=send, recv_sem=recv, device_id=device, device_id_type=MESH
    )


def barrier(devices):
    sem = pltpu.get_barrier_semaphore()
    for device in devices:
        pl.semaphore_signal(sem, inc=1, device_id=device, device_id_type=MESH)
    pl.semaphore_wait(sem, len(devices))


def coordinates():
    return lax.axis_index("ctx"), lax.axis_index("tile"), lax.axis_index("mp")


PACE, MIX_PACE = (4.5, 9.0), 4.8


class Gather:
    def __init__(self, over, sources, dst, send, recv, local):
        ctx, tile, mp = coordinates()
        self.dst, self.send, self.recv, self.local = dst, send, recv, local
        self.rows = dst.shape[2]
        parts = dst.shape[1] // len(sources)
        self.sources = [
            source.at[pl.ds(part * self.rows, self.rows)] for source in sources for part in range(parts)
        ]
        self.counts, self.own_copies = {}, {}
        if over != "ctx":
            a = tile // 2
            self.a, self.r, self.core = a, mp, tile % 2
            self.dev = lambda a, r, core: (ctx, a * 2 + core, r)
            if over == "xz":
                self.slot = lambda a, r, core: (a * 2 + core) * 4 + r
            else:
                self.slot = lambda a, r, core: a * 2 + core
            self.sibling = 1 - self.core
            near = a + 1 - 2 * (a % 2)
            cross = 2 - a // 2
            self.order = [a, near, cross, 3 * (1 - a // 2)]
            self.onward = [None, 3 - a, near, near]
            self.middle = (a == 1) | (a == 2)
            self.inner, self.outer = 1 + a % 2, near
            self.others = [(a + d) % 4 for d in range(1, 4)]
        else:
            a = ctx // 4
            self.a, self.r, self.core = a, ctx % 4, 0
            self.dev = lambda a, r, core: (a * 4 + r, tile, mp)
            self.slot = lambda a, r, core: a * 4 + r
            self.sibling = None
            self.order = [a, 1 - a]
            self.middle = None
            self.inner = 1 - a
            self.others = [1 - a]
        self.right, self.left, self.far = (self.r + 1) % 4, (self.r + 3) % 4, (self.r + 2) % 4

    def partners(self):
        found = [self.dev(a, self.r, self.core) for a in self.others]
        found += [self.dev(self.a, self.right, self.core), self.dev(self.a, self.left, self.core)]
        if self.sibling is not None:
            found.append(self.dev(self.a, self.r, self.sibling))
        return found

    def push(self, src, slot, unit, device, half=None, when=None, twin=False):
        dst = self.dst.at[slot, unit]
        if half is not None:
            rows = pl.ds(half * (self.rows // 2), self.rows // 2)
            src, dst = src.at[rows], dst.at[rows]
        kind = 0 if when is None else 1
        count = self.counts.setdefault(unit, [0, 0])
        count[kind] += 2 if half is None else 1
        recv = self.recv.at[unit, 32] if twin else self.recv.at[unit, slot]
        copy = remote(src, dst, self.send.at[unit, kind], recv, device)
        if when is None:
            copy.start()
        else:
            pl.when(when)(copy.start)

    def take(self, unit, blocks, send, recv):
        ref = self.dst.at[pl.ds(0, blocks), unit]
        return remote(ref, ref, send, recv, self.dev(self.a, self.right, self.core))

    def arrive(self, slot, unit):
        dst = self.dst.at[slot, unit]
        device = self.dev(self.a, self.right, self.core)
        remote(dst, dst, self.send.at[unit, 0], self.recv.at[unit, slot], device).wait_recv()

    def arrive_twins(self, unit, blocks):
        self.take(unit, blocks, self.send.at[unit, 0], self.recv.at[unit, 32]).wait_recv()

    def close(self):
        for unit, (always, sometimes) in self.counts.items():
            self.take(unit, always // 2, self.send.at[unit, 0], self.recv.at[unit, 0]).wait_send()
            if sometimes:
                copy = self.take(unit, sometimes // 2, self.send.at[unit, 1], self.recv.at[unit, 0])
                pl.when(self.middle)(copy.wait_send)

    def forward(self, k, unit):
        slot = self.slot(self.order[k], self.r, self.core)
        self.arrive(slot, unit)
        src = self.dst.at[slot, unit]
        if self.middle is not None:
            self.push(src, slot, unit, self.dev(self.onward[k], self.r, self.core), when=self.middle)
        self.push(src, slot, unit, self.dev(self.a, self.right, self.core))
        self.push(src, slot, unit, self.dev(self.a, self.left, self.core))
        self.twin(slot, unit)

    def twin(self, slot, unit):
        if self.sibling is not None:
            src = self.dst.at[slot, unit]
            self.push(src, slot, unit, self.dev(self.a, self.r, self.sibling), twin=True)

    def halves(self, k, unit):
        for ring, target, half in ((self.left, self.right, 0), (self.right, self.left, 1)):
            slot = self.slot(self.order[k], ring, self.core)
            self.arrive(slot, unit)
            self.push(self.dst.at[slot, unit], slot, unit, self.dev(self.a, target, self.core), half)
            self.twin(slot, unit)

    def ends(self, k, unit):
        slot = self.slot(self.order[k], self.far, self.core)
        self.arrive(slot, unit)
        self.twin(slot, unit)

    def events(self, starts):
        pace = PACE[0 if self.sibling is not None else 1] * self.rows / UNIT
        found = []
        for u, start in enumerate(starts):
            found.append((start, lambda u=u: self.begin(u)))
            for k in range(len(self.order)):
                at = start + k * pace
                if k > 0:
                    found.append((at, lambda k=k, u=u: self.forward(k, u)))
                found.append((at + pace + 0.3, lambda k=k, u=u: self.halves(k, u)))
                found.append((at + 2 * pace + 0.6, lambda k=k, u=u: self.ends(k, u)))
            found.append((at + 3 * pace, lambda u=u: self.complete(u)))
        found.append((2000.0, self.close))
        return found

    def begin(self, u):
        own = self.slot(self.a, self.r, self.core)
        src = self.sources[u]
        self.push(src, own, u, self.dev(self.inner, self.r, self.core))
        if self.middle is not None:
            self.push(src, own, u, self.dev(self.outer, self.r, self.core), when=self.middle)
        self.push(src, own, u, self.dev(self.a, self.right, self.core))
        self.push(src, own, u, self.dev(self.a, self.left, self.core))
        if self.sibling is not None:
            self.push(src, own, u, self.dev(self.a, self.r, self.sibling), twin=True)
        copy = pltpu.make_async_copy(src, self.dst.at[own, u], self.local.at[u])
        copy.start()
        self.own_copies[u] = copy

    def complete(self, u):
        if self.sibling is not None:
            self.arrive_twins(u, 16)
        self.own_copies[u].wait()

    def column_events(self, done):
        units = len(self.sources)
        own = self.slot(self.a, self.r, self.core)
        twin = self.dev(self.a, self.r, self.sibling)

        def begin(u):
            src = self.sources[u]
            self.push(src, own, u, self.dev(self.inner, self.r, self.core))
            self.push(src, own, u, self.dev(self.outer, self.r, self.core), when=self.middle)
            self.push(src, own, u, twin, twin=True)
            copy = pltpu.make_async_copy(src, self.dst.at[own, u], self.local.at[u])
            copy.start()
            self.own_copies[u] = copy

        def pass_on(k, u):
            slot = self.slot(self.order[k], self.r, self.core)
            self.arrive(slot, u)
            src = self.dst.at[slot, u]
            self.push(src, slot, u, self.dev(self.onward[k], self.r, self.core), when=self.middle)
            self.push(src, slot, u, twin, twin=True)

        def whole(u):
            self.own_copies[u].wait()
            self.arrive_twins(u, 4)
            done(u)

        found = []
        for u in range(units):
            at = TILE_TIMES[u + 1]
            found.append((at - 0.1, lambda u=u: begin(u)))
            for k in range(1, 4):
                found.append((at + k * MIX_PACE, lambda k=k, u=u: pass_on(k, u)))
            found.append((at + 3 * MIX_PACE + 3.0, lambda u=u: whole(u)))
        return found


def perform(events):
    for _, act in sorted(events, key=lambda event: event[0]):
        act()


def gather_sems(units):
    return [
        pltpu.SemaphoreType.DMA((units, 2)),
        pltpu.SemaphoreType.DMA((units, 33)),
        pltpu.SemaphoreType.DMA((units,)),
    ]


class Weights:
    def __init__(self, out_weight, patch_out, out_all, patch_all, out_send, out_recv, patch_send, patch_recv, local):
        self.ctx, self.tile, self.mp = coordinates()
        self.core, self.z = self.tile % 2, self.tile // 2
        self.out_weight, self.patch_out, self.out_all, self.patch_all = out_weight, patch_out, out_all, patch_all
        self.out_send, self.out_recv, self.patch_send, self.patch_recv = out_send, out_recv, patch_send, patch_recv
        self.local = local

    def mates(self):
        found = []
        for i in range(1, 8):
            core, mp = (self.core + i // 4) % 2, (self.mp + i) % 4
            found.append((core, mp, (self.ctx, self.z * 2 + core, mp)))
        return found

    def partners(self):
        return [device for _, _, device in self.mates()]

    def columns(self, core, mp):
        return self.patch_out.at[:, pl.ds(pl.multiple_of(mp * 1024 + core * 512, 512), 512)]

    def events(self, start=0.0):
        own = self.core * 4 + self.mp
        copies = []
        for i, (core, mp, device) in enumerate(self.mates()):
            if i < 3:
                copies.append(
                    remote(
                        self.out_weight.at[:, mp], self.out_all.at[self.mp], self.out_send.at[i],
                        self.out_recv.at[self.mp], device,
                    )
                )
            copies.append(
                remote(
                    self.columns(core, mp), self.patch_all.at[own], self.patch_send.at[i],
                    self.patch_recv.at[own], device,
                )
            )
        here = [
            pltpu.make_async_copy(self.out_weight.at[:, self.mp], self.out_all.at[self.mp], self.local.at[0]),
            pltpu.make_async_copy(self.columns(self.core, self.mp), self.patch_all.at[own], self.local.at[1]),
        ]

        def begin():
            for copy in copies + here:
                copy.start()

        def end():
            for i, (core, mp, device) in enumerate(self.mates()):
                slot = core * 4 + mp
                if i < 3:
                    dst = self.out_all.at[mp]
                    remote(dst, dst, self.out_send.at[0], self.out_recv.at[mp], device).wait_recv()
                dst = self.patch_all.at[slot]
                remote(dst, dst, self.patch_send.at[0], self.patch_recv.at[slot], device).wait_recv()
            for copy in copies:
                copy.wait_send()
            for copy in here:
                copy.wait()

        return [(start, begin), (1000.0, end)]


def weight_sems():
    return [pltpu.SemaphoreType.DMA((n,)) for n in (3, 4, 7, 8, 2)]


def merge(groups):
    return [device for group in groups for device in group]


def silu(v):
    half = 0.5 * v
    return half + half * jnp.tanh(half)


OPENING_TIMES = ((0.0, 4.0), (5.2, 9.6, 13.0, 18.0))


def opening_kernel(
    pairs, down, text, patch_in, gain_ref, image_ref, text_all,
    pairs_all, down_all, rows, weights, total, patch_ref,
    pair_send, pair_recv, down_send, down_recv, own_sem, send, recv, local,
):
    ctx, tile, mp = coordinates()
    job = Gather("ctx", [text], text_all, send, recv, local)
    tiles = [((tile + i) % 8) for i in range(1, 8)]
    mps = [((mp + i) % 4) for i in range(1, 4)]
    barrier([(ctx, t, mp) for t in tiles] + [(ctx, tile, m) for m in mps] + job.partners())
    copies = []
    for i, t in enumerate(tiles):
        copies.append(remote(pairs, pairs_all.at[tile], pair_send.at[i], pair_recv.at[tile], (ctx, t, mp)))
    for i, m in enumerate(mps):
        copies.append(remote(down, down_all.at[mp], down_send.at[i], down_recv.at[mp], (ctx, tile, m)))
    own = [
        pltpu.make_async_copy(pairs, pairs_all.at[tile], own_sem.at[0]),
        pltpu.make_async_copy(down, down_all.at[mp], own_sem.at[1]),
        pltpu.make_async_copy(patch_in, patch_ref, own_sem.at[2]),
    ]
    for copy in copies + own:
        copy.start()

    def prepare():
        rows[...] = jnp.zeros_like(rows)
        weights[...] = jnp.zeros_like(weights)

    def arrange():
        for copy in own:
            copy.wait()
        for m in mps:
            remote(down, down_all.at[m], down_send.at[0], down_recv.at[m], (ctx, tile, m)).wait_recv()
        taps = sum(down_all[m].astype(F32) for m in range(4))
        for kind in range(2):
            for a in range(3):
                at = (a + 1 - kind) // 2 * HD + (a + 1 - kind) % 2 * 48
                for pc in range(4):
                    weights[kind * 4 + pc, at + 8 * pc : at + 8 * pc + 24] = taps[24 * a : 24 * a + 24]
        for t in tiles:
            remote(pairs, pairs_all.at[t], pair_send.at[0], pair_recv.at[t], (ctx, t, mp)).wait_recv()
        for t in range(8):
            for s in range(2):
                for i in range(4):
                    at = 1 + 4 * t + i
                    rows[s, at // 2, at % 2] = pairs_all[t, s, i]

    def pixel_row(pr):
        first = (0, 1, 1, 2)[pr]
        lhs = jnp.concatenate(
            [rows[:, p // 2 : p // 2 + 16, p % 2].reshape(UNIT, HD) for p in (first, first + 1)], axis=1
        )
        acts = [
            silu(jnp.dot(lhs, weights[pr % 2 * 4 + pc].astype(BF), preferred_element_type=F32)).astype(BF)
            for pc in range(4)
        ]
        term = jnp.dot(
            jnp.concatenate(acts, axis=1), patch_ref[pr * 1024 : (pr + 1) * 1024], preferred_element_type=F32
        )
        if pr == 0:
            total[...] = term
        elif pr < 3:
            total[...] += term
        else:
            image_ref[:32] = jnp.broadcast_to(gain_ref[...], (32, HD))
            image_ref[32:] = (total[...] + term).astype(BF)

    perform(
        job.events(OPENING_TIMES[0])
        + [(0.1, prepare), (5.0, arrange)]
        + [(at, lambda pr=pr: pixel_row(pr)) for pr, at in enumerate(OPENING_TIMES[1])]
    )
    for copy in copies:
        copy.wait_send()


def opening(pairs, down, text, patch_in, gain, parts=2):
    dma = pltpu.SemaphoreType.DMA
    vmem = pl.BlockSpec(memory_space=pltpu.VMEM)
    return pl.pallas_call(
        opening_kernel,
        out_shape=[
            jax.ShapeDtypeStruct((UNIT + 32, HD), BF),
            jax.ShapeDtypeStruct((8, parts, 1024 // parts, HD), BF),
        ],
        in_specs=[ANY, ANY, ANY, ANY, vmem],
        out_specs=[vmem, ANY],
        scratch_shapes=[
            pltpu.VMEM((8,) + pairs.shape, BF),
            pltpu.VMEM((4,) + down.shape, BF),
            pltpu.VMEM((2, 17, 2, 16, HD), BF),
            pltpu.VMEM((8, 2 * HD, CH), F32),
            pltpu.VMEM((UNIT, HD), F32),
            pltpu.VMEM((4096, HD), BF),
        ]
        + [dma((7,)), dma((8,)), dma((3,)), dma((4,)), dma((3,))]
        + gather_sems(parts),
        compiler_params=pltpu.CompilerParams(
            collective_id=1, has_side_effects=True, vmem_limit_bytes=32 * 1024 * 1024
        ),
    )(pairs, down, text, patch_in, gain)


TILE = 256


HEADS_TIMES = (8.0, 31.0, 39.0, 41.0)


def heads_kernel(
    image, text, wq, wk, wv, qg_ref, kg_ref, out_weight, patch_out,
    q_ref, image_kv, text_kv, out_all, patch_all,
    x_image, x_text, image_own, text_own, wq_ref, wk_ref, wv_ref, own_sem, *sems
):
    jobs = [
        Gather("xz", [image], x_image, *sems[0:3]),
        Gather("xz", [text], x_text, *sems[3:6]),
    ]
    keys = [
        Gather("ctx", [image_own.at[0], image_own.at[1]], image_kv, *sems[6:9]),
        Gather("ctx", [text_own.at[0], text_own.at[1]], text_kv, *sems[9:12]),
    ]
    moved = Weights(out_weight, patch_out, out_all, patch_all, *sems[12:])
    barrier(merge([jobs[0].partners(), keys[0].partners(), moved.partners()]))
    loads = [
        pltpu.make_async_copy(src, dst, own_sem.at[i])
        for i, (src, dst) in enumerate(((wq, wq_ref), (wk, wk_ref), (wv, wv_ref)))
    ]

    def load():
        for copy in loads:
            copy.start()

    def heads(x_ref, unit, start, own, half, at):
        if at == 0:
            for copy in loads:
                copy.wait()
        rows = slice(start, start + TILE)
        squares = jnp.zeros((TILE, HD), F32)
        for i in range(32):
            piece = x_ref[i, unit, rows].astype(F32)
            squares += piece * piece
        scale = lax.rsqrt(jnp.sum(squares, axis=1, keepdims=True) * (1.0 / 4096.0) + EPSILON)
        normed = jnp.concatenate(
            [
                (x_ref[i, unit, rows].astype(F32) * scale * x_image[i, 0, 0:1].astype(F32)).astype(BF)
                for i in range(32)
            ],
            axis=1,
        )

        def head(weight, gain, factor):
            raw = jnp.dot(normed, weight, preferred_element_type=F32)
            mean = jnp.mean(raw * raw, axis=1, keepdims=True)
            return (raw * lax.rsqrt(mean + EPSILON) * gain * factor).astype(BF)

        own[half, 0:TILE] = head(wk_ref[...], kg_ref[...], 1.0)
        own[half, TILE:] = jnp.dot(normed, wv_ref[...], preferred_element_type=F32).astype(BF)
        q_ref[at : at + TILE] = head(wq_ref[...], qg_ref[...], HD**-0.5)

    text_start, image_ready, text_ready, moving = HEADS_TIMES
    perform(
        jobs[0].events([0.0])
        + jobs[1].events([text_start])
        + [(0.1, load)]
        + [
            (image_ready, lambda: heads(x_image, 0, 32, image_own, 0, 0)),
            (image_ready + 0.1, lambda: heads(x_image, 0, 32 + TILE, image_own, 1, TILE)),
            (text_ready, lambda: heads(x_text, 0, 0, text_own, 0, 2 * TILE)),
            (text_ready + 0.1, lambda: heads(x_text, 0, TILE, text_own, 1, 3 * TILE)),
        ]
        + keys[0].events([image_ready + 0.2, image_ready + 0.3])
        + keys[1].events([text_ready + 0.2, text_ready + 0.3])
        + moved.events(moving)
    )


def heads_of(image, text, wq, wk, wv, qg, kg, out_weight, patch_out):
    vmem = pl.BlockSpec(memory_space=pltpu.VMEM)
    keys = jax.ShapeDtypeStruct((8, 2, UNIT, HD), BF)
    return pl.pallas_call(
        heads_kernel,
        out_shape=[
            jax.ShapeDtypeStruct((2 * UNIT, HD), BF),
            keys,
            keys,
            jax.ShapeDtypeStruct((4, 8, HD, HD), BF),
            jax.ShapeDtypeStruct((8, HD, 512), BF),
        ],
        in_specs=[ANY] * 5 + [vmem] * 2 + [ANY] * 2,
        out_specs=[vmem] * 3 + [ANY] * 2,
        scratch_shapes=[
            pltpu.VMEM((32, 1) + image.shape, BF),
            pltpu.VMEM((32, 1) + text.shape, BF),
            pltpu.VMEM((2, UNIT, HD), BF),
            pltpu.VMEM((2, UNIT, HD), BF),
        ]
        + [pltpu.VMEM((4096, HD), BF)] * 3
        + [pltpu.SemaphoreType.DMA((3,))]
        + gather_sems(1)
        + gather_sems(1)
        + gather_sems(2)
        + gather_sems(2)
        + weight_sems(),
        compiler_params=pltpu.CompilerParams(
            collective_id=3, has_side_effects=True, vmem_limit_bytes=60 * 1024 * 1024
        ),
    )(image, text, wq, wk, wv, qg, kg, out_weight, patch_out)


MIX = 256
STEP = 2048
TILE_TIMES = (0.0, 5.0, 10.0, 14.0, 19.0)


def mix_kernel(
    slots, q_ref, lim_t_ref, lim_i_ref, image_kv, text_kv, w, image_stream, text_stream, image_out, text_out,
    mixed, image_ref, text_ref, blocks, outgoing, incoming, w_ref, send, recv, local, part_send, part_recv, own_sem,
):
    ctx, tile, mp = coordinates()
    units = blocks.shape[1]
    job = Gather("z", [mixed], blocks, send, recv, local)
    loads = [
        pltpu.make_async_copy(src, dst, own_sem.at[i])
        for i, (src, dst) in enumerate(((image_kv, image_ref), (text_kv, text_ref), (w, w_ref)))
    ]
    for load in loads:
        load.start()
    rings = [(mp + 1) % 4, (mp + 3) % 4, (mp + 2) % 4]
    barrier(merge([job.partners(), [(ctx, tile, rings[2])]]))
    per = STEP // IMG_TOK

    def text_places(n):
        first = n * per
        return [(first + u, 0) if n == 0 else (15 - first - u, 1) for u in range(per)]

    def image_places(n):
        places = [slots[n * per + u] for u in range(per)]
        return [(slot // 2, slot % 2) for slot in places]

    def attend(u):
        rows = slice(u * TILE, (u + 1) * TILE)
        q = q_ref[rows]
        cols = lax.broadcasted_iota(jnp.int32, (TILE, STEP), 1)
        top = jnp.full((TILE, 1), NEGATIVE, F32)
        total, acc = jnp.zeros((TILE, 1), F32), jnp.zeros((TILE, HD), F32)
        steps = [(image_ref, image_places, lim_i_ref, n) for n in range(2)]
        steps += [(text_ref, text_places, lim_t_ref, n) for n in range(1 if u == 2 else 2)]
        for ref, places, lim, n in steps:
            if u == 0 and n == 0:
                loads[0 if ref is image_ref else 1].wait()
            found = places(n)
            k = jnp.concatenate([ref[at, which, :IMG_TOK] for at, which in found], axis=0)
            v = jnp.concatenate([ref[at, which, IMG_TOK:] for at, which in found], axis=0)
            s = lax.dot_general(q, k, (((1,), (1,)), ((), ())), preferred_element_type=F32)
            if not (u == 3 and ref is text_ref and n == 0):
                s = jnp.where(cols < lim[rows] - n * STEP, s, NEGATIVE)
            new = jnp.maximum(top, jnp.max(s, axis=1, keepdims=True))
            weights = jnp.exp(s - new)
            factor = jnp.exp(top - new)
            total = total * factor + jnp.sum(weights, axis=1, keepdims=True)
            acc = acc * factor + jnp.dot(weights.astype(BF), v, preferred_element_type=F32)
            top = new
        mixed[rows] = (acc / total).astype(BF)

    def settle(u):
        for i, ring in enumerate(rings):
            dst = incoming.at[ring, u]
            remote(dst, dst, part_send.at[0, 0], part_recv.at[ring, u], (ctx, tile, ring)).wait_recv()
        stream, out, row = (image_stream, image_out, u * MIX) if u < 2 else (text_stream, text_out, u * MIX - UNIT)
        first = row + 32 if u < 2 else row
        total = stream[first : first + MIX].astype(F32) + kept[u]
        for ring in rings:
            total = total + incoming[ring, u].astype(F32)
        out[row : row + MIX] = total.astype(BF)

    kept, copies = {}, []

    def multiply(u):
        if u == 0:
            loads[2].wait()
        x = jnp.concatenate([blocks[t, u] for t in range(8)], axis=1)
        for i, ring in enumerate(rings):
            outgoing[i, u] = jnp.dot(x, w_ref[ring], preferred_element_type=F32).astype(BF)
            copy = remote(
                outgoing.at[i, u], incoming.at[mp, u], part_send.at[i, u], part_recv.at[mp, u], (ctx, tile, ring)
            )
            copy.start()
            copies.append(copy)
        kept[u] = jnp.dot(x, w_ref[mp], preferred_element_type=F32)
        if u > 0:
            settle(u - 1)

    perform([(at, lambda u=u: attend(u)) for u, at in enumerate(TILE_TIMES[:4])] + job.column_events(multiply))
    settle(units - 1)
    job.close()
    for copy in copies:
        copy.wait_send()


def mix(slots, q, lim_t, lim_i, image_kv, text_kv, w, image_stream, text_stream):
    dma = pltpu.SemaphoreType.DMA
    units = 2 * UNIT // MIX
    vmem = pl.BlockSpec(memory_space=pltpu.VMEM)
    return pl.pallas_call(
        mix_kernel,
        out_shape=[jax.ShapeDtypeStruct((UNIT, HD), BF)] * 2,
        in_specs=[pl.BlockSpec(memory_space=pltpu.SMEM), vmem, vmem, vmem, ANY, ANY, ANY, vmem, vmem],
        out_specs=[vmem, vmem],
        scratch_shapes=[
            pltpu.VMEM((2 * UNIT, HD), BF),
            pltpu.VMEM((8, 2, UNIT, HD), BF),
            pltpu.VMEM((8, 2, UNIT, HD), BF),
            pltpu.VMEM((8, units, MIX, HD), BF),
            pltpu.VMEM((3, units, MIX, HD), BF),
            pltpu.VMEM((4, units, MIX, HD), BF),
            pltpu.VMEM((4, 1024, HD), BF),
        ]
        + gather_sems(units)
        + [dma((3, units)), dma((4, units)), dma((3,))],
        compiler_params=pltpu.CompilerParams(
            collective_id=2, has_side_effects=True, vmem_limit_bytes=48 * 1024 * 1024
        ),
    )(slots, q, lim_t[:, None], lim_i[:, None], image_kv, text_kv, w, image_stream, text_stream)


UP_TIMES = (8.1, 24.0, 32.0, (0.0, 4.0))


def up_kernel(
    image, text, w, up_ref, work, cells_ref,
    blocks, product, terms, grid, above, below, w_ref,
    work_send, work_recv, work_local,
    block_send, block_recv, twin_send, twin_recv, term_send, term_recv, grid_send, grid_recv, edge_send, edge_recv,
    own_sem,
):
    ctx, tile, mp = coordinates()
    z, core = tile // 2, tile % 2
    job = Gather("ctx", [image, text], work, work_send, work_recv, work_local)
    me = tile * 4 + mp
    group = []
    for i in range(1, 32):
        peer = (me + i) % 32
        group.append((ctx, peer // 4, peer % 4))
    barrier(merge([group, job.partners()]))
    rings = [(mp + 1) % 4, (mp + 3) % 4, (mp + 2) % 4]
    twin = (ctx, z * 2 + 1 - core, mp)
    own = core * 4 + mp
    copies = []

    def go(copy):
        copy.start()
        copies.append(copy)

    mine = [
        pltpu.make_async_copy(image, blocks.at[own], own_sem.at[0]),
        pltpu.make_async_copy(product.at[tile], terms.at[tile], own_sem.at[1]),
        pltpu.make_async_copy(w, w_ref, own_sem.at[2]),
    ]
    tiles = [(tile + i) % 8 for i in (2, 6, 4, 1, 7, 3, 5)]
    down_edge = (mp == 3) & (tile < 7)
    up_edge = (mp == 0) & (tile > 0)
    down_copies = [
        lambda m=m: remote(
            grid.at[mp, :, pl.ds(16, 16)], above, edge_send.at[m], edge_recv.at[0], (ctx, (tile + 1) % 8, m)
        )
        for m in range(4)
    ]
    up_copies = [
        lambda m=m: remote(
            grid.at[mp, :, pl.ds(0, 16)], below, edge_send.at[m], edge_recv.at[1], (ctx, (tile + 7) % 8, m)
        )
        for m in range(4)
    ]

    def begin():
        for i, ring in enumerate(rings):
            go(remote(image, blocks.at[own], block_send.at[i], block_recv.at[mp], (ctx, tile, ring)))
        go(remote(image, blocks.at[own], twin_send.at[mp], twin_recv.at[mp], twin))
        mine[0].start()
        mine[2].start()

    def pair(i):
        ring = rings[i]
        dst = blocks.at[core * 4 + ring]
        remote(dst, dst, block_send.at[0], block_recv.at[ring], (ctx, tile, ring)).wait_recv()
        go(remote(dst, dst, twin_send.at[ring], twin_recv.at[ring], twin))

    def multiply():
        mine[0].wait()
        mine[2].wait()
        for ring in range(4):
            dst = blocks.at[(1 - core) * 4 + ring]
            remote(dst, dst, twin_send.at[0], twin_recv.at[ring], twin).wait_recv()
        for s in range(2):
            x = jnp.concatenate([blocks[i, s * IMG_TOK : (s + 1) * IMG_TOK] for i in range(8)], axis=1)
            part = jnp.dot(x, w_ref[...].reshape(1024, 512), preferred_element_type=F32).astype(BF)
            product[:, s] = part.reshape(8, 32, 512)
        for i, t in enumerate(tiles):
            go(remote(product.at[t], terms.at[tile], term_send.at[i], term_recv.at[tile], (ctx, t, mp)))
        mine[1].start()

        @pl.when(tile == 0)
        def _():
            above[...] = jnp.zeros_like(above)

        @pl.when(tile == 7)
        def _():
            below[...] = jnp.zeros_like(below)

    def total():
        for t in tiles:
            dst = terms.at[t]
            remote(dst, dst, term_send.at[0], term_recv.at[t], (ctx, t, mp)).wait_recv()
        mine[1].wait()
        for c in range(2):
            total = terms[c].astype(F32)
            for k in range(1, 4):
                total = total + terms[2 * k + c].astype(F32)
            grid[mp, :, :, c * 512 : (c + 1) * 512] = silu(total).astype(BF)

        @pl.when(down_edge)
        def _():
            for make in down_copies:
                make().start()

        @pl.when(up_edge)
        def _():
            for make in up_copies:
                make().start()

        for i, ring in enumerate(rings):
            go(remote(grid.at[mp], grid.at[mp], grid_send.at[i], grid_recv.at[mp], (ctx, tile, ring)))

    def gathered():
        for ring in rings:
            dst = grid.at[ring]
            remote(dst, dst, grid_send.at[0], grid_recv.at[ring], (ctx, tile, ring)).wait_recv()

        @pl.when(tile > 0)
        def _():
            remote(above, above, edge_send.at[0], edge_recv.at[0], (ctx, tile, rings[0])).wait_recv()

        @pl.when(tile < 7)
        def _():
            remote(below, below, edge_send.at[0], edge_recv.at[1], (ctx, tile, rings[0])).wait_recv()

        convolve()

    def convolve():
        sums = [jnp.zeros((64, HD), F32) for _ in range(3)]
        for wr in range(6):
            for wc in range(6):
                pc = 3 if wc == 0 else 0 if wc == 5 else wc - 1
                lanes = slice(pc * CH, (pc + 1) * CH)
                if wr == 0:
                    a = jnp.concatenate([above[:, :, lanes], grid[3, :, 0:16, lanes]], axis=1)
                elif wr == 5:
                    a = jnp.concatenate([grid[0, :, 16:32, lanes], below[:, :, lanes]], axis=1)
                else:
                    a = grid[wr - 1, :, :, lanes]
                cell = wr * 6 + wc
                term = jnp.dot(
                    a.reshape(64, CH), up_ref[:, cell * HD : (cell + 1) * HD], preferred_element_type=F32
                )
                which = 0 if wc == 0 else 2 if wc == 5 else 1
                sums[which] = sums[which] + term
        column = lax.broadcasted_iota(jnp.int32, (64, HD), 0) % 16
        blank = jnp.zeros((1, HD), F32)
        from_left = jnp.concatenate([blank, sums[0][:63]], axis=0)
        from_right = jnp.concatenate([sums[2][1:], blank], axis=0)
        cells_ref[...] = (
            sums[1] + jnp.where(column == 0, 0.0, from_left) + jnp.where(column == 15, 0.0, from_right)
        )

    perform(
        [(0.0, begin)]
        + job.events(UP_TIMES[3])
        + [(5.4, lambda: pair(0)), (5.4, lambda: pair(1)), (7.0, lambda: pair(2))]
        + [(UP_TIMES[0], multiply), (UP_TIMES[1], total), (UP_TIMES[2], gathered)]
    )
    for copy in copies:
        copy.wait_send()

    @pl.when(down_edge)
    def _():
        for make in down_copies:
            make().wait_send()

    @pl.when(up_edge)
    def _():
        for make in up_copies:
            make().wait_send()


def up_block(image, text, w, up_w):
    dma = pltpu.SemaphoreType.DMA
    vmem = pl.BlockSpec(memory_space=pltpu.VMEM)
    work = jax.ShapeDtypeStruct((8, 2, UNIT, HD), BF)
    return pl.pallas_call(
        up_kernel,
        out_shape=[work, jax.ShapeDtypeStruct((64, HD), F32)],
        in_specs=[ANY, ANY, ANY, vmem],
        out_specs=[ANY, vmem],
        scratch_shapes=[
            pltpu.VMEM((8, UNIT, HD), BF),
            pltpu.VMEM((8, 2, 32, 512), BF),
            pltpu.VMEM((8, 2, 32, 512), BF),
            pltpu.VMEM((4, 2, 32, 1024), BF),
            pltpu.VMEM((2, 16, 1024), BF),
            pltpu.VMEM((2, 16, 1024), BF),
            pltpu.VMEM((8, HD, 512), BF),
        ]
        + gather_sems(2)
        + [dma((n,)) for n in (3, 4, 4, 4, 7, 8, 3, 4, 4, 2, 3)],
        compiler_params=pltpu.CompilerParams(
            collective_id=6, has_side_effects=True, vmem_limit_bytes=32 * 1024 * 1024
        ),
    )(image, text, w, up_w)


def window_pairs(latents):
    wide = jnp.pad(latents, ((0, 0), (0, 0), (8, 32)))
    before = wide[..., 0:512].reshape(2, 8, 16, 32)[..., :8]
    middle = latents.reshape(2, 8, 16, 32)
    after = wide[..., 40:552].reshape(2, 8, 16, 32)[..., :8]
    joined = jnp.concatenate([before, middle, after], axis=-1)
    return jnp.concatenate([joined[:, 0::2], joined[:, 1::2], jnp.zeros((2, 4, 16, 32), BF)], axis=-1)


def up_weights(up_conv):
    taps = up_conv.reshape(9, CH, CIN).transpose(1, 0, 2).reshape(CH, 72)
    row = lax.broadcasted_iota(jnp.int32, (72, 36 * HD), 0)
    col = lax.broadcasted_iota(jnp.int32, (72, 36 * HD), 1)
    cell, inner = col // HD, col % HD
    a, b = cell // 6 - inner // 32, cell % 6 - (inner // 8) % 4
    inside = (a >= 0) & (a <= 2) & (b >= 0) & (b <= 2)
    pick = jnp.where(inside & (row == (a * 3 + b) * 8 + inner % 8), 1.0, 0.0).astype(BF)
    return jnp.dot(taps, pick, preferred_element_type=F32).astype(BF)


def shards(
    text_embed,
    latents,
    down_conv,
    patch_in,
    norm_gain,
    query_weight,
    key_weight,
    value_weight,
    query_gain,
    key_gain,
    out_weight,
    patch_out,
    up_conv,
    span_start,
    image_of_slot,
):
    ctx = lax.axis_index("ctx")
    images = jnp.arange(16, dtype=jnp.int32)
    before = span_start - images * IMG_TOK
    is_slot = image_of_slot[None, :] == images[:, None]
    slot_of = jnp.sum(jnp.where(is_slot, images[None, :], 0), axis=1)

    mp = lax.axis_index("mp")
    channels = jnp.arange(CH, dtype=jnp.int32)[None, :] // 64 == mp
    down = jnp.where(channels, jnp.tile(down_conv, (1, 4)), 0)
    image, text_all = opening(
        window_pairs(latents), jnp.pad(down, ((0, 8), (0, 0))), text_embed, patch_in, norm_gain[None, :]
    )

    inner = jnp.arange(IMG_TOK, dtype=jnp.int32)
    text_rows = jnp.concatenate([ctx * IMG_TOK + inner, (15 - ctx) * IMG_TOK + inner])
    seen = jnp.sum((before[None, :] <= text_rows[:, None]).astype(jnp.int32), axis=1)
    text = jnp.take(text_all.reshape(8192, HD), text_rows + IMG_TOK * seen, axis=0, mode="clip")
    q, image_kv, text_kv, out_all, patch_all = heads_of(
        image, text, query_weight, key_weight, value_weight, query_gain.reshape(1, HD), key_gain.reshape(1, HD),
        out_weight.reshape(8, 4, HD, HD), patch_out,
    )

    slots = ctx * 2 + jnp.arange(2, dtype=jnp.int32)
    here = slots[:, None] == images[None, :]
    own_image = jnp.sum(jnp.where(here, image_of_slot[None, :], 0), axis=1)
    own_before = jnp.sum(jnp.where(own_image[:, None] == images[None, :], before[None, :], 0), axis=1)
    spread = lambda pair: jnp.broadcast_to(pair[:, None], (2, IMG_TOK)).reshape(UNIT)
    lim_t = jnp.concatenate([spread(own_before), text_rows + 1])
    lim_i = jnp.concatenate([spread((own_image + 1) * IMG_TOK), seen * IMG_TOK])
    image_out, text_out = mix(
        slot_of, q, lim_t, lim_i, image_kv, text_kv, out_all.reshape(4, 1024, HD), image, text
    )
    work, cells = up_block(image_out, text_out, patch_all, up_weights(up_conv))
    noise_pred = cells.reshape(2, 2, 16, 4, 32).transpose(0, 1, 3, 2, 4).reshape(2, 8, 512)

    positions = ctx * 1024 + jnp.arange(1024, dtype=jnp.int32)
    started = (span_start[None, :] <= positions[:, None]).astype(jnp.int32)
    passed = jnp.sum((span_start[None, :] + IMG_TOK <= positions[:, None]).astype(jnp.int32), axis=1)
    inside = jnp.sum(started, axis=1) > passed
    now = passed[:, None] == images[None, :]
    slot = jnp.sum(jnp.where(now, slot_of[None, :], 0), axis=1)
    start = jnp.sum(jnp.where(now, span_start[None, :], 0), axis=1)
    row = positions - passed * IMG_TOK
    block = row // IMG_TOK
    text_source = jnp.minimum(block, 15 - block) * 1024 + UNIT + block // 8 * IMG_TOK + row % IMG_TOK
    image_source = slot // 2 * 1024 + slot % 2 * IMG_TOK + positions - start
    source = jnp.where(inside, image_source, text_source)
    layer_out = jnp.take(work.reshape(8192, HD), source, axis=0, mode="clip")
    return layer_out, noise_pred


def solution(mesh):
    return jax.shard_map(
        shards,
        mesh=mesh,
        in_specs=(
            P("ctx", ("tile", "mp")),
            P("ctx", "tile", None),
            P(None, "mp"),
            P(None, ("tile", "mp")),
            P(("tile", "mp")),
            P(None, ("tile", "mp")),
            P(None, ("tile", "mp")),
            P(None, ("tile", "mp")),
            P(),
            P(),
            P(None, ("tile", "mp")),
            P(("tile", "mp"), None),
            P(),
            P(),
            P(),
        ),
        out_specs=(P("ctx", ("tile", "mp")), P("ctx", "tile", None)),
        check_vma=False,
    )
```

```python
import functools

import jax
import jax.numpy as jnp
from jax import lax
from jax.experimental import pallas as pl
from jax.experimental.pallas import tpu as pltpu
from jax.sharding import PartitionSpec as P

HD = 128
CH = 256
CIN = 8
PATCH = 4
IMG_TOK = 256
UNIT = 512
EPSILON = 1e-05
NEGATIVE = -1e30
MESH = pl.DeviceIdType.MESH
ANY = pl.BlockSpec(memory_space=pl.ANY)
BF = jnp.bfloat16
F32 = jnp.float32


def remote(src, dst, send, recv, device):
    return pltpu.make_async_remote_copy(
        src_ref=src, dst_ref=dst, send_sem=send, recv_sem=recv, device_id=device, device_id_type=MESH
    )


def barrier(devices):
    sem = pltpu.get_barrier_semaphore()
    for device in devices:
        pl.semaphore_signal(sem, inc=1, device_id=device, device_id_type=MESH)
    pl.semaphore_wait(sem, len(devices))


def coordinates():
    return lax.axis_index("ctx"), lax.axis_index("tile"), lax.axis_index("mp")


PACE, MIX_PACE = (4.5, 9.0), 4.8


class Gather:
    def __init__(self, over, sources, dst, send, recv, local):
        ctx, tile, mp = coordinates()
        self.dst, self.send, self.recv, self.local = dst, send, recv, local
        self.rows = dst.shape[2]
        parts = dst.shape[1] // len(sources)
        self.sources = [
            source.at[pl.ds(part * self.rows, self.rows)] for source in sources for part in range(parts)
        ]
        self.counts, self.own_copies = {}, {}
        if over != "ctx":
            a = tile // 2
            self.a, self.r, self.core = a, mp, tile % 2
            self.dev = lambda a, r, core: (ctx, a * 2 + core, r)
            if over == "xz":
                self.slot = lambda a, r, core: (a * 2 + core) * 4 + r
            else:
                self.slot = lambda a, r, core: a * 2 + core
            self.sibling = 1 - self.core
            near = a + 1 - 2 * (a % 2)
            cross = 2 - a // 2
            self.order = [a, near, cross, 3 * (1 - a // 2)]
            self.onward = [None, 3 - a, near, near]
            self.middle = (a == 1) | (a == 2)
            self.inner, self.outer = 1 + a % 2, near
            self.others = [(a + d) % 4 for d in range(1, 4)]
        else:
            a = ctx // 4
            self.a, self.r, self.core = a, ctx % 4, 0
            self.dev = lambda a, r, core: (a * 4 + r, tile, mp)
            self.slot = lambda a, r, core: a * 4 + r
            self.sibling = None
            self.order = [a, 1 - a]
            self.middle = None
            self.inner = 1 - a
            self.others = [1 - a]
        self.right, self.left, self.far = (self.r + 1) % 4, (self.r + 3) % 4, (self.r + 2) % 4

    def partners(self):
        found = [self.dev(a, self.r, self.core) for a in self.others]
        found += [self.dev(self.a, self.right, self.core), self.dev(self.a, self.left, self.core)]
        if self.sibling is not None:
            found.append(self.dev(self.a, self.r, self.sibling))
        return found

    def push(self, src, slot, unit, device, half=None, when=None, twin=False):
        dst = self.dst.at[slot, unit]
        if half is not None:
            rows = pl.ds(half * (self.rows // 2), self.rows // 2)
            src, dst = src.at[rows], dst.at[rows]
        kind = 0 if when is None else 1
        count = self.counts.setdefault(unit, [0, 0])
        count[kind] += 2 if half is None else 1
        recv = self.recv.at[unit, 32] if twin else self.recv.at[unit, slot]
        copy = remote(src, dst, self.send.at[unit, kind], recv, device)
        if when is None:
            copy.start()
        else:
            pl.when(when)(copy.start)

    def take(self, unit, blocks, send, recv):
        ref = self.dst.at[pl.ds(0, blocks), unit]
        return remote(ref, ref, send, recv, self.dev(self.a, self.right, self.core))

    def arrive(self, slot, unit):
        dst = self.dst.at[slot, unit]
        device = self.dev(self.a, self.right, self.core)
        remote(dst, dst, self.send.at[unit, 0], self.recv.at[unit, slot], device).wait_recv()

    def arrive_twins(self, unit, blocks):
        self.take(unit, blocks, self.send.at[unit, 0], self.recv.at[unit, 32]).wait_recv()

    def close(self):
        for unit, (always, sometimes) in self.counts.items():
            self.take(unit, always // 2, self.send.at[unit, 0], self.recv.at[unit, 0]).wait_send()
            if sometimes:
                copy = self.take(unit, sometimes // 2, self.send.at[unit, 1], self.recv.at[unit, 0])
                pl.when(self.middle)(copy.wait_send)

    def forward(self, k, unit):
        slot = self.slot(self.order[k], self.r, self.core)
        self.arrive(slot, unit)
        src = self.dst.at[slot, unit]
        if self.middle is not None:
            self.push(src, slot, unit, self.dev(self.onward[k], self.r, self.core), when=self.middle)
        self.push(src, slot, unit, self.dev(self.a, self.right, self.core))
        self.push(src, slot, unit, self.dev(self.a, self.left, self.core))
        self.twin(slot, unit)

    def twin(self, slot, unit):
        if self.sibling is not None:
            src = self.dst.at[slot, unit]
            self.push(src, slot, unit, self.dev(self.a, self.r, self.sibling), twin=True)

    def halves(self, k, unit):
        for ring, target, half in ((self.left, self.right, 0), (self.right, self.left, 1)):
            slot = self.slot(self.order[k], ring, self.core)
            self.arrive(slot, unit)
            self.push(self.dst.at[slot, unit], slot, unit, self.dev(self.a, target, self.core), half)
            self.twin(slot, unit)

    def ends(self, k, unit):
        slot = self.slot(self.order[k], self.far, self.core)
        self.arrive(slot, unit)
        self.twin(slot, unit)

    def events(self, starts, lag=0.0):
        pace = PACE[0 if self.sibling is not None else 1] * self.rows / UNIT
        found = []
        for u, start in enumerate(starts):
            found.append((start, lambda u=u: self.begin(u)))
            for k in range(len(self.order)):
                at = start + lag + k * pace
                if k > 0:
                    found.append((at, lambda k=k, u=u: self.forward(k, u)))
                found.append((at + pace + 0.3, lambda k=k, u=u: self.halves(k, u)))
                found.append((at + 2 * pace + 0.6, lambda k=k, u=u: self.ends(k, u)))
            found.append((at + 2 * pace + 1.0, lambda u=u: self.complete(u)))
        found.append((2000.0, self.close))
        return found

    def begin(self, u):
        own = self.slot(self.a, self.r, self.core)
        src = self.sources[u]
        self.push(src, own, u, self.dev(self.inner, self.r, self.core))
        if self.middle is not None:
            self.push(src, own, u, self.dev(self.outer, self.r, self.core), when=self.middle)
        self.push(src, own, u, self.dev(self.a, self.right, self.core))
        self.push(src, own, u, self.dev(self.a, self.left, self.core))
        if self.sibling is not None:
            self.push(src, own, u, self.dev(self.a, self.r, self.sibling), twin=True)
        copy = pltpu.make_async_copy(src, self.dst.at[own, u], self.local.at[u])
        copy.start()
        self.own_copies[u] = copy

    def complete(self, u):
        if self.sibling is not None:
            self.arrive_twins(u, 16)
        self.own_copies[u].wait()

    def column_events(self, done):
        units = len(self.sources)
        own = self.slot(self.a, self.r, self.core)
        twin = self.dev(self.a, self.r, self.sibling)

        def begin(u):
            src = self.sources[u]
            self.push(src, own, u, self.dev(self.inner, self.r, self.core))
            self.push(src, own, u, self.dev(self.outer, self.r, self.core), when=self.middle)
            self.push(src, own, u, twin, twin=True)
            copy = pltpu.make_async_copy(src, self.dst.at[own, u], self.local.at[u])
            copy.start()
            self.own_copies[u] = copy

        def pass_on(k, u):
            slot = self.slot(self.order[k], self.r, self.core)
            self.arrive(slot, u)
            src = self.dst.at[slot, u]
            self.push(src, slot, u, self.dev(self.onward[k], self.r, self.core), when=self.middle)
            self.push(src, slot, u, twin, twin=True)

        def whole(u):
            self.own_copies[u].wait()
            self.arrive_twins(u, 4)
            done(u)

        found = []
        for u in range(units):
            at = TILE_TIMES[u + 1]
            found.append((at - 0.1, lambda u=u: begin(u)))
            for k in range(1, 4):
                found.append((at + k * MIX_PACE, lambda k=k, u=u: pass_on(k, u)))
            found.append((at + 3 * MIX_PACE + 3.0, lambda u=u: whole(u)))
        return found


def perform(events):
    for _, act in sorted(events, key=lambda event: event[0]):
        act()


def gather_sems(units):
    return [
        pltpu.SemaphoreType.DMA((units, 2)),
        pltpu.SemaphoreType.DMA((units, 33)),
        pltpu.SemaphoreType.DMA((units,)),
    ]


class Weights:
    def __init__(self, out_weight, patch_out, out_all, patch_all, out_send, out_recv, patch_send, patch_recv, local):
        self.ctx, self.tile, self.mp = coordinates()
        self.core, self.z = self.tile % 2, self.tile // 2
        self.out_weight, self.patch_out, self.out_all, self.patch_all = out_weight, patch_out, out_all, patch_all
        self.out_send, self.out_recv, self.patch_send, self.patch_recv = out_send, out_recv, patch_send, patch_recv
        self.local = local

    def mates(self):
        found = []
        for i in range(1, 8):
            core, mp = (self.core + i // 4) % 2, (self.mp + i) % 4
            found.append((core, mp, (self.ctx, self.z * 2 + core, mp)))
        return found

    def partners(self):
        return [device for _, _, device in self.mates()]

    def columns(self, core, mp):
        return self.patch_out.at[:, pl.ds(pl.multiple_of(mp * 1024 + core * 512, 512), 512)]

    def events(self, start=0.0):
        own = self.core * 4 + self.mp
        copies = []
        for i, (core, mp, device) in enumerate(self.mates()):
            if i < 3:
                copies.append(
                    remote(
                        self.out_weight.at[:, mp], self.out_all.at[self.mp], self.out_send.at[i],
                        self.out_recv.at[self.mp], device,
                    )
                )
            copies.append(
                remote(
                    self.columns(core, mp), self.patch_all.at[own], self.patch_send.at[i],
                    self.patch_recv.at[own], device,
                )
            )
        here = [
            pltpu.make_async_copy(self.out_weight.at[:, self.mp], self.out_all.at[self.mp], self.local.at[0]),
            pltpu.make_async_copy(self.columns(self.core, self.mp), self.patch_all.at[own], self.local.at[1]),
        ]

        def begin():
            for copy in copies + here:
                copy.start()

        def end():
            for i, (core, mp, device) in enumerate(self.mates()):
                slot = core * 4 + mp
                if i < 3:
                    dst = self.out_all.at[mp]
                    remote(dst, dst, self.out_send.at[0], self.out_recv.at[mp], device).wait_recv()
                dst = self.patch_all.at[slot]
                remote(dst, dst, self.patch_send.at[0], self.patch_recv.at[slot], device).wait_recv()
            for copy in copies:
                copy.wait_send()
            for copy in here:
                copy.wait()

        return [(start, begin), (1000.0, end)]


def weight_sems():
    return [pltpu.SemaphoreType.DMA((n,)) for n in (3, 4, 7, 8, 2)]


def merge(groups):
    return [device for group in groups for device in group]


def silu(v):
    half = 0.5 * v
    return half + half * jnp.tanh(half)


OPENING_TIMES = ((0.0, 4.0), (5.2, 9.6, 13.0, 18.0))


def opening_kernel(
    pairs, down, text, patch_in, gain_ref, image_ref, text_all,
    pairs_all, down_all, rows, weights, total, patch_ref,
    pair_send, pair_recv, down_send, down_recv, own_sem, send, recv, local,
):
    ctx, tile, mp = coordinates()
    job = Gather("ctx", [text], text_all, send, recv, local)
    tiles = [((tile + i) % 8) for i in range(1, 8)]
    mps = [((mp + i) % 4) for i in range(1, 4)]
    barrier([(ctx, t, mp) for t in tiles] + [(ctx, tile, m) for m in mps] + job.partners())
    copies = []
    for i, t in enumerate(tiles):
        copies.append(remote(pairs, pairs_all.at[tile], pair_send.at[i], pair_recv.at[tile], (ctx, t, mp)))
    for i, m in enumerate(mps):
        copies.append(remote(down, down_all.at[mp], down_send.at[i], down_recv.at[mp], (ctx, tile, m)))
    own = [
        pltpu.make_async_copy(pairs, pairs_all.at[tile], own_sem.at[0]),
        pltpu.make_async_copy(down, down_all.at[mp], own_sem.at[1]),
        pltpu.make_async_copy(patch_in, patch_ref, own_sem.at[2]),
    ]
    for copy in copies + own:
        copy.start()

    def prepare():
        rows[...] = jnp.zeros_like(rows)
        weights[...] = jnp.zeros_like(weights)

    def arrange():
        for copy in own:
            copy.wait()
        for m in mps:
            remote(down, down_all.at[m], down_send.at[0], down_recv.at[m], (ctx, tile, m)).wait_recv()
        taps = sum(down_all[m].astype(F32) for m in range(4))
        for kind in range(2):
            for a in range(3):
                at = (a + 1 - kind) // 2 * HD + (a + 1 - kind) % 2 * 48
                for pc in range(4):
                    weights[kind * 4 + pc, at + 8 * pc : at + 8 * pc + 24] = taps[24 * a : 24 * a + 24]
        for t in tiles:
            remote(pairs, pairs_all.at[t], pair_send.at[0], pair_recv.at[t], (ctx, t, mp)).wait_recv()
        for t in range(8):
            for s in range(2):
                for i in range(4):
                    at = 1 + 4 * t + i
                    rows[s, at // 2, at % 2] = pairs_all[t, s, i]

    def pixel_row(pr):
        first = (0, 1, 1, 2)[pr]
        lhs = jnp.concatenate(
            [rows[:, p // 2 : p // 2 + 16, p % 2].reshape(UNIT, HD) for p in (first, first + 1)], axis=1
        )
        acts = [
            silu(jnp.dot(lhs, weights[pr % 2 * 4 + pc].astype(BF), preferred_element_type=F32)).astype(BF)
            for pc in range(4)
        ]
        term = jnp.dot(
            jnp.concatenate(acts, axis=1), patch_ref[pr * 1024 : (pr + 1) * 1024], preferred_element_type=F32
        )
        if pr == 0:
            total[...] = term
        elif pr < 3:
            total[...] += term
        else:
            image_ref[:32] = jnp.broadcast_to(gain_ref[...], (32, HD))
            image_ref[32:] = (total[...] + term).astype(BF)

    perform(
        job.events(OPENING_TIMES[0])
        + [(0.1, prepare), (5.0, arrange)]
        + [(at, lambda pr=pr: pixel_row(pr)) for pr, at in enumerate(OPENING_TIMES[1])]
    )
    for copy in copies:
        copy.wait_send()


def opening(pairs, down, text, patch_in, gain, parts=2):
    dma = pltpu.SemaphoreType.DMA
    vmem = pl.BlockSpec(memory_space=pltpu.VMEM)
    return pl.pallas_call(
        opening_kernel,
        out_shape=[
            jax.ShapeDtypeStruct((UNIT + 32, HD), BF),
            jax.ShapeDtypeStruct((8, parts, 1024 // parts, HD), BF),
        ],
        in_specs=[ANY, ANY, ANY, ANY, vmem],
        out_specs=[vmem, ANY],
        scratch_shapes=[
            pltpu.VMEM((8,) + pairs.shape, BF),
            pltpu.VMEM((4,) + down.shape, BF),
            pltpu.VMEM((2, 17, 2, 16, HD), BF),
            pltpu.VMEM((8, 2 * HD, CH), F32),
            pltpu.VMEM((UNIT, HD), F32),
            pltpu.VMEM((4096, HD), BF),
        ]
        + [dma((7,)), dma((8,)), dma((3,)), dma((4,)), dma((3,))]
        + gather_sems(parts),
        compiler_params=pltpu.CompilerParams(
            collective_id=1, has_side_effects=True, vmem_limit_bytes=32 * 1024 * 1024
        ),
    )(pairs, down, text, patch_in, gain)


TILE = 256


STEP = 2048


def attend_step(state, q, k, v, limit):
    top, total, acc = state
    s = lax.dot_general(q, k, (((1,), (1,)), ((), ())), preferred_element_type=F32)
    if limit is not None:
        s = jnp.where(lax.broadcasted_iota(jnp.int32, s.shape, 1) < limit, s, NEGATIVE)
    new = jnp.maximum(top, jnp.max(s, axis=1, keepdims=True))
    weights = jnp.exp(s - new)
    factor = jnp.exp(top - new)
    total = total * factor + jnp.sum(weights, axis=1, keepdims=True)
    acc = acc * factor + jnp.dot(weights.astype(BF), v, preferred_element_type=F32)
    return new, total, acc


def keys_at(ref, places):
    k = jnp.concatenate([ref[at, which, :IMG_TOK] for at, which in places], axis=0)
    v = jnp.concatenate([ref[at, which, IMG_TOK:] for at, which in places], axis=0)
    return k, v


HEADS_TIMES = (8.0, 31.0, 39.0, 41.0)
ATTEND_TIMES = (59.5, 59.6, 61.5, 61.6)


def heads_kernel(
    slots, image, text, wq, wk, wv, qg_ref, kg_ref, lim_i_ref, out_weight, patch_out,
    q_ref, image_kv, text_kv, top_ref, total_ref, acc_ref, out_all, patch_all,
    x_image, x_text, image_own, text_own, wq_ref, wk_ref, wv_ref, own_sem, *sems
):
    jobs = [
        Gather("xz", [image], x_image, *sems[0:3]),
        Gather("xz", [text], x_text, *sems[3:6]),
    ]
    keys = [
        Gather("ctx", [image_own.at[0], image_own.at[1]], image_kv, *sems[6:9]),
        Gather("ctx", [text_own.at[0], text_own.at[1]], text_kv, *sems[9:12]),
    ]
    moved = Weights(out_weight, patch_out, out_all, patch_all, *sems[12:])
    barrier(merge([jobs[0].partners(), keys[0].partners(), moved.partners()]))
    loads = [
        pltpu.make_async_copy(src, dst, own_sem.at[i])
        for i, (src, dst) in enumerate(((wq, wq_ref), (wk, wk_ref), (wv, wv_ref)))
    ]

    def load():
        for copy in loads:
            copy.start()

    def heads(x_ref, unit, start, own, half, at):
        if at == 0:
            for copy in loads:
                copy.wait()
        rows = slice(start, start + TILE)
        squares = jnp.zeros((TILE, HD), F32)
        for i in range(32):
            piece = x_ref[i, unit, rows].astype(F32)
            squares += piece * piece
        scale = lax.rsqrt(jnp.sum(squares, axis=1, keepdims=True) * (1.0 / 4096.0) + EPSILON)
        normed = jnp.concatenate(
            [
                (x_ref[i, unit, rows].astype(F32) * scale * x_image[i, 0, 0:1].astype(F32)).astype(BF)
                for i in range(32)
            ],
            axis=1,
        )

        def head(weight, gain, factor):
            raw = jnp.dot(normed, weight, preferred_element_type=F32)
            mean = jnp.mean(raw * raw, axis=1, keepdims=True)
            return (raw * lax.rsqrt(mean + EPSILON) * gain * factor).astype(BF)

        own[half, 0:TILE] = head(wk_ref[...], kg_ref[...], 1.0)
        own[half, TILE:] = jnp.dot(normed, wv_ref[...], preferred_element_type=F32).astype(BF)
        q_ref[at : at + TILE] = head(wq_ref[...], qg_ref[...], HD**-0.5)

    def attend(u):
        rows = slice(u * TILE, (u + 1) * TILE)
        state = (jnp.full((TILE, 1), NEGATIVE, F32), jnp.zeros((TILE, 1), F32), jnp.zeros((TILE, HD), F32))
        for n in range(2):
            found = [slots[n * (STEP // IMG_TOK) + i] for i in range(STEP // IMG_TOK)]
            k, v = keys_at(image_kv, [(slot // 2, slot % 2) for slot in found])
            state = attend_step(state, q_ref[rows], k, v, lim_i_ref[rows] - n * STEP)
        top_ref[rows] = jnp.broadcast_to(state[0], (TILE, HD))
        total_ref[rows] = jnp.broadcast_to(state[1], (TILE, HD))
        acc_ref[rows] = state[2]

    text_start, image_ready, text_ready, moving = HEADS_TIMES
    perform(
        jobs[0].events([0.0])
        + jobs[1].events([text_start])
        + [(0.1, load)]
        + [
            (image_ready, lambda: heads(x_image, 0, 32, image_own, 0, 0)),
            (image_ready + 0.1, lambda: heads(x_image, 0, 32 + TILE, image_own, 1, TILE)),
            (text_ready, lambda: heads(x_text, 0, 0, text_own, 0, 2 * TILE)),
            (text_ready + 0.1, lambda: heads(x_text, 0, TILE, text_own, 1, 3 * TILE)),
        ]
        + keys[0].events([image_ready + 0.2, image_ready + 0.3])
        + keys[1].events([text_ready + 0.2, text_ready + 0.3], 3.0)
        + [(at, lambda u=u: attend(u)) for u, at in enumerate(ATTEND_TIMES)]
        + moved.events(moving)
    )


def heads_of(slots, image, text, wq, wk, wv, qg, kg, lim_i, out_weight, patch_out):
    vmem = pl.BlockSpec(memory_space=pltpu.VMEM)
    keys = jax.ShapeDtypeStruct((8, 2, UNIT, HD), BF)
    return pl.pallas_call(
        heads_kernel,
        out_shape=[
            jax.ShapeDtypeStruct((2 * UNIT, HD), BF),
            keys,
            keys,
            *[jax.ShapeDtypeStruct((2 * UNIT, HD), F32)] * 3,
            jax.ShapeDtypeStruct((4, 8, HD, HD), BF),
            jax.ShapeDtypeStruct((8, HD, 512), BF),
        ],
        in_specs=[pl.BlockSpec(memory_space=pltpu.SMEM)] + [ANY] * 5 + [vmem] * 3 + [ANY] * 2,
        out_specs=[vmem] * 6 + [ANY] * 2,
        scratch_shapes=[
            pltpu.VMEM((32, 1) + image.shape, BF),
            pltpu.VMEM((32, 1) + text.shape, BF),
            pltpu.VMEM((2, UNIT, HD), BF),
            pltpu.VMEM((2, UNIT, HD), BF),
        ]
        + [pltpu.VMEM((4096, HD), BF)] * 3
        + [pltpu.SemaphoreType.DMA((3,))]
        + gather_sems(1)
        + gather_sems(1)
        + gather_sems(2)
        + gather_sems(2)
        + weight_sems(),
        compiler_params=pltpu.CompilerParams(
            collective_id=3, has_side_effects=True, vmem_limit_bytes=60 * 1024 * 1024
        ),
    )(slots, image, text, wq, wk, wv, qg, kg, lim_i[:, None], out_weight, patch_out)


MIX = 256
TILE_TIMES = (0.0, 2.5, 5.0, 6.3, 8.8)


def mix_kernel(
    q, lim_t, top, total, acc, text_kv, w, image_stream, text_stream, image_out, text_out,
    q_ref, lim_t_ref, top_ref, total_ref, acc_ref, mixed, text_ref, blocks, outgoing, incoming, w_ref, send, recv, local, part_send, part_recv, own_sem,
):
    ctx, tile, mp = coordinates()
    units = blocks.shape[1]
    job = Gather("z", [mixed], blocks, send, recv, local)
    loads = [
        pltpu.make_async_copy(src, dst, own_sem.at[i])
        for i, (src, dst) in enumerate(
            (
                (text_kv, text_ref),
                (q, q_ref),
                (lim_t, lim_t_ref),
                (top, top_ref),
                (total, total_ref),
                (acc, acc_ref),
                (w, w_ref),
            )
        )
    ]
    for load in loads:
        load.start()
    rings = [(mp + 1) % 4, (mp + 3) % 4, (mp + 2) % 4]
    barrier(merge([job.partners(), [(ctx, tile, rings[2])]]))
    per = STEP // IMG_TOK

    def text_places(n):
        first = n * per
        return [(first + u, 0) if n == 0 else (15 - first - u, 1) for u in range(per)]

    def attend(u):
        rows = slice(u * TILE, (u + 1) * TILE)
        if u == 0:
            for load in loads[:6]:
                load.wait()
        state = (top_ref[rows, 0:1], total_ref[rows, 0:1], acc_ref[rows])
        for n in range(1 if u == 2 else 2):
            limit = None if u == 3 and n == 0 else lim_t_ref[rows] - n * STEP
            state = attend_step(state, q_ref[rows], *keys_at(text_ref, text_places(n)), limit)
        mixed[rows] = (state[2] / state[1]).astype(BF)

    def settle(u):
        for i, ring in enumerate(rings):
            dst = incoming.at[ring, u]
            remote(dst, dst, part_send.at[0, 0], part_recv.at[ring, u], (ctx, tile, ring)).wait_recv()
        stream, out, row = (image_stream, image_out, u * MIX) if u < 2 else (text_stream, text_out, u * MIX - UNIT)
        first = row + 32 if u < 2 else row
        whole = stream[first : first + MIX].astype(F32) + kept[u]
        for ring in rings:
            whole = whole + incoming[ring, u].astype(F32)
        out[row : row + MIX] = whole.astype(BF)

    kept, copies = {}, []

    def multiply(u):
        if u == 0:
            loads[6].wait()
        x = jnp.concatenate([blocks[t, u] for t in range(8)], axis=1)
        for i, ring in enumerate(rings):
            outgoing[i, u] = jnp.dot(x, w_ref[ring], preferred_element_type=F32).astype(BF)
            copy = remote(
                outgoing.at[i, u], incoming.at[mp, u], part_send.at[i, u], part_recv.at[mp, u], (ctx, tile, ring)
            )
            copy.start()
            copies.append(copy)
        kept[u] = jnp.dot(x, w_ref[mp], preferred_element_type=F32)
        if u > 0:
            settle(u - 1)

    perform([(at, lambda u=u: attend(u)) for u, at in enumerate(TILE_TIMES[:4])] + job.column_events(multiply))
    settle(units - 1)
    job.close()
    for copy in copies:
        copy.wait_send()


def mix(q, lim_t, top, total, acc, text_kv, w, image_stream, text_stream):
    dma = pltpu.SemaphoreType.DMA
    units = 2 * UNIT // MIX
    vmem = pl.BlockSpec(memory_space=pltpu.VMEM)
    return pl.pallas_call(
        mix_kernel,
        out_shape=[jax.ShapeDtypeStruct((UNIT, HD), BF)] * 2,
        in_specs=[ANY] * 7 + [vmem, vmem],
        out_specs=[vmem, vmem],
        scratch_shapes=[
            pltpu.VMEM((2 * UNIT, HD), BF),
            pltpu.VMEM((2 * UNIT, 1), jnp.int32),
        ]
        + [pltpu.VMEM((2 * UNIT, HD), F32)] * 3
        + [
            pltpu.VMEM((2 * UNIT, HD), BF),
            pltpu.VMEM((8, 2, UNIT, HD), BF),
            pltpu.VMEM((8, units, MIX, HD), BF),
            pltpu.VMEM((3, units, MIX, HD), BF),
            pltpu.VMEM((4, units, MIX, HD), BF),
            pltpu.VMEM((4, 1024, HD), BF),
        ]
        + gather_sems(units)
        + [dma((3, units)), dma((4, units)), dma((7,))],
        compiler_params=pltpu.CompilerParams(
            collective_id=2, has_side_effects=True, vmem_limit_bytes=60 * 1024 * 1024
        ),
    )(q, lim_t[:, None], top, total, acc, text_kv, w, image_stream, text_stream)


UP_TIMES = (8.1, 24.0, 32.0, (0.0, 4.0))


def up_kernel(
    image, text, w, up_ref, work, cells_ref,
    blocks, product, terms, grid, above, below, w_ref,
    work_send, work_recv, work_local,
    block_send, block_recv, twin_send, twin_recv, term_send, term_recv, grid_send, grid_recv, edge_send, edge_recv,
    own_sem,
):
    ctx, tile, mp = coordinates()
    z, core = tile // 2, tile % 2
    job = Gather("ctx", [image, text], work, work_send, work_recv, work_local)
    me = tile * 4 + mp
    group = []
    for i in range(1, 32):
        peer = (me + i) % 32
        group.append((ctx, peer // 4, peer % 4))
    barrier(merge([group, job.partners()]))
    rings = [(mp + 1) % 4, (mp + 3) % 4, (mp + 2) % 4]
    twin = (ctx, z * 2 + 1 - core, mp)
    own = core * 4 + mp
    copies = []

    def go(copy):
        copy.start()
        copies.append(copy)

    mine = [
        pltpu.make_async_copy(image, blocks.at[own], own_sem.at[0]),
        pltpu.make_async_copy(product.at[tile], terms.at[tile], own_sem.at[1]),
        pltpu.make_async_copy(w, w_ref, own_sem.at[2]),
    ]
    tiles = [(tile + i) % 8 for i in (2, 6, 4, 1, 7, 3, 5)]
    down_edge = (mp == 3) & (tile < 7)
    up_edge = (mp == 0) & (tile > 0)
    down_copies = [
        lambda m=m: remote(
            grid.at[mp, :, pl.ds(16, 16)], above, edge_send.at[m], edge_recv.at[0], (ctx, (tile + 1) % 8, m)
        )
        for m in range(4)
    ]
    up_copies = [
        lambda m=m: remote(
            grid.at[mp, :, pl.ds(0, 16)], below, edge_send.at[m], edge_recv.at[1], (ctx, (tile + 7) % 8, m)
        )
        for m in range(4)
    ]

    def begin():
        for i, ring in enumerate(rings):
            go(remote(image, blocks.at[own], block_send.at[i], block_recv.at[mp], (ctx, tile, ring)))
        go(remote(image, blocks.at[own], twin_send.at[mp], twin_recv.at[mp], twin))
        mine[0].start()
        mine[2].start()

    def pair(i):
        ring = rings[i]
        dst = blocks.at[core * 4 + ring]
        remote(dst, dst, block_send.at[0], block_recv.at[ring], (ctx, tile, ring)).wait_recv()
        go(remote(dst, dst, twin_send.at[ring], twin_recv.at[ring], twin))

    def multiply():
        mine[0].wait()
        mine[2].wait()
        for ring in range(4):
            dst = blocks.at[(1 - core) * 4 + ring]
            remote(dst, dst, twin_send.at[0], twin_recv.at[ring], twin).wait_recv()
        for s in range(2):
            x = jnp.concatenate([blocks[i, s * IMG_TOK : (s + 1) * IMG_TOK] for i in range(8)], axis=1)
            part = jnp.dot(x, w_ref[...].reshape(1024, 512), preferred_element_type=F32).astype(BF)
            product[:, s] = part.reshape(8, 32, 512)
        for i, t in enumerate(tiles):
            go(remote(product.at[t], terms.at[tile], term_send.at[i], term_recv.at[tile], (ctx, t, mp)))
        mine[1].start()

        @pl.when(tile == 0)
        def _():
            above[...] = jnp.zeros_like(above)

        @pl.when(tile == 7)
        def _():
            below[...] = jnp.zeros_like(below)

    def total():
        for t in tiles:
            dst = terms.at[t]
            remote(dst, dst, term_send.at[0], term_recv.at[t], (ctx, t, mp)).wait_recv()
        mine[1].wait()
        for c in range(2):
            total = terms[c].astype(F32)
            for k in range(1, 4):
                total = total + terms[2 * k + c].astype(F32)
            grid[mp, :, :, c * 512 : (c + 1) * 512] = silu(total).astype(BF)

        @pl.when(down_edge)
        def _():
            for make in down_copies:
                make().start()

        @pl.when(up_edge)
        def _():
            for make in up_copies:
                make().start()

        for i, ring in enumerate(rings):
            go(remote(grid.at[mp], grid.at[mp], grid_send.at[i], grid_recv.at[mp], (ctx, tile, ring)))

    def gathered():
        for ring in rings:
            dst = grid.at[ring]
            remote(dst, dst, grid_send.at[0], grid_recv.at[ring], (ctx, tile, ring)).wait_recv()

        @pl.when(tile > 0)
        def _():
            remote(above, above, edge_send.at[0], edge_recv.at[0], (ctx, tile, rings[0])).wait_recv()

        @pl.when(tile < 7)
        def _():
            remote(below, below, edge_send.at[0], edge_recv.at[1], (ctx, tile, rings[0])).wait_recv()

        convolve()

    def convolve():
        sums = [jnp.zeros((64, HD), F32) for _ in range(3)]
        for wr in range(6):
            for wc in range(6):
                pc = 3 if wc == 0 else 0 if wc == 5 else wc - 1
                lanes = slice(pc * CH, (pc + 1) * CH)
                if wr == 0:
                    a = jnp.concatenate([above[:, :, lanes], grid[3, :, 0:16, lanes]], axis=1)
                elif wr == 5:
                    a = jnp.concatenate([grid[0, :, 16:32, lanes], below[:, :, lanes]], axis=1)
                else:
                    a = grid[wr - 1, :, :, lanes]
                cell = wr * 6 + wc
                term = jnp.dot(
                    a.reshape(64, CH), up_ref[:, cell * HD : (cell + 1) * HD], preferred_element_type=F32
                )
                which = 0 if wc == 0 else 2 if wc == 5 else 1
                sums[which] = sums[which] + term
        column = lax.broadcasted_iota(jnp.int32, (64, HD), 0) % 16
        blank = jnp.zeros((1, HD), F32)
        from_left = jnp.concatenate([blank, sums[0][:63]], axis=0)
        from_right = jnp.concatenate([sums[2][1:], blank], axis=0)
        cells_ref[...] = (
            sums[1] + jnp.where(column == 0, 0.0, from_left) + jnp.where(column == 15, 0.0, from_right)
        )

    perform(
        [(0.0, begin)]
        + job.events(UP_TIMES[3])
        + [(5.4, lambda: pair(0)), (5.4, lambda: pair(1)), (7.0, lambda: pair(2))]
        + [(UP_TIMES[0], multiply), (UP_TIMES[1], total), (UP_TIMES[2], gathered)]
    )
    for copy in copies:
        copy.wait_send()

    @pl.when(down_edge)
    def _():
        for make in down_copies:
            make().wait_send()

    @pl.when(up_edge)
    def _():
        for make in up_copies:
            make().wait_send()


def up_block(image, text, w, up_w):
    dma = pltpu.SemaphoreType.DMA
    vmem = pl.BlockSpec(memory_space=pltpu.VMEM)
    work = jax.ShapeDtypeStruct((8, 2, UNIT, HD), BF)
    return pl.pallas_call(
        up_kernel,
        out_shape=[work, jax.ShapeDtypeStruct((64, HD), F32)],
        in_specs=[ANY, ANY, ANY, vmem],
        out_specs=[vmem, vmem],
        scratch_shapes=[
            pltpu.VMEM((8, UNIT, HD), BF),
            pltpu.VMEM((8, 2, 32, 512), BF),
            pltpu.VMEM((8, 2, 32, 512), BF),
            pltpu.VMEM((4, 2, 32, 1024), BF),
            pltpu.VMEM((2, 16, 1024), BF),
            pltpu.VMEM((2, 16, 1024), BF),
            pltpu.VMEM((8, HD, 512), BF),
        ]
        + gather_sems(2)
        + [dma((n,)) for n in (3, 4, 4, 4, 7, 8, 3, 4, 4, 2, 3)],
        compiler_params=pltpu.CompilerParams(
            collective_id=6, has_side_effects=True, vmem_limit_bytes=32 * 1024 * 1024
        ),
    )(image, text, w, up_w)


def window_pairs(latents):
    wide = jnp.pad(latents, ((0, 0), (0, 0), (8, 32)))
    before = wide[..., 0:512].reshape(2, 8, 16, 32)[..., :8]
    middle = latents.reshape(2, 8, 16, 32)
    after = wide[..., 40:552].reshape(2, 8, 16, 32)[..., :8]
    joined = jnp.concatenate([before, middle, after], axis=-1)
    return jnp.concatenate([joined[:, 0::2], joined[:, 1::2], jnp.zeros((2, 4, 16, 32), BF)], axis=-1)


def up_weights(up_conv):
    taps = up_conv.reshape(9, CH, CIN).transpose(1, 0, 2).reshape(CH, 72)
    row = lax.broadcasted_iota(jnp.int32, (72, 36 * HD), 0)
    col = lax.broadcasted_iota(jnp.int32, (72, 36 * HD), 1)
    cell, inner = col // HD, col % HD
    a, b = cell // 6 - inner // 32, cell % 6 - (inner // 8) % 4
    inside = (a >= 0) & (a <= 2) & (b >= 0) & (b <= 2)
    pick = jnp.where(inside & (row == (a * 3 + b) * 8 + inner % 8), 1.0, 0.0).astype(BF)
    return jnp.dot(taps, pick, preferred_element_type=F32).astype(BF)


def shards(
    text_embed,
    latents,
    down_conv,
    patch_in,
    norm_gain,
    query_weight,
    key_weight,
    value_weight,
    query_gain,
    key_gain,
    out_weight,
    patch_out,
    up_conv,
    span_start,
    image_of_slot,
):
    ctx = lax.axis_index("ctx")
    images = jnp.arange(16, dtype=jnp.int32)
    before = span_start - images * IMG_TOK
    is_slot = image_of_slot[None, :] == images[:, None]
    slot_of = jnp.sum(jnp.where(is_slot, images[None, :], 0), axis=1)

    mp = lax.axis_index("mp")
    channels = jnp.arange(CH, dtype=jnp.int32)[None, :] // 64 == mp
    down = jnp.where(channels, jnp.tile(down_conv, (1, 4)), 0)
    image, text_all = opening(
        window_pairs(latents), jnp.pad(down, ((0, 8), (0, 0))), text_embed, patch_in, norm_gain[None, :]
    )

    inner = jnp.arange(IMG_TOK, dtype=jnp.int32)
    text_rows = jnp.concatenate([ctx * IMG_TOK + inner, (15 - ctx) * IMG_TOK + inner])
    seen = jnp.sum((before[None, :] <= text_rows[:, None]).astype(jnp.int32), axis=1)
    text = jnp.take(text_all.reshape(8192, HD), text_rows + IMG_TOK * seen, axis=0, mode="clip")
    slots = ctx * 2 + jnp.arange(2, dtype=jnp.int32)
    here = slots[:, None] == images[None, :]
    own_image = jnp.sum(jnp.where(here, image_of_slot[None, :], 0), axis=1)
    own_before = jnp.sum(jnp.where(own_image[:, None] == images[None, :], before[None, :], 0), axis=1)
    spread = lambda pair: jnp.broadcast_to(pair[:, None], (2, IMG_TOK)).reshape(UNIT)
    lim_t = jnp.concatenate([spread(own_before), text_rows + 1])
    lim_i = jnp.concatenate([spread((own_image + 1) * IMG_TOK), seen * IMG_TOK])
    q, _, text_kv, top, total, acc, out_all, patch_all = heads_of(
        slot_of, image, text, query_weight, key_weight, value_weight, query_gain.reshape(1, HD),
        key_gain.reshape(1, HD), lim_i, out_weight.reshape(8, 4, HD, HD), patch_out,
    )
    image_out, text_out = mix(q, lim_t, top, total, acc, text_kv, out_all.reshape(4, 1024, HD), image, text)
    work, cells = up_block(image_out, text_out, patch_all, up_weights(up_conv))
    noise_pred = cells.reshape(2, 2, 16, 4, 32).transpose(0, 1, 3, 2, 4).reshape(2, 8, 512)

    positions = ctx * 1024 + jnp.arange(1024, dtype=jnp.int32)
    started = (span_start[None, :] <= positions[:, None]).astype(jnp.int32)
    passed = jnp.sum((span_start[None, :] + IMG_TOK <= positions[:, None]).astype(jnp.int32), axis=1)
    inside = jnp.sum(started, axis=1) > passed
    now = passed[:, None] == images[None, :]
    slot = jnp.sum(jnp.where(now, slot_of[None, :], 0), axis=1)
    start = jnp.sum(jnp.where(now, span_start[None, :], 0), axis=1)
    row = positions - passed * IMG_TOK
    block = row // IMG_TOK
    text_source = jnp.minimum(block, 15 - block) * 1024 + UNIT + block // 8 * IMG_TOK + row % IMG_TOK
    image_source = slot // 2 * 1024 + slot % 2 * IMG_TOK + positions - start
    source = jnp.where(inside, image_source, text_source)
    layer_out = jnp.take(work.reshape(8192, HD), source, axis=0, mode="clip")
    return layer_out, noise_pred


def solution(mesh):
    return jax.shard_map(
        shards,
        mesh=mesh,
        in_specs=(
            P("ctx", ("tile", "mp")),
            P("ctx", "tile", None),
            P(None, "mp"),
            P(None, ("tile", "mp")),
            P(("tile", "mp")),
            P(None, ("tile", "mp")),
            P(None, ("tile", "mp")),
            P(None, ("tile", "mp")),
            P(),
            P(),
            P(None, ("tile", "mp")),
            P(("tile", "mp"), None),
            P(),
            P(),
            P(),
        ),
        out_specs=(P("ctx", ("tile", "mp")), P("ctx", "tile", None)),
        check_vma=False,
    )
```
